32 devices in a mesh: rep: 2 (over x), exp: 16 (over z, y, core).
Axes of the slice: x: 2, y: 2, z: 4, core: 2. Of those that a mesh axis runs over, the one named last changes fastest.
Arguments:
- tokens: bfloat16 [128, 256, 1280], P(('rep', 'exp')), may hold values from -19 to 19
- slot_params: bfloat16 [1280, 16], replicated, may hold values from -1 to 1
- expert_in: bfloat16 [16, 1280, 2560], P('exp'), may hold values from -0.15625 to 0.15625
- expert_out: bfloat16 [16, 2560, 1280], P('exp'), may hold values from -0.125 to 0.125
- grad_out: bfloat16 [128, 256, 1280], P(('rep', 'exp')), may hold values from -6 to 6
Outputs:
- grad_tokens: bfloat16 [128, 256, 1280], P(('rep', 'exp'))
- grad_params: float32 [1280, 16], replicated
- grad_expert_in: bfloat16 [16, 1280, 2560], P('exp', 'rep')
- grad_expert_out: bfloat16 [16, 2560, 1280], P('exp', 'rep')
The draws below stay inside these ranges and needn't reach their ends.
All inputs are finite; a program needn't handle non-finite values.
Results may differ from the reference program's by a relative error of at most 0.0093.
Values may be sent and summed in bfloat16 or wider, within the bound.
No kernel may reach another device: no remote copies, remote signals or barrier semaphores. Data moves between devices by JAX's collectives and lax.ppermute only.
A program may use at most 128 MiB of HBM per device.

```python
import math
import jax
import jax.numpy as jnp
from jax import lax

D = 1280
F = 2560
M = 256
SLOTS = 16
IMAGES = 128
N_REP = 2


def draw_slot_params(key, part):
    key = jax.random.fold_in(key, 5)
    second_key = jax.random.fold_in(key, 1)
    values = jax.random.normal(second_key, (D, SLOTS), jnp.float32) / math.sqrt(D)
    return values.astype(jnp.bfloat16)


def draw_tokens(key, part):
    key = jax.random.fold_in(key, 9)
    keys_list = jax.random.split(key, 1)
    values = jnp.clip(jax.random.normal(keys_list[0], (IMAGES, M, D), jnp.float32), -6.0, 6.0)
    return values.astype(jnp.bfloat16)


def level_of(key, dims, cuts, smallest, largest):
    factor_of, own = 1.0, jax.random.fold_in(key, 6)
    for axis_at, blocks in cuts:
        draws = jnp.exp(jax.random.uniform(jax.random.fold_in(own, axis_at), (blocks,), jnp.float32, smallest / len(cuts), largest / len(cuts)))
        factor_of = factor_of * jnp.repeat(draws, dims[axis_at] // blocks).reshape([-1 if axis == axis_at else 1 for axis in range(len(dims))])
    return factor_of


def normal_values(stream_key, dims, spread, most, cuts=(), dtype=jnp.bfloat16):
    result = jax.random.normal(stream_key, dims, jnp.float32) * spread
    if len(cuts) > 0:
        result = level_of(stream_key, dims, cuts, -0.22, 0.18) * result
    return jnp.clip(result, min=-most, max=most).astype(dtype)


def setup_inputs(seed: int = 0) -> dict:
    splits = jax.random.split(jax.random.key(seed), 6)
    return {
        "tokens": draw_tokens(jax.random.fold_in(splits[5], 71), 0),
        "slot_params": draw_slot_params(jax.random.fold_in(splits[5], 71), 0),
        "expert_in": normal_values(splits[2], (SLOTS, D, F), D ** -0.5, 0.15625, ((0, 16),)),
        "expert_out": normal_values(splits[3], (SLOTS, F, D), F ** -0.5, 0.125, ((0, 16),)),
        "grad_out": normal_values(splits[4], (IMAGES, M, D), 1.0, 6.0, ((0, 32),)),
    }


GELU_C = math.sqrt(2.0 / math.pi)
CUBIC = 0.044715

def gelu_tanh(values):
    inner = GELU_C * (values + CUBIC * values * values * values)
    return 0.5 * values * (1.0 + jnp.tanh(inner))

def gelu_slope(values):
    tangent = jnp.tanh(GELU_C * (values + CUBIC * values * values * values))
    return 0.5 * (1.0 + tangent) + 0.5 * values * (1.0 - tangent * tangent) * GELU_C * (1.0 + 3.0 * CUBIC * values * values)

def replica_sum(left, right):
    left_wide = left.astype(jnp.float32).reshape(N_REP, -1, left.shape[1])
    right_wide = right.astype(jnp.float32).reshape(N_REP, -1, right.shape[1])
    terms = jnp.einsum('rka,rkb->rab', left_wide, right_wide).astype(jnp.bfloat16)
    terms = lax.optimization_barrier(terms)
    return lax.optimization_barrier(jnp.sum(terms.astype(jnp.float32), axis=0)).astype(jnp.bfloat16)

def expert_pass(operands):
    rows_in, rows_grad, weight_in, weight_out = operands
    preact = jnp.dot(rows_in, weight_in, preferred_element_type=jnp.float32)
    activations = gelu_tanh(preact).astype(jnp.bfloat16)
    rows_out = jnp.dot(activations, weight_out, preferred_element_type=jnp.float32).astype(jnp.bfloat16)
    d_acts = jnp.dot(rows_grad, weight_out.T, preferred_element_type=jnp.float32)
    d_hidden = (d_acts * gelu_slope(preact)).astype(jnp.bfloat16)
    d_rows = jnp.dot(d_hidden, weight_in.T, preferred_element_type=jnp.float32).astype(jnp.bfloat16)
    return (rows_out, d_rows, replica_sum(rows_in, d_hidden), replica_sum(activations, rows_grad))

def reference(tokens, slot_params, expert_in, expert_out, grad_out):
    tokens_wide = tokens.astype(jnp.float32)
    grads_wide = grad_out.astype(jnp.float32)
    params_wide = slot_params.astype(jnp.float32)
    logits = jnp.einsum('bmd,ds->bsm', tokens_wide, params_wide)
    dispatch = jax.nn.softmax(logits, axis=2)
    combine = jax.nn.softmax(logits, axis=1)
    dispatch_low = dispatch.astype(jnp.bfloat16)
    combine_low = combine.astype(jnp.bfloat16)
    slot_in = jnp.einsum('bsm,bmd->bsd', dispatch_low.astype(jnp.float32), tokens_wide).astype(jnp.bfloat16)
    slot_grad = jnp.einsum('bsm,bmd->bsd', combine_low.astype(jnp.float32), grads_wide).astype(jnp.bfloat16)
    slot_out, d_slot_in, grad_expert_in, grad_expert_out = lax.map(expert_pass, (jnp.swapaxes(slot_in, 0, 1), jnp.swapaxes(slot_grad, 0, 1), expert_in, expert_out))
    slot_out = jnp.swapaxes(slot_out, 0, 1).astype(jnp.float32)
    d_slot_in = jnp.swapaxes(d_slot_in, 0, 1).astype(jnp.float32)
    d_combine = jnp.einsum('bmd,bsd->bsm', grads_wide, slot_out)
    d_dispatch = jnp.einsum('bmd,bsd->bsm', tokens_wide, d_slot_in)
    d_logits = combine * (d_combine - lax.optimization_barrier(jnp.sum(combine * d_combine, axis=1, keepdims=True)))
    d_logits = d_logits + dispatch * (d_dispatch - lax.optimization_barrier(jnp.sum(dispatch * d_dispatch, axis=2, keepdims=True)))
    d_logits_low = d_logits.astype(jnp.bfloat16).astype(jnp.float32)
    grad_tokens = jnp.einsum('bsm,bsd->bmd', dispatch_low.astype(jnp.float32), d_slot_in)
    grad_tokens = grad_tokens + jnp.einsum('bsm,ds->bmd', d_logits_low, params_wide)
    grad_params = jnp.einsum('bmd,bsm->ds', tokens_wide, d_logits_low)
    return (grad_tokens.astype(jnp.bfloat16), grad_params, grad_expert_in, grad_expert_out)
```

```python
import math

import jax
import jax.numpy as jnp
from jax import lax
from jax.sharding import PartitionSpec as P

GELU_C = math.sqrt(2.0 / math.pi)
CUBIC = 0.044715


def gelu_parts(values):
    tangent = jnp.tanh(GELU_C * (values + CUBIC * values * values * values))
    acts = 0.5 * values * (1.0 + tangent)
    slope = 0.5 * (1.0 + tangent) + 0.5 * values * (1.0 - tangent * tangent) * GELU_C * (
        1.0 + 3.0 * CUBIC * values * values
    )
    return acts, slope


def dot(left, right, contract):
    return lax.dot_general(
        left, right, (contract, ((), ())), preferred_element_type=jnp.float32
    )


def expert_hidden(rows_in, rows_grad, weight_in, weight_out):
    preact = dot(rows_in, weight_in, ((1,), (0,)))
    acts, slope = gelu_parts(preact)
    d_acts = dot(rows_grad, weight_out, ((1,), (1,)))
    return acts.astype(jnp.bfloat16), (d_acts * slope).astype(jnp.bfloat16)


def sum_everywhere(part, axes):
    count = lax.axis_size(axes)
    pieces = part.reshape(count, -1)
    pieces = lax.all_to_all(pieces, axes, split_axis=0, concat_axis=0, tiled=True)
    mine = jnp.sum(pieces, axis=0, keepdims=True)
    mine = jnp.broadcast_to(mine, pieces.shape)
    whole = lax.all_to_all(mine, axes, split_axis=0, concat_axis=0, tiled=True)
    return whole.reshape(part.shape)


def body(tokens, slot_params, expert_in, expert_out, grad_out):
    images, _, width = tokens.shape
    weight_in = expert_in[0]
    weight_out = expert_out[0]
    hidden = weight_in.shape[1]
    replicas = lax.axis_size("rep")
    logits = jnp.einsum("bmd,ds->bsm", tokens, slot_params, preferred_element_type=jnp.float32)
    dispatch = jax.nn.softmax(logits, axis=2)
    combine = jax.nn.softmax(logits, axis=1)
    dispatch_low = dispatch.astype(jnp.bfloat16)
    combine_low = combine.astype(jnp.bfloat16)
    slot_in = jnp.einsum(
        "bsm,bmd->bsd", dispatch_low, tokens, preferred_element_type=jnp.float32
    ).astype(jnp.bfloat16)
    slot_grad = jnp.einsum(
        "bsm,bmd->bsd", combine_low, grad_out, preferred_element_type=jnp.float32
    ).astype(jnp.bfloat16)
    slots = slot_in.shape[1]
    sent = jnp.swapaxes(jnp.concatenate([slot_in, slot_grad], axis=0), 0, 1)
    rows = lax.all_to_all(sent, "exp", split_axis=0, concat_axis=0, tiled=True)
    others = lax.ppermute(rows, "rep", [(i, (i + 1) % replicas) for i in range(replicas)])

    rows_in = rows[:, :images].reshape(-1, width)
    rows_grad = rows[:, images:].reshape(-1, width)
    acts, d_hidden = expert_hidden(rows_in, rows_grad, weight_in, weight_out)
    rows_out = dot(acts, weight_out, ((1,), (0,))).astype(jnp.bfloat16)
    d_rows = dot(d_hidden, weight_in, ((1,), (1,))).astype(jnp.bfloat16)
    back = jnp.concatenate(
        [rows_out.reshape(slots, images, width), d_rows.reshape(slots, images, width)], axis=1
    )
    back = lax.all_to_all(back, "exp", split_axis=0, concat_axis=0, tiled=True)

    others_in = others[:, :images].reshape(-1, width)
    others_grad = others[:, images:].reshape(-1, width)
    others_acts, others_hidden = expert_hidden(others_in, others_grad, weight_in, weight_out)
    mine = lax.axis_index("rep")

    def share(array, full):
        size = full // replicas
        return lax.dynamic_slice_in_dim(array, mine * size, size, axis=1)

    left_in = share(jnp.concatenate([rows_in, others_in], axis=0), width)
    left_acts = share(jnp.concatenate([acts, others_acts], axis=0), hidden)
    all_hidden = jnp.concatenate([d_hidden, others_hidden], axis=0)
    all_grad = jnp.concatenate([rows_grad, others_grad], axis=0)
    grad_expert_in = dot(left_in, all_hidden, ((0,), (0,))).astype(jnp.bfloat16)[None]
    grad_expert_out = dot(left_acts, all_grad, ((0,), (0,))).astype(jnp.bfloat16)[None]

    slot_out = back[:, :images]
    d_slot_in = back[:, images:]
    d_combine = jnp.einsum("bmd,sbd->bsm", grad_out, slot_out, preferred_element_type=jnp.float32)
    d_dispatch = jnp.einsum("bmd,sbd->bsm", tokens, d_slot_in, preferred_element_type=jnp.float32)
    d_logits = combine * (d_combine - jnp.sum(combine * d_combine, axis=1, keepdims=True))
    d_logits = d_logits + dispatch * (
        d_dispatch - jnp.sum(dispatch * d_dispatch, axis=2, keepdims=True)
    )
    d_logits_low = d_logits.astype(jnp.bfloat16)
    local_params = jnp.einsum(
        "bsm,bmd->sd", d_logits_low, tokens, preferred_element_type=jnp.float32
    )
    grad_params = sum_everywhere(local_params, ("rep", "exp")).T
    grad_tokens = jnp.einsum(
        "bsm,sbd->bmd", dispatch_low, d_slot_in, preferred_element_type=jnp.float32
    )
    grad_tokens = grad_tokens + jnp.einsum(
        "bsm,ds->bmd", d_logits_low, slot_params, preferred_element_type=jnp.float32
    )
    return (grad_tokens.astype(jnp.bfloat16), grad_params, grad_expert_in, grad_expert_out)


def solution(mesh):
    in_specs = (
        P(("rep", "exp"), None, None),
        P(),
        P("exp", None, None),
        P("exp", None, None),
        P(("rep", "exp"), None, None),
    )
    out_specs = (P(("rep", "exp"), None, None), P(), P("exp", "rep", None), P("exp", "rep", None))
    return jax.shard_map(body, mesh=mesh, in_specs=in_specs, out_specs=out_specs, check_vma=False)
```

```python
import math

import jax
import jax.numpy as jnp
from jax import lax
from jax.experimental import pallas as pl
from jax.experimental.pallas import tpu as pltpu
from jax.sharding import PartitionSpec as P

GELU_C = math.sqrt(2.0 / math.pi)
CUBIC = 0.044715
LOW = jnp.bfloat16
WIDE = jnp.float32
LANES = 128
VMEM_BYTES = 24 * 1024 * 1024
WHOLE = pl.BlockSpec(memory_space=pltpu.VMEM)


def params_of(limit=VMEM_BYTES):
    return pltpu.CompilerParams(vmem_limit_bytes=limit)


def gelu_parts(values):
    square = values * values
    tangent = jnp.tanh(GELU_C * (values + CUBIC * square * values))
    half = 0.5 * (1.0 + tangent)
    slope = half + 0.5 * values * (1.0 - tangent * tangent) * GELU_C * (1.0 + 3.0 * CUBIC * square)
    return values * half, slope


def dot(left, right, over_left, over_right):
    return lax.dot_general(
        left, right, (((over_left,), (over_right,)), ((), ())), preferred_element_type=WIDE
    )


def softmax(values, axis):
    raised = jnp.exp(values - jnp.max(values, axis=axis, keepdims=True))
    return raised / jnp.sum(raised, axis=axis, keepdims=True)


def fill(ref, array):
    for tile in range(ref.shape[0]):
        ref[tile] = array[:, tile * LANES : (tile + 1) * LANES].astype(WIDE)


def whole(ref):
    return jnp.concatenate([ref[tile] for tile in range(ref.shape[0])], axis=1)


def take(ref, start, count, stride, first=0, tiles=None):
    tiles = ref.shape[0] if tiles is None else tiles
    picked = [ref[first + tile, pl.ds(start, count, stride=stride), :] for tile in range(tiles)]
    return jnp.concatenate(picked, axis=1)


def put(ref, start, count, stride, array):
    for tile in range(ref.shape[0]):
        ref[tile, pl.ds(start, count, stride=stride), :] = array[
            :, tile * LANES : (tile + 1) * LANES
        ]


def tiles_of(total, width):
    return pltpu.VMEM((width // LANES, total, LANES), WIDE)


def gather_kernel(tokens, params, grads, sent, dispatch, combine, tokens_v, grads_v, rows, sems):
    images = tokens.shape[0]
    slots = params.shape[0]
    copies = []
    for kind, (source, target) in enumerate(((tokens, tokens_v), (grads, grads_v))):
        for image in range(images):
            copy = pltpu.make_async_copy(
                source.at[image], target.at[image], sems.at[kind, image]
            )
            copy.start()
            copies.append(copy)
    low = []
    for image in range(images):
        copies[image].wait()
        logits = dot(params[...], tokens_v[image], 1, 1)
        over_tokens = softmax(logits, 1)
        over_slots = softmax(logits, 0)
        dispatch[image] = over_tokens
        combine[image] = over_slots
        low.append((over_tokens.astype(LOW), over_slots.astype(LOW)))
    stride = 2 * images
    for image in range(images):
        put(rows, 2 * image, slots, stride, dot(low[image][0], tokens_v[image], 1, 0))
    for image in range(images):
        copies[images + image].wait()
        put(rows, 2 * image + 1, slots, stride, dot(low[image][1], grads_v[image], 1, 0))
    sent[...] = whole(rows).astype(LOW)


def gather(tokens, params, grads):
    images, length, width = tokens.shape
    slots = params.shape[0]
    weights = jax.ShapeDtypeStruct((images, slots, length), WIDE)
    place = pl.BlockSpec(memory_space=pl.ANY)
    return pl.pallas_call(
        gather_kernel,
        out_shape=(
            jax.ShapeDtypeStruct((slots * images * 2, width), LOW),
            weights,
            weights,
        ),
        in_specs=[place, WHOLE, place],
        out_specs=(WHOLE, WHOLE, WHOLE),
        scratch_shapes=[
            pltpu.VMEM(tokens.shape, LOW),
            pltpu.VMEM(grads.shape, LOW),
            tiles_of(slots * images * 2, width),
            pltpu.SemaphoreType.DMA((2, images)),
        ],
        compiler_params=params_of(),
        cost_estimate=pl.CostEstimate(
            flops=6 * images * slots * length * width,
            bytes_accessed=4 * images * length * width,
            transcendentals=2 * images * slots * length,
        ),
        name="gather_slots",
    )(tokens, params, grads)


def expert_kernel(rows, w_in, w_out, back, acts, hidden, wide, low, sums):
    step = pl.program_id(0)
    count = rows.shape[0] // 2

    @pl.when(step == 0)
    def _():
        fill(wide, rows[...])
        low[0] = take(wide, 0, count, 2).astype(LOW)
        low[1] = take(wide, 1, count, 2).astype(LOW)
        sums[...] = jnp.zeros_like(sums)

    preact = dot(low[0], w_in[...], 1, 0)
    d_acts = dot(low[1], w_out[...], 1, 1)
    values, slope = gelu_parts(preact)
    values = values.astype(LOW)
    d_hidden = (d_acts * slope).astype(LOW)
    acts[...] = values
    hidden[...] = d_hidden
    sums[0] += dot(values, w_out[...], 1, 0)
    sums[1] += dot(d_hidden, w_in[...], 1, 1)

    @pl.when(step == pl.num_programs(0) - 1)
    def _():
        put(wide, 0, count, 2, sums[0])
        put(wide, 1, count, 2, sums[1])
        back[...] = whole(wide).astype(LOW)


def expert(rows, w_in, w_out, tile):
    total, width = rows.shape
    hidden = w_in.shape[1]
    count = total // 2
    kept = jax.ShapeDtypeStruct((count, hidden), LOW)
    return pl.pallas_call(
        expert_kernel,
        grid=(hidden // tile,),
        out_shape=(jax.ShapeDtypeStruct(rows.shape, LOW), kept, kept),
        in_specs=[
            pl.BlockSpec((total, width), lambda i: (0, 0)),
            pl.BlockSpec((width, tile), lambda i: (0, i)),
            pl.BlockSpec((tile, width), lambda i: (i, 0)),
        ],
        out_specs=(
            pl.BlockSpec((total, width), lambda i: (0, 0)),
            pl.BlockSpec((count, tile), lambda i: (0, i)),
            pl.BlockSpec((count, tile), lambda i: (0, i)),
        ),
        scratch_shapes=[
            tiles_of(total, width),
            pltpu.VMEM((2, count, width), LOW),
            pltpu.VMEM((2, count, width), WIDE),
        ],
        compiler_params=params_of(),
        cost_estimate=pl.CostEstimate(
            flops=8 * count * hidden * width,
            bytes_accessed=4 * hidden * width,
            transcendentals=count * hidden,
        ),
        name="expert_rows",
    )(rows, w_in, w_out)


def weights_kernel(
    mine, rows, others, w_in, w_out, acts, hidden, grad_in, grad_out, wide, low, grads, turned
):
    step = pl.program_id(0)
    count = rows.shape[0] // 2
    share = turned.shape[0]
    replicas = low.shape[1] // share

    @pl.when(step == 0)
    def _():
        left, right = [], []
        for source in (rows, others):
            fill(wide, source[...])
            tiles = share // LANES
            left.append(take(wide, 0, count, 2, mine[0] * tiles, tiles))
            right.append(take(wide, 1, count, 2))
        low[...] = take(wide, 0, count, 2).astype(LOW)
        turned[...] = jnp.concatenate(left, axis=0).T.astype(LOW)
        grads[...] = jnp.concatenate(right, axis=0).astype(LOW)

    preact = dot(low[...], w_in[...], 1, 0)
    d_acts = dot(grads[count:, :], w_out[...], 1, 1)
    values, slope = gelu_parts(preact)
    all_hidden = jnp.concatenate([hidden[...], (d_acts * slope).astype(LOW)], axis=0)
    grad_in[...] = dot(turned[...], all_hidden, 1, 0).astype(LOW)

    @pl.when(step < pl.num_programs(0) // replicas)
    def _():
        all_acts = jnp.concatenate([acts[...], values.astype(LOW)], axis=0)
        grad_out[...] = dot(all_acts, grads[...], 0, 0).astype(LOW)


def weight_grads(mine, rows, others, w_in, w_out, acts, hidden_low, replicas, tile):
    total, width = rows.shape
    hidden = w_in.shape[1]
    count = total // 2
    steps = hidden // tile
    own = steps // replicas

    def column(i, mine):
        return (0, lax.rem(i + mine[0] * own, steps))

    def row(i, mine):
        return (lax.rem(i + mine[0] * own, steps), 0)

    def fixed(i, mine):
        return (0, 0)

    return pl.pallas_call(
        weights_kernel,
        grid_spec=pltpu.PrefetchScalarGridSpec(
            num_scalar_prefetch=1,
            grid=(steps,),
            in_specs=[
                pl.BlockSpec((total, width), fixed),
                pl.BlockSpec((total, width), fixed),
                pl.BlockSpec((width, tile), column),
                pl.BlockSpec((tile, width), row),
                pl.BlockSpec((count, tile), column),
                pl.BlockSpec((count, tile), column),
            ],
            out_specs=(
                pl.BlockSpec((width // replicas, tile), column),
                pl.BlockSpec((tile, width), lambda i, mine: (jnp.minimum(i, own - 1), 0)),
            ),
            scratch_shapes=[
                tiles_of(total, width),
                pltpu.VMEM((count, width), LOW),
                pltpu.VMEM((2 * count, width), LOW),
                pltpu.VMEM((width // replicas, 2 * count), LOW),
            ],
        ),
        out_shape=(
            jax.ShapeDtypeStruct((width // replicas, hidden), LOW),
            jax.ShapeDtypeStruct((hidden // replicas, width), LOW),
        ),
        compiler_params=params_of(),
        cost_estimate=pl.CostEstimate(
            flops=(4 + 8 // replicas) * count * hidden * width,
            bytes_accessed=(4 + 4 // replicas) * hidden * width,
            transcendentals=count * hidden,
        ),
        name="weight_grads",
    )(mine, rows, others, w_in, w_out, acts, hidden_low)


def logits_kernel(back, tokens, params, grads, dispatch, combine, left, right, local, wide):
    images = tokens.shape[0]
    slots = params.shape[0]
    stride = 2 * images
    fill(wide, back[...])
    total = jnp.zeros(local.shape, WIDE)
    for image in range(images):
        slot_out = take(wide, 2 * image, slots, stride).astype(LOW)
        d_slot_in = take(wide, 2 * image + 1, slots, stride).astype(LOW)
        over_tokens = dispatch[image]
        over_slots = combine[image]
        d_combine = dot(slot_out, grads[image], 1, 1)
        d_dispatch = dot(d_slot_in, tokens[image], 1, 1)
        d_logits = over_slots * (
            d_combine - jnp.sum(over_slots * d_combine, axis=0, keepdims=True)
        )
        d_logits += over_tokens * (
            d_dispatch - jnp.sum(over_tokens * d_dispatch, axis=1, keepdims=True)
        )
        low = d_logits.astype(LOW)
        left[image, :slots, :] = over_tokens.astype(LOW)
        left[image, slots:, :] = low
        right[image, :slots, :] = d_slot_in
        right[image, slots:, :] = params[...]
        total += dot(low, tokens[image], 1, 0)
    local[...] = total


def logits_grads(back, tokens, params, grads, dispatch, combine):
    images, length, width = tokens.shape
    slots = params.shape[0]
    return pl.pallas_call(
        logits_kernel,
        out_shape=(
            jax.ShapeDtypeStruct((images, 2 * slots, length), LOW),
            jax.ShapeDtypeStruct((images, 2 * slots, width), LOW),
            jax.ShapeDtypeStruct((slots, width), WIDE),
        ),
        in_specs=[WHOLE] * 6,
        out_specs=(WHOLE,) * 3,
        scratch_shapes=[tiles_of(*back.shape)],
        compiler_params=params_of(),
        cost_estimate=pl.CostEstimate(
            flops=6 * images * slots * length * width,
            bytes_accessed=4 * images * length * width,
            transcendentals=0,
        ),
        name="logits_grads",
    )(back, tokens, params, grads, dispatch, combine)


def tokens_kernel(left, right, out):
    out[0] = dot(left[0], right[0], 0, 0).astype(LOW)


def tokens_grads(left, right):
    images, deep, length = left.shape
    width = right.shape[2]
    return pl.pallas_call(
        tokens_kernel,
        grid=(images,),
        out_shape=jax.ShapeDtypeStruct((images, length, width), LOW),
        in_specs=[
            pl.BlockSpec((1, deep, length), lambda i: (i, 0, 0)),
            pl.BlockSpec((1, deep, width), lambda i: (i, 0, 0)),
        ],
        out_specs=pl.BlockSpec((1, length, width), lambda i: (i, 0, 0)),
        compiler_params=params_of(),
        cost_estimate=pl.CostEstimate(
            flops=2 * images * deep * length * width,
            bytes_accessed=2 * images * length * width,
            transcendentals=0,
        ),
        name="tokens_grads",
    )(left, right)


def sum_everywhere(part, axes):
    count = lax.axis_size(axes)
    pieces = part.reshape(count, -1)
    pieces = lax.all_to_all(pieces, axes, split_axis=0, concat_axis=0, tiled=True)
    mine = jnp.sum(pieces, axis=0, keepdims=True)
    mine = jnp.broadcast_to(mine, pieces.shape)
    whole = lax.all_to_all(mine, axes, split_axis=0, concat_axis=0, tiled=True)
    return whole.reshape(part.shape)


def body(tokens, slot_params, expert_in, expert_out, grad_out):
    weight_in = expert_in[0]
    weight_out = expert_out[0]
    params = slot_params.T
    replicas = lax.axis_size("rep")
    mine = lax.axis_index("rep").astype(jnp.int32).reshape(1)

    sent, dispatch, combine = gather(tokens, params, grad_out)
    rows = lax.all_to_all(sent, "exp", split_axis=0, concat_axis=0, tiled=True)
    others = lax.ppermute(rows, "rep", [(i, (i + 1) % replicas) for i in range(replicas)])
    back, acts, hidden = expert(rows, weight_in, weight_out, 512)
    back = lax.all_to_all(back, "exp", split_axis=0, concat_axis=0, tiled=True)
    grad_expert_in, grad_expert_out = weight_grads(
        mine, rows, others, weight_in, weight_out, acts, hidden, replicas, 256
    )
    left, right, local = logits_grads(back, tokens, params, grad_out, dispatch, combine)
    grad_params = sum_everywhere(local, ("rep", "exp")).T
    grad_tokens = tokens_grads(left, right)
    return (grad_tokens, grad_params, grad_expert_in[None], grad_expert_out[None])


def solution(mesh):
    in_specs = (
        P(("rep", "exp"), None, None),
        P(),
        P("exp", None, None),
        P("exp", None, None),
        P(("rep", "exp"), None, None),
    )
    out_specs = (P(("rep", "exp"), None, None), P(), P("exp", "rep", None), P("exp", "rep", None))
    return jax.shard_map(body, mesh=mesh, in_specs=in_specs, out_specs=out_specs, check_vma=False)
```

```python
import math

import jax
import jax.numpy as jnp
from jax import lax
from jax.experimental import pallas as pl
from jax.experimental.pallas import tpu as pltpu
from jax.sharding import PartitionSpec as P

GELU_C = math.sqrt(2.0 / math.pi)
CUBIC = 0.044715
LOW = jnp.bfloat16
WIDE = jnp.float32
LANES = 128
FOLD = 2
VMEM_BYTES = 60 * 1024 * 1024
WHOLE = pl.BlockSpec(memory_space=pltpu.VMEM)
PLACE = pl.BlockSpec(memory_space=pl.ANY)


def call(kernel, name, flops, nbytes, exps=0, **kwargs):
    return pl.pallas_call(
        kernel,
        name=name,
        compiler_params=pltpu.CompilerParams(vmem_limit_bytes=VMEM_BYTES),
        cost_estimate=pl.CostEstimate(
            flops=flops, bytes_accessed=nbytes, transcendentals=exps
        ),
        **kwargs,
    )


def shaped(shape, dtype):
    return jax.ShapeDtypeStruct(shape, dtype)


def gelu_parts(values):
    square = values * values
    tangent = jnp.tanh(GELU_C * (values + CUBIC * square * values))
    half = 0.5 * (1.0 + tangent)
    slope = half + 0.5 * values * (1.0 - tangent * tangent) * GELU_C * (1.0 + 3.0 * CUBIC * square)
    return values * half, slope


def dot(left, right, over_left, over_right):
    return lax.dot_general(
        left, right, (((over_left,), (over_right,)), ((), ())), preferred_element_type=WIDE
    )


def softmax(values, axis):
    raised = jnp.exp(values - jnp.max(values, axis=axis, keepdims=True))
    return raised / jnp.sum(raised, axis=axis, keepdims=True)


def scratch_rows(shape):
    return pltpu.VMEM((shape[1] // LANES, shape[0], LANES), WIDE)


def load_rows(ref, array):
    for tile in range(ref.shape[0]):
        ref[tile] = array[:, tile * LANES : (tile + 1) * LANES].astype(WIDE)


def packed(ref):
    return jnp.concatenate([ref[tile] for tile in range(ref.shape[0])], axis=1).astype(LOW)


def take_part(ref, start, count, stride):
    picked = [ref[tile, pl.ds(start, count, stride=stride), :] for tile in range(ref.shape[0])]
    return jnp.concatenate(picked, axis=1)


def take(ref, start, count, stride):
    parts = [take_part(ref, start + part, count, stride) for part in range(FOLD)]
    return jnp.concatenate(parts, axis=1).astype(LOW)


def put(ref, start, count, stride, array):
    tiles = ref.shape[0]
    for part in range(FOLD):
        for tile in range(tiles):
            at = (part * tiles + tile) * LANES
            ref[tile, pl.ds(start + part, count, stride=stride), :] = array[:, at : at + LANES]


def start_copies(source, target, sems):
    copies = []
    for index in range(source.shape[0]):
        copy = pltpu.make_async_copy(source.at[index], target.at[index], sems.at[index])
        copy.start()
        copies.append(copy)
    return copies


def slot_in_kernel(tokens, params, sent, dispatch, combine, tokens_v, rows, sems):
    images = tokens.shape[0]
    slots = params.shape[0]
    copies = start_copies(tokens, tokens_v, sems)
    logits = []
    for image in range(images):
        copies[image].wait()
        logits.append(dot(params[...], tokens_v[image], 1, 1))
    for image in range(images):
        over_tokens = softmax(logits[image], 1)
        dispatch[image] = over_tokens
        value = dot(over_tokens.astype(LOW), tokens_v[image], 1, 0)
        put(rows, FOLD * image, slots, FOLD * images, value)
    for image in range(images):
        combine[image] = softmax(logits[image], 0)
    sent[...] = packed(rows)


def slot_in_rows(tokens, params):
    images, length, width = tokens.shape
    slots = params.shape[0]
    weights = shaped((images, slots, length), WIDE)
    rows = (slots * images * FOLD, width // FOLD)
    return call(
        slot_in_kernel,
        "slot_in",
        4 * images * slots * length * width,
        2 * images * length * width,
        2 * images * slots * length,
        out_shape=(shaped(rows, LOW), weights, weights),
        in_specs=[PLACE, WHOLE],
        out_specs=(WHOLE, WHOLE, WHOLE),
        scratch_shapes=[
            pltpu.VMEM(tokens.shape, LOW),
            scratch_rows(rows),
            pltpu.SemaphoreType.DMA((images,)),
        ],
    )(tokens, params)


def slot_grad_kernel(grads, combine, sent, grads_v, rows, sems):
    images = grads.shape[0]
    slots = combine.shape[1]
    copies = start_copies(grads, grads_v, sems)
    for image in range(images):
        copies[image].wait()
        value = dot(combine[image].astype(LOW), grads_v[image], 1, 0)
        put(rows, FOLD * image, slots, FOLD * images, value)
    sent[...] = packed(rows)


def slot_grad_rows(grads, combine):
    images, length, width = grads.shape
    slots = combine.shape[1]
    rows = (slots * images * FOLD, width // FOLD)
    return call(
        slot_grad_kernel,
        "slot_grad",
        2 * images * slots * length * width,
        2 * images * length * width,
        out_shape=shaped(rows, LOW),
        in_specs=[PLACE, WHOLE],
        out_specs=WHOLE,
        scratch_shapes=[
            pltpu.VMEM(grads.shape, LOW),
            scratch_rows(rows),
            pltpu.SemaphoreType.DMA((images,)),
        ],
    )(grads, combine)


def unfold(source, wide, low):
    load_rows(wide, source[...])
    low[...] = take(wide, 0, low.shape[0], FOLD)


def forward_kernel(rows, w_in, w_out, back, acts, slopes, wide, low, total):
    step = pl.program_id(0)

    @pl.when(step == 0)
    def _():
        unfold(rows, wide, low)
        total[...] = jnp.zeros_like(total)

    values, slope = gelu_parts(dot(low[...], w_in[...], 1, 0))
    values = values.astype(LOW)
    acts[...] = values
    slopes[...] = slope
    total[...] += dot(values, w_out[...], 1, 0)

    @pl.when(step == pl.num_programs(0) - 1)
    def _():
        put(wide, 0, low.shape[0], FOLD, total[...])
        back[...] = packed(wide)


def backward_kernel(rows, slopes, w_in, w_out, back, hidden, wide, low, total):
    step = pl.program_id(0)

    @pl.when(step == 0)
    def _():
        unfold(rows, wide, low)
        total[...] = jnp.zeros_like(total)

    values = (dot(low[...], w_out[...], 1, 1) * slopes[...]).astype(LOW)
    hidden[...] = values
    total[...] += dot(values, w_in[...], 1, 1)

    @pl.when(step == pl.num_programs(0) - 1)
    def _():
        put(wide, 0, low.shape[0], FOLD, total[...])
        back[...] = packed(wide)


def others_kernel(after, rows, grad_rows, w_in, w_out, acts, hidden, wide, low, low_grads):
    del after

    @pl.when(pl.program_id(0) == 0)
    def _():
        unfold(rows, wide, low)
        unfold(grad_rows, wide, low_grads)

    values, slope = gelu_parts(dot(low[...], w_in[...], 1, 0))
    acts[...] = values.astype(LOW)
    hidden[...] = (dot(low_grads[...], w_out[...], 1, 1) * slope).astype(LOW)


class Expert:
    def __init__(self, rows, w_in, w_out, tile):
        self.weights = (w_in, w_out)
        self.folded, part = rows.shape
        self.part = part
        self.width, self.hidden = w_in.shape
        self.count = self.folded // FOLD
        self.grid = (self.hidden // tile,)
        self.rows = pl.BlockSpec(rows.shape, lambda i: (0, 0))
        self.columns = pl.BlockSpec((self.count, tile), lambda i: (0, i))
        self.w_specs = [
            pl.BlockSpec((self.width, tile), lambda i: (0, i)),
            pl.BlockSpec((tile, self.width), lambda i: (i, 0)),
        ]
        self.back = shaped(rows.shape, LOW)
        self.kept = shaped((self.count, self.hidden), LOW)
        self.low = pltpu.VMEM((self.count, self.width), LOW)
        self.cost = (
            4 * self.count * self.hidden * self.width,
            4 * self.hidden * self.width,
            self.count * self.hidden,
        )
        self.wide = scratch_rows(rows.shape)
        self.total = pltpu.VMEM((self.count, self.width), WIDE)

    def forward(self, rows):
        return call(
            forward_kernel,
            "expert_forward",
            *self.cost,
            grid=self.grid,
            out_shape=(self.back, self.kept, shaped(self.kept.shape, WIDE)),
            in_specs=[self.rows, *self.w_specs],
            out_specs=(self.rows, self.columns, self.columns),
            scratch_shapes=[self.wide, self.low, self.total],
        )(rows, *self.weights)

    def backward(self, rows, slopes):
        return call(
            backward_kernel,
            "expert_backward",
            *self.cost,
            grid=self.grid,
            out_shape=(self.back, self.kept),
            in_specs=[self.rows, self.columns, *self.w_specs],
            out_specs=(self.rows, self.columns),
            scratch_shapes=[self.wide, self.low, self.total],
        )(rows, slopes, *self.weights)

    def others(self, after, rows, grad_rows):
        return call(
            others_kernel,
            "expert_others",
            *self.cost,
            grid=self.grid,
            out_shape=(self.kept, self.kept),
            in_specs=[PLACE, self.rows, self.rows, *self.w_specs],
            out_specs=(self.columns, self.columns),
            scratch_shapes=[self.wide, self.low, self.low],
        )(after, rows, grad_rows, *self.weights)


def weights_kernel(
    mine,
    after,
    rows,
    grad_rows,
    other_rows,
    other_grad_rows,
    acts,
    other_acts,
    hidden,
    other_hidden,
    grad_in,
    grad_out,
    wide,
    grads,
    turned,
):
    del after
    count = rows.shape[0] // FOLD

    @pl.when(pl.program_id(0) == 0)
    def _():
        left = []
        for source in (rows, other_rows):
            load_rows(wide, source[...])
            parts = [take_part(wide, part, count, FOLD) for part in range(FOLD)]
            left.append(jnp.where(mine[0] == 0, parts[0], parts[1]))
        turned[...] = jnp.concatenate(left, axis=0).T.astype(LOW)
        unfold(grad_rows, wide, grads.at[pl.ds(0, count)])
        unfold(other_grad_rows, wide, grads.at[pl.ds(count, count)])

    all_hidden = jnp.concatenate([hidden[...], other_hidden[...]], axis=0)
    grad_in[...] = dot(turned[...], all_hidden, 1, 0).astype(LOW)
    all_acts = jnp.concatenate([acts[...], other_acts[...]], axis=0)
    grad_out[...] = dot(all_acts, grads[...], 0, 0).astype(LOW)


def weight_grads(mine, after, rows, grad_rows, acts, hidden, steps, replicas):
    folded, part = rows[0].shape
    width = part * FOLD
    size = acts[0].shape[1]
    count = folded // FOLD
    in_tile, out_tile = size // steps, size // replicas // steps
    whole_rows = pl.BlockSpec((folded, part), lambda i, mine: (0, 0))
    acts_spec = pl.BlockSpec((count, out_tile), lambda i, mine: (0, mine[0] * steps + i))
    hidden_spec = pl.BlockSpec((count, in_tile), lambda i, mine: (0, i))
    return call(
        weights_kernel,
        "weight_grads",
        8 * count * size * width // replicas,
        4 * size * width // replicas,
        grid_spec=pltpu.PrefetchScalarGridSpec(
            num_scalar_prefetch=1,
            grid=(steps,),
            in_specs=[PLACE] + [whole_rows] * 4 + [acts_spec] * 2 + [hidden_spec] * 2,
            out_specs=(
                pl.BlockSpec((width // replicas, in_tile), lambda i, mine: (0, i)),
                pl.BlockSpec((out_tile, width), lambda i, mine: (i, 0)),
            ),
            scratch_shapes=[
                scratch_rows((folded, part)),
                pltpu.VMEM((2 * count, width), LOW),
                pltpu.VMEM((width // replicas, 2 * count), LOW),
            ],
        ),
        out_shape=(
            shaped((width // replicas, size), LOW),
            shaped((size // replicas, width), LOW),
        ),
    )(mine, after, rows[0], grad_rows[0], rows[1], grad_rows[1], *acts, *hidden)


def combine_kernel(after, back, grads, combine, part, grads_v, wide, sems):
    del after
    images, slots, _ = combine.shape
    copies = start_copies(grads, grads_v, sems)
    load_rows(wide, back[...])
    for image in range(images):
        slot_out = take(wide, FOLD * image, slots, FOLD * images)
        weights = combine[image]
        copies[image].wait()
        d_combine = dot(slot_out, grads_v[image], 1, 1)
        part[image] = weights * (
            d_combine - jnp.sum(weights * d_combine, axis=0, keepdims=True)
        )


def combine_part(after, back, grads, combine):
    images, length, width = grads.shape
    slots = combine.shape[1]
    return call(
        combine_kernel,
        "combine_part",
        2 * images * slots * length * width,
        2 * images * length * width,
        out_shape=shaped(combine.shape, WIDE),
        in_specs=[PLACE, WHOLE, PLACE, WHOLE],
        out_specs=WHOLE,
        scratch_shapes=[
            pltpu.VMEM(grads.shape, LOW),
            scratch_rows(back.shape),
            pltpu.SemaphoreType.DMA((images,)),
        ],
    )(after, back, grads, combine)


def logits_kernel(
    after, back, tokens, params, dispatch, part, left, right, local, tokens_v, wide, sems
):
    del after
    images, slots, _ = dispatch.shape
    copies = start_copies(tokens, tokens_v, sems)
    load_rows(wide, back[...])
    total = jnp.zeros(params.shape, WIDE)
    for image in range(images):
        d_slot_in = take(wide, FOLD * image, slots, FOLD * images)
        right[image, :slots, :] = d_slot_in
        right[image, slots:, :] = params[...]
        weights = dispatch[image]
        copies[image].wait()
        d_dispatch = dot(d_slot_in, tokens_v[image], 1, 1)
        d_logits = part[image] + weights * (
            d_dispatch - jnp.sum(weights * d_dispatch, axis=1, keepdims=True)
        )
        low = d_logits.astype(LOW)
        left[image, :slots, :] = weights.astype(LOW)
        left[image, slots:, :] = low
        total += dot(low, tokens_v[image], 1, 0)
    for slot in range(slots):
        local[slot] = total[slot : slot + 1, :]


def logits_grads(after, back, tokens, params, dispatch, part):
    images, length, width = tokens.shape
    slots = params.shape[0]
    return call(
        logits_kernel,
        "logits_grads",
        4 * images * slots * length * width,
        2 * images * length * width,
        out_shape=(
            shaped((images, 2 * slots, length), LOW),
            shaped((images, 2 * slots, width), LOW),
            shaped((slots, 1, width), WIDE),
        ),
        in_specs=[PLACE, WHOLE, PLACE, WHOLE, WHOLE, WHOLE],
        out_specs=(WHOLE,) * 3,
        scratch_shapes=[
            pltpu.VMEM(tokens.shape, LOW),
            scratch_rows(back.shape),
            pltpu.SemaphoreType.DMA((images,)),
        ],
    )(after, back, tokens, params, dispatch, part)


def tokens_kernel(after, left, right, out):
    del after
    out[0] = dot(left[0], right[0], 0, 0).astype(LOW)


def tokens_grads(after, left, right):
    images, deep, length = left.shape
    width = right.shape[2]
    return call(
        tokens_kernel,
        "tokens_grads",
        2 * images * deep * length * width,
        2 * images * length * width,
        grid=(images,),
        out_shape=shaped((images, length, width), LOW),
        in_specs=[
            PLACE,
            pl.BlockSpec((1, deep, length), lambda i: (i, 0, 0)),
            pl.BlockSpec((1, deep, width), lambda i: (i, 0, 0)),
        ],
        out_specs=pl.BlockSpec((1, length, width), lambda i: (i, 0, 0)),
    )(after, left, right)


def exchange(rows):
    return lax.all_to_all(rows, "exp", split_axis=0, concat_axis=0, tiled=True)


def body(tokens, slot_params, expert_in, expert_out, grad_out):
    params = slot_params.T
    replicas = lax.axis_size("rep")
    mine = lax.axis_index("rep").astype(jnp.int32).reshape(1)

    def swap(array):
        return lax.ppermute(array, "rep", [(i, (i + 1) % replicas) for i in range(replicas)])

    sent, dispatch, combine = slot_in_rows(tokens, params)
    rows = exchange(sent)
    grad_rows = exchange(slot_grad_rows(grad_out, combine))
    expert = Expert(rows, expert_in[0], expert_out[0], 512)
    other_rows = swap(rows)
    back, acts, slopes = expert.forward(rows)
    back = exchange(back)
    other_grad_rows = swap(grad_rows)
    d_back, hidden = expert.backward(grad_rows, slopes)
    part = combine_part(hidden, back, grad_out, combine)
    other_acts, other_hidden = expert.others(hidden, other_rows, other_grad_rows)
    d_back = exchange(d_back)
    left, right, local = logits_grads(other_hidden, d_back, tokens, params, dispatch, part)

    share = jnp.sum(exchange(local), axis=0, keepdims=True)
    grad_expert_in, grad_expert_out = weight_grads(
        mine,
        local,
        (rows, other_rows),
        (grad_rows, other_grad_rows),
        (acts, other_acts),
        (hidden, other_hidden),
        5,
        replicas,
    )
    share = share + swap(share)
    grad_params = exchange(jnp.broadcast_to(share, local.shape))
    grad_tokens = tokens_grads(share, left, right)
    return (
        grad_tokens,
        grad_params.reshape(params.shape).T,
        grad_expert_in[None],
        grad_expert_out[None],
    )


def solution(mesh):
    in_specs = (
        P(("rep", "exp"), None, None),
        P(),
        P("exp", None, None),
        P("exp", None, None),
        P(("rep", "exp"), None, None),
    )
    out_specs = (P(("rep", "exp"), None, None), P(), P("exp", "rep", None), P("exp", "rep", None))
    return jax.shard_map(body, mesh=mesh, in_specs=in_specs, out_specs=out_specs, check_vma=False)
```

```python
import math

import jax
import jax.numpy as jnp
from jax import lax
from jax.experimental import pallas as pl
from jax.experimental.pallas import tpu as pltpu
from jax.sharding import PartitionSpec as P

GELU_C = math.sqrt(2.0 / math.pi)
CUBIC = 0.044715
LOW = jnp.bfloat16
WIDE = jnp.float32
LANES = 128
KINDS = 2
VMEM_BYTES = 60 * 1024 * 1024
WHOLE = pl.BlockSpec(memory_space=pltpu.VMEM)
FAR = pl.BlockSpec(memory_space=pltpu.HBM)
PLACE = pl.BlockSpec(memory_space=pl.ANY)


def call(kernel, name, flops, nbytes, exps=0, **kwargs):
    return pl.pallas_call(
        kernel,
        name=name,
        compiler_params=pltpu.CompilerParams(vmem_limit_bytes=VMEM_BYTES),
        cost_estimate=pl.CostEstimate(
            flops=flops, bytes_accessed=nbytes, transcendentals=exps
        ),
        **kwargs,
    )


def shaped(shape, dtype):
    return jax.ShapeDtypeStruct(shape, dtype)


def gelu_parts(values):
    square = values * values
    tangent = jnp.tanh(GELU_C * (values + CUBIC * square * values))
    half = 0.5 * (1.0 + tangent)
    slope = half + 0.5 * values * (1.0 - tangent * tangent) * GELU_C * (1.0 + 3.0 * CUBIC * square)
    return values * half, slope


def dot(left, right, over_left, over_right):
    return lax.dot_general(
        left, right, (((over_left,), (over_right,)), ((), ())), preferred_element_type=WIDE
    )


def softmax(values, axis):
    raised = jnp.exp(values - jnp.max(values, axis=axis, keepdims=True))
    return raised / jnp.sum(raised, axis=axis, keepdims=True)


def scratch_rows(shape):
    return pltpu.VMEM((shape[1] // LANES, shape[0], LANES), WIDE)


def load_rows(ref, array):
    for tile in range(ref.shape[0]):
        ref[tile] = array[:, tile * LANES : (tile + 1) * LANES].astype(WIDE)


def packed(ref):
    return jnp.concatenate([ref[tile] for tile in range(ref.shape[0])], axis=1).astype(LOW)


def take(ref, start, count, stride, first=0, tiles=None):
    tiles = ref.shape[0] if tiles is None else tiles
    picked = [ref[first + tile, pl.ds(start, count, stride=stride), :] for tile in range(tiles)]
    return jnp.concatenate(picked, axis=1)


def put(ref, start, count, stride, array):
    for tile in range(ref.shape[0]):
        ref[tile, pl.ds(start, count, stride=stride), :] = array[
            :, tile * LANES : (tile + 1) * LANES
        ]


def start_copies(source, target, sems):
    copies = []
    for index in range(source.shape[0]):
        copy = pltpu.make_async_copy(source.at[index], target.at[index], sems.at[index])
        copy.start()
        copies.append(copy)
    return copies


def gather_kernel(
    tokens, params, grads, sent, dispatch, combine, tokens_v, grads_v, rows, sems, grad_sems
):
    images = tokens.shape[0]
    slots = params.shape[0]
    stride = KINDS * images
    copies = start_copies(tokens, tokens_v, sems)
    grad_copies = start_copies(grads, grads_v, grad_sems)
    logits = []
    for image in range(images):
        copies[image].wait()
        logits.append(dot(params[...], tokens_v[image], 1, 1))
    over_slots = []
    for image in range(images):
        over_tokens = softmax(logits[image], 1)
        dispatch[image] = over_tokens
        put(
            rows, KINDS * image, slots, stride, dot(over_tokens.astype(LOW), tokens_v[image], 1, 0)
        )
        over_slots.append(softmax(logits[image], 0))
        combine[image] = over_slots[image]
    for image in range(images):
        grad_copies[image].wait()
        value = dot(over_slots[image].astype(LOW), grads_v[image], 1, 0)
        put(rows, KINDS * image + 1, slots, stride, value)
    sent[...] = packed(rows)


def gather(tokens, params, grads):
    images, length, width = tokens.shape
    slots = params.shape[0]
    weights = shaped((images, slots, length), WIDE)
    rows = (slots * images * KINDS, width)
    return call(
        gather_kernel,
        "gather_slots",
        6 * images * slots * length * width,
        4 * images * length * width,
        2 * images * slots * length,
        out_shape=(shaped(rows, LOW), weights, weights),
        in_specs=[FAR, WHOLE, FAR],
        out_specs=(WHOLE, WHOLE, WHOLE),
        scratch_shapes=[
            pltpu.VMEM(tokens.shape, LOW),
            pltpu.VMEM(grads.shape, LOW),
            scratch_rows(rows),
            pltpu.SemaphoreType.DMA((images,)),
            pltpu.SemaphoreType.DMA((images,)),
        ],
    )(tokens, params, grads)


def start_weights(w_in, w_out, w_in_v, w_out_v, sems):
    chunks, tile = w_out_v.shape[:2]
    copies = []
    for chunk in range(chunks):
        units = pl.ds(chunk * tile, tile)
        pair = (
            pltpu.make_async_copy(w_in.at[:, units], w_in_v.at[chunk], sems.at[0, chunk]),
            pltpu.make_async_copy(w_out.at[units, :], w_out_v.at[chunk], sems.at[1, chunk]),
        )
        for copy in pair:
            copy.start()
        copies.append(pair)
    return copies


def weight_scratch(width, hidden, tile):
    chunks = hidden // tile
    return [
        pltpu.VMEM((chunks, width, tile), LOW),
        pltpu.VMEM((chunks, tile, width), LOW),
        pltpu.SemaphoreType.DMA((2, chunks)),
    ]


def expert_kernel(rows, w_in, w_out, back, acts, hidden, w_in_v, w_out_v, sems, wide):
    copies = start_weights(w_in, w_out, w_in_v, w_out_v, sems)
    count = rows.shape[0] // KINDS
    chunks, tile = w_out_v.shape[:2]
    load_rows(wide, rows[...])
    rows_in = take(wide, 0, count, KINDS).astype(LOW)
    rows_grad = take(wide, 1, count, KINDS).astype(LOW)
    out = d_in = None
    for chunk in range(chunks):
        units = slice(chunk * tile, (chunk + 1) * tile)
        copies[chunk][0].wait()
        preact = dot(rows_in, w_in_v[chunk], 1, 0)
        copies[chunk][1].wait()
        d_acts = dot(rows_grad, w_out_v[chunk], 1, 1)
        values, slope = gelu_parts(preact)
        values = values.astype(LOW)
        d_hidden = (d_acts * slope).astype(LOW)
        acts[:, units] = values
        hidden[:, units] = d_hidden
        out_part = dot(values, w_out_v[chunk], 1, 0)
        d_in_part = dot(d_hidden, w_in_v[chunk], 1, 1)
        out = out_part if chunk == 0 else out + out_part
        d_in = d_in_part if chunk == 0 else d_in + d_in_part
    put(wide, 0, count, KINDS, out)
    put(wide, 1, count, KINDS, d_in)
    back[...] = packed(wide)


def expert(rows, w_in, w_out, tile):
    total, width = rows.shape
    hidden = w_in.shape[1]
    count = total // KINDS
    kept = shaped((count, hidden), LOW)
    return call(
        expert_kernel,
        "expert_rows",
        8 * count * hidden * width,
        4 * hidden * width,
        count * hidden,
        out_shape=(shaped(rows.shape, LOW), kept, kept),
        in_specs=[WHOLE, FAR, FAR],
        out_specs=(WHOLE,) * 3,
        scratch_shapes=[*weight_scratch(width, hidden, tile), scratch_rows(rows.shape)],
    )(rows, w_in, w_out)


def others_kernel(after, rows, w_in, w_out, acts, hidden, w_in_v, w_out_v, sems, wide):
    del after
    copies = start_weights(w_in, w_out, w_in_v, w_out_v, sems)
    count = rows.shape[0] // KINDS
    chunks, tile = w_out_v.shape[:2]
    load_rows(wide, rows[...])
    rows_in = take(wide, 0, count, KINDS).astype(LOW)
    rows_grad = take(wide, 1, count, KINDS).astype(LOW)
    for chunk in range(chunks):
        units = slice(chunk * tile, (chunk + 1) * tile)
        copies[chunk][0].wait()
        values, slope = gelu_parts(dot(rows_in, w_in_v[chunk], 1, 0))
        acts[:, units] = values.astype(LOW)
        copies[chunk][1].wait()
        d_acts = dot(rows_grad, w_out_v[chunk], 1, 1)
        hidden[:, units] = (d_acts * slope).astype(LOW)


def others_hidden(after, rows, w_in, w_out, tile):
    total, width = rows.shape
    hidden = w_in.shape[1]
    count = total // KINDS
    kept = shaped((count, hidden), LOW)
    return call(
        others_kernel,
        "others_hidden",
        64 * count * hidden * width,
        32 * hidden * width,
        count * hidden,
        out_shape=(kept, kept),
        in_specs=[PLACE, WHOLE, FAR, FAR],
        out_specs=(WHOLE,) * 2,
        scratch_shapes=[*weight_scratch(width, hidden, tile), scratch_rows(rows.shape)],
    )(after, rows, w_in, w_out)


def weights_kernel(
    mine, after, rows, other_rows, acts, other_acts, hidden, other_hidden, grad_in, grad_out,
    wide, grads, turned,
):
    del after
    count = rows.shape[0] // KINDS

    @pl.when(pl.program_id(0) == 0)
    def _():
        left, right = [], []
        tiles = turned.shape[0] // LANES
        for source in (rows, other_rows):
            load_rows(wide, source[...])
            left.append(take(wide, 0, count, KINDS, mine[0] * tiles, tiles))
            right.append(take(wide, 1, count, KINDS))
        turned[...] = jnp.concatenate(left, axis=0).T.astype(LOW)
        grads[...] = jnp.concatenate(right, axis=0).astype(LOW)

    all_hidden = jnp.concatenate([hidden[...], other_hidden[...]], axis=0)
    grad_in[...] = dot(turned[...], all_hidden, 1, 0).astype(LOW)
    all_acts = jnp.concatenate([acts[...], other_acts[...]], axis=0)
    grad_out[...] = dot(all_acts, grads[...], 0, 0).astype(LOW)


def weight_grads(mine, after, rows, acts, hidden, steps, replicas):
    total, width = rows[0].shape
    size = acts[0].shape[1]
    count = total // KINDS
    in_tile, out_tile = size // steps, size // replicas // steps
    whole_rows = pl.BlockSpec((total, width), lambda i, mine: (0, 0))
    acts_spec = pl.BlockSpec((count, out_tile), lambda i, mine: (0, mine[0] * steps + i))
    hidden_spec = pl.BlockSpec((count, in_tile), lambda i, mine: (0, i))
    return call(
        weights_kernel,
        "weight_grads",
        8 * count * size * width // replicas,
        4 * size * width // replicas,
        grid_spec=pltpu.PrefetchScalarGridSpec(
            num_scalar_prefetch=1,
            grid=(steps,),
            in_specs=[PLACE] + [whole_rows] * 2 + [acts_spec] * 2 + [hidden_spec] * 2,
            out_specs=(
                pl.BlockSpec((width // replicas, in_tile), lambda i, mine: (0, i)),
                pl.BlockSpec((out_tile, width), lambda i, mine: (i, 0)),
            ),
            scratch_shapes=[
                scratch_rows((total, width)),
                pltpu.VMEM((2 * count, width), LOW),
                pltpu.VMEM((width // replicas, 2 * count), LOW),
            ],
        ),
        out_shape=(
            shaped((width // replicas, size), LOW),
            shaped((size // replicas, width), LOW),
        ),
    )(mine, after, *rows, *acts, *hidden)


def logits_kernel(
    after, back, tokens, params, grads, dispatch, combine, left, right, local,
    tokens_v, grads_v, wide, sems, grad_sems,
):
    del after
    images, slots, _ = dispatch.shape
    grad_copies = start_copies(grads, grads_v, grad_sems)
    copies = start_copies(tokens, tokens_v, sems)
    load_rows(wide, back[...])
    stride = KINDS * images
    parts = []
    for image in range(images):
        slot_out = take(wide, KINDS * image, slots, stride).astype(LOW)
        weights = combine[image]
        grad_copies[image].wait()
        d_combine = dot(slot_out, grads_v[image], 1, 1)
        parts.append(
            weights * (d_combine - jnp.sum(weights * d_combine, axis=0, keepdims=True))
        )
    total = jnp.zeros(params.shape, WIDE)
    for image in range(images):
        d_slot_in = take(wide, KINDS * image + 1, slots, stride).astype(LOW)
        right[image, :slots, :] = d_slot_in
        right[image, slots:, :] = params[...]
        weights = dispatch[image]
        copies[image].wait()
        d_dispatch = dot(d_slot_in, tokens_v[image], 1, 1)
        d_logits = parts[image] + weights * (
            d_dispatch - jnp.sum(weights * d_dispatch, axis=1, keepdims=True)
        )
        low = d_logits.astype(LOW)
        left[image, :slots, :] = weights.astype(LOW)
        left[image, slots:, :] = low
        total += dot(low, tokens_v[image], 1, 0)
    pieces, _, size = local.shape
    for slot in range(slots):
        for piece in range(pieces // slots):
            local[slot * (pieces // slots) + piece] = total[
                slot : slot + 1, piece * size : (piece + 1) * size
            ]


def logits_grads(after, back, tokens, params, grads, dispatch, combine, pieces):
    images, length, width = tokens.shape
    slots = params.shape[0]
    return call(
        logits_kernel,
        "logits_grads",
        6 * images * slots * length * width,
        4 * images * length * width,
        out_shape=(
            shaped((images, 2 * slots, length), LOW),
            shaped((images, 2 * slots, width), LOW),
            shaped((pieces, 1, slots * width // pieces), WIDE),
        ),
        in_specs=[PLACE, WHOLE, FAR, WHOLE, FAR, WHOLE, WHOLE],
        out_specs=(WHOLE,) * 3,
        scratch_shapes=[
            pltpu.VMEM(tokens.shape, LOW),
            pltpu.VMEM(grads.shape, LOW),
            scratch_rows(back.shape),
            pltpu.SemaphoreType.DMA((images,)),
            pltpu.SemaphoreType.DMA((images,)),
        ],
    )(after, back, tokens, params, grads, dispatch, combine)


def tokens_kernel(after, left, right, out):
    del after
    out[0] = dot(left[0], right[0], 0, 0).astype(LOW)


def tokens_grads(after, left, right):
    images, deep, length = left.shape
    width = right.shape[2]
    return call(
        tokens_kernel,
        "tokens_grads",
        2 * images * deep * length * width,
        2 * images * length * width,
        grid=(images,),
        out_shape=shaped((images, length, width), LOW),
        in_specs=[
            PLACE,
            pl.BlockSpec((1, deep, length), lambda i: (i, 0, 0)),
            pl.BlockSpec((1, deep, width), lambda i: (i, 0, 0)),
        ],
        out_specs=pl.BlockSpec((1, length, width), lambda i: (i, 0, 0)),
    )(after, left, right)


def exchange(rows, axes):
    return lax.all_to_all(rows, axes, split_axis=0, concat_axis=0, tiled=True)


def body(tokens, slot_params, expert_in, expert_out, grad_out):
    params = slot_params.T
    weights = (expert_in[0], expert_out[0])
    replicas = lax.axis_size("rep")
    everyone = ("rep", "exp")
    mine = lax.axis_index("rep").astype(jnp.int32).reshape(1)

    sent, dispatch, combine = gather(tokens, params, grad_out)
    rows = exchange(sent, "exp")
    other_rows = lax.ppermute(rows, "rep", [(i, (i + 1) % replicas) for i in range(replicas)])
    back, acts, hidden = expert(rows, *weights, 512)
    other_acts, other_hidden = others_hidden(hidden, other_rows, *weights, 512)
    back = exchange(back, "exp")
    left, right, local = logits_grads(
        other_hidden, back, tokens, params, grad_out, dispatch, combine, lax.axis_size(everyone)
    )
    share = jnp.sum(exchange(local, everyone), axis=0, keepdims=True)
    grad_expert_in, grad_expert_out = weight_grads(
        mine, local, (rows, other_rows), (acts, other_acts), (hidden, other_hidden), 5, replicas
    )
    grad_params = exchange(jnp.broadcast_to(share, local.shape), everyone)
    grad_tokens = tokens_grads(share, left, right)
    return (
        grad_tokens,
        grad_params.reshape(params.shape).T,
        grad_expert_in[None],
        grad_expert_out[None],
    )


def solution(mesh):
    in_specs = (
        P(("rep", "exp"), None, None),
        P(),
        P("exp", None, None),
        P("exp", None, None),
        P(("rep", "exp"), None, None),
    )
    out_specs = (P(("rep", "exp"), None, None), P(), P("exp", "rep", None), P("exp", "rep", None))
    return jax.shard_map(body, mesh=mesh, in_specs=in_specs, out_specs=out_specs, check_vma=False)
```

```python
import math

import jax
import jax.numpy as jnp
from jax import lax
from jax.experimental import pallas as pl
from jax.experimental.pallas import tpu as pltpu
from jax.sharding import PartitionSpec as P

GELU_C = math.sqrt(2.0 / math.pi)
CUBIC = 0.044715
LOW = jnp.bfloat16
WIDE = jnp.float32
LANES = 128
KINDS = 2
ALONE = 60 * 1024 * 1024
SHARED = 52 * 1024 * 1024
WHOLE = pl.BlockSpec(memory_space=pltpu.VMEM)
PLACE = pl.BlockSpec(memory_space=pl.ANY)


def call(kernel, name, grant, flops, nbytes, exps=0, **kwargs):
    return pl.pallas_call(
        kernel,
        name=name,
        compiler_params=pltpu.CompilerParams(vmem_limit_bytes=grant),
        cost_estimate=pl.CostEstimate(
            flops=flops, bytes_accessed=nbytes, transcendentals=exps
        ),
        **kwargs,
    )


def shaped(shape, dtype):
    return jax.ShapeDtypeStruct(shape, dtype)


MARK = shaped((8, LANES), WIDE)


def gelu_parts(values):
    square = values * values
    tangent = jnp.tanh(GELU_C * (values + CUBIC * square * values))
    half = 0.5 * (1.0 + tangent)
    slope = half + 0.5 * values * (1.0 - tangent * tangent) * GELU_C * (1.0 + 3.0 * CUBIC * square)
    return values * half, slope


def dot(left, right, over_left, over_right):
    return lax.dot_general(
        left, right, (((over_left,), (over_right,)), ((), ())), preferred_element_type=WIDE
    )


def softmax(values, axis):
    raised = jnp.exp(values - jnp.max(values, axis=axis, keepdims=True))
    return raised / jnp.sum(raised, axis=axis, keepdims=True)


def scratch_rows(shape):
    return pltpu.VMEM((shape[1] // LANES, shape[0], LANES), WIDE)


def load_rows(ref, array):
    for tile in range(ref.shape[0]):
        ref[tile] = array[:, tile * LANES : (tile + 1) * LANES].astype(WIDE)


def packed(ref):
    return jnp.concatenate([ref[tile] for tile in range(ref.shape[0])], axis=1).astype(LOW)


def take(ref, start, count, stride, first=0, tiles=None):
    tiles = ref.shape[0] if tiles is None else tiles
    picked = [ref[first + tile, pl.ds(start, count, stride=stride), :] for tile in range(tiles)]
    return jnp.concatenate(picked, axis=1)


def put(ref, start, count, stride, array):
    for tile in range(ref.shape[0]):
        ref[tile, pl.ds(start, count, stride=stride), :] = array[
            :, tile * LANES : (tile + 1) * LANES
        ]


def start_copies(source, target, sems):
    copies = []
    for index in range(source.shape[0]):
        copy = pltpu.make_async_copy(source.at[index], target.at[index], sems.at[index])
        copy.start()
        copies.append(copy)
    return copies


def start_copy(source, target, sem):
    copy = pltpu.make_async_copy(source, target, sem)
    copy.start()
    return copy


def gather_kernel(
    tokens, params_far, grads, sent_far, dispatch_far, combine_far,
    tokens_v, grads_v, params, sent, dispatch, combine, rows, sems, grad_sems, more_sems,
):
    images = tokens.shape[0]
    slots = params.shape[0]
    stride = KINDS * images
    params_copy = start_copy(params_far, params, more_sems.at[0])
    copies = start_copies(tokens, tokens_v, sems)
    grad_copies = start_copies(grads, grads_v, grad_sems)
    logits = []
    params_copy.wait()
    for image in range(images):
        copies[image].wait()
        logits.append(dot(params[...], tokens_v[image], 1, 1))
    over_slots = []
    for image in range(images):
        over_tokens = softmax(logits[image], 1)
        dispatch[image] = over_tokens
        put(
            rows, KINDS * image, slots, stride, dot(over_tokens.astype(LOW), tokens_v[image], 1, 0)
        )
        over_slots.append(softmax(logits[image], 0))
        combine[image] = over_slots[image]
    results = [
        start_copy(dispatch, dispatch_far, more_sems.at[1]),
        start_copy(combine, combine_far, more_sems.at[2]),
    ]
    for image in range(images):
        grad_copies[image].wait()
        value = dot(over_slots[image].astype(LOW), grads_v[image], 1, 0)
        put(rows, KINDS * image + 1, slots, stride, value)
    sent[...] = packed(rows)
    results.append(start_copy(sent, sent_far, more_sems.at[3]))
    for copy in results:
        copy.wait()


def gather(tokens, params, grads):
    images, length, width = tokens.shape
    slots = params.shape[0]
    weights = shaped((images, slots, length), WIDE)
    rows = (slots * images * KINDS, width)
    return call(
        gather_kernel,
        "gather_slots",
        ALONE,
        6 * images * slots * length * width,
        4 * images * length * width,
        2 * images * slots * length,
        out_shape=(shaped(rows, LOW), weights, weights),
        in_specs=[PLACE] * 3,
        out_specs=(PLACE,) * 3,
        scratch_shapes=[
            pltpu.VMEM(tokens.shape, LOW),
            pltpu.VMEM(grads.shape, LOW),
            pltpu.VMEM(params.shape, LOW),
            pltpu.VMEM(rows, LOW),
            pltpu.VMEM(weights.shape, WIDE),
            pltpu.VMEM(weights.shape, WIDE),
            scratch_rows(rows),
            pltpu.SemaphoreType.DMA((images,)),
            pltpu.SemaphoreType.DMA((images,)),
            pltpu.SemaphoreType.DMA((4,)),
        ],
    )(tokens, params, grads)


def start_weights(w_in, w_out, w_in_v, w_out_v, sems):
    chunks, tile = w_out_v.shape[:2]
    copies = []
    for chunk in range(chunks):
        units = pl.ds(chunk * tile, tile)
        pair = (
            pltpu.make_async_copy(w_in.at[:, units], w_in_v.at[chunk], sems.at[0, chunk]),
            pltpu.make_async_copy(w_out.at[units, :], w_out_v.at[chunk], sems.at[1, chunk]),
        )
        for copy in pair:
            copy.start()
        copies.append(pair)
    return copies


def weight_scratch(width, hidden, tile):
    chunks = hidden // tile
    return [
        pltpu.VMEM((chunks, width, tile), LOW),
        pltpu.VMEM((chunks, tile, width), LOW),
        pltpu.SemaphoreType.DMA((2, chunks)),
    ]


def expert_kernel(
    rows_far, w_in, w_out, back_far, acts_far, hidden_far, mark,
    w_in_v, w_out_v, sems, wide, rows, back, acts, hidden, more_sems,
):
    del mark
    rows_copy = start_copy(rows_far, rows, more_sems.at[0])
    copies = start_weights(w_in, w_out, w_in_v, w_out_v, sems)
    count = rows.shape[0] // KINDS
    chunks, tile = w_out_v.shape[:2]
    rows_copy.wait()
    load_rows(wide, rows[...])
    rows_in = take(wide, 0, count, KINDS).astype(LOW)
    rows_grad = take(wide, 1, count, KINDS).astype(LOW)
    out = d_in = None
    for chunk in range(chunks):
        units = slice(chunk * tile, (chunk + 1) * tile)
        copies[chunk][0].wait()
        preact = dot(rows_in, w_in_v[chunk], 1, 0)
        copies[chunk][1].wait()
        d_acts = dot(rows_grad, w_out_v[chunk], 1, 1)
        values, slope = gelu_parts(preact)
        values = values.astype(LOW)
        d_hidden = (d_acts * slope).astype(LOW)
        acts[:, units] = values
        hidden[:, units] = d_hidden
        out_part = dot(values, w_out_v[chunk], 1, 0)
        d_in_part = dot(d_hidden, w_in_v[chunk], 1, 1)
        out = out_part if chunk == 0 else out + out_part
        d_in = d_in_part if chunk == 0 else d_in + d_in_part
    results = [
        start_copy(acts, acts_far, more_sems.at[1]),
        start_copy(hidden, hidden_far, more_sems.at[2]),
    ]
    put(wide, 0, count, KINDS, out)
    put(wide, 1, count, KINDS, d_in)
    back[...] = packed(wide)
    results.append(start_copy(back, back_far, more_sems.at[3]))
    for copy in results:
        copy.wait()


def expert(rows, w_in, w_out, tile):
    total, width = rows.shape
    hidden = w_in.shape[1]
    count = total // KINDS
    kept = shaped((count, hidden), LOW)
    return call(
        expert_kernel,
        "expert_rows",
        ALONE,
        8 * count * hidden * width,
        4 * hidden * width,
        count * hidden,
        out_shape=(shaped(rows.shape, LOW), kept, kept, MARK),
        in_specs=[PLACE] * 3,
        out_specs=(PLACE,) * 4,
        scratch_shapes=[
            *weight_scratch(width, hidden, tile),
            scratch_rows(rows.shape),
            pltpu.VMEM(rows.shape, LOW),
            pltpu.VMEM(rows.shape, LOW),
            pltpu.VMEM(kept.shape, LOW),
            pltpu.VMEM(kept.shape, LOW),
            pltpu.SemaphoreType.DMA((4,)),
        ],
    )(rows, w_in, w_out)


def others_kernel(after, rows, w_in, w_out, acts, hidden, mark, w_in_v, w_out_v, sems, wide):
    del after, mark
    copies = start_weights(w_in, w_out, w_in_v, w_out_v, sems)
    count = rows.shape[0] // KINDS
    chunks, tile = w_out_v.shape[:2]
    load_rows(wide, rows[...])
    rows_in = take(wide, 0, count, KINDS).astype(LOW)
    rows_grad = take(wide, 1, count, KINDS).astype(LOW)
    for chunk in range(chunks):
        units = slice(chunk * tile, (chunk + 1) * tile)
        copies[chunk][0].wait()
        values, slope = gelu_parts(dot(rows_in, w_in_v[chunk], 1, 0))
        acts[:, units] = values.astype(LOW)
        copies[chunk][1].wait()
        d_acts = dot(rows_grad, w_out_v[chunk], 1, 1)
        hidden[:, units] = (d_acts * slope).astype(LOW)


def others_hidden(after, rows, w_in, w_out, tile):
    total, width = rows.shape
    hidden = w_in.shape[1]
    count = total // KINDS
    kept = shaped((count, hidden), LOW)
    return call(
        others_kernel,
        "others_hidden",
        SHARED,
        64 * count * hidden * width,
        32 * hidden * width,
        count * hidden,
        out_shape=(kept, kept, MARK),
        in_specs=[PLACE, WHOLE, PLACE, PLACE],
        out_specs=(WHOLE, WHOLE, PLACE),
        scratch_shapes=[*weight_scratch(width, hidden, tile), scratch_rows(rows.shape)],
    )(after, rows, w_in, w_out)


def weights_kernel(
    mine, after, rows, other_rows, acts, other_acts, hidden, other_hidden, grad_in, grad_out, mark,
    wide, grads, turned,
):
    del after, mark
    count = rows.shape[0] // KINDS

    @pl.when(pl.program_id(0) == 0)
    def _():
        left, right = [], []
        tiles = turned.shape[0] // LANES
        for source in (rows, other_rows):
            load_rows(wide, source[...])
            left.append(take(wide, 0, count, KINDS, mine[0] * tiles, tiles))
            right.append(take(wide, 1, count, KINDS))
        turned[...] = jnp.concatenate(left, axis=0).T.astype(LOW)
        grads[...] = jnp.concatenate(right, axis=0).astype(LOW)

    all_hidden = jnp.concatenate([hidden[...], other_hidden[...]], axis=0)
    grad_in[...] = dot(turned[...], all_hidden, 1, 0).astype(LOW)
    all_acts = jnp.concatenate([acts[...], other_acts[...]], axis=0)
    grad_out[...] = dot(all_acts, grads[...], 0, 0).astype(LOW)


def weight_grads(mine, after, rows, acts, hidden, steps, replicas):
    total, width = rows[0].shape
    size = acts[0].shape[1]
    count = total // KINDS
    in_tile, out_tile = size // steps, size // replicas // steps
    whole_rows = pl.BlockSpec((total, width), lambda i, mine: (0, 0))
    acts_spec = pl.BlockSpec((count, out_tile), lambda i, mine: (0, mine[0] * steps + i))
    hidden_spec = pl.BlockSpec((count, in_tile), lambda i, mine: (0, i))
    return call(
        weights_kernel,
        "weight_grads",
        SHARED,
        8 * count * size * width // replicas,
        4 * size * width // replicas,
        grid_spec=pltpu.PrefetchScalarGridSpec(
            num_scalar_prefetch=1,
            grid=(steps,),
            in_specs=[PLACE] + [whole_rows] * 2 + [acts_spec] * 2 + [hidden_spec] * 2,
            out_specs=(
                pl.BlockSpec((width // replicas, in_tile), lambda i, mine: (0, i)),
                pl.BlockSpec((out_tile, width), lambda i, mine: (i, 0)),
                PLACE,
            ),
            scratch_shapes=[
                scratch_rows((total, width)),
                pltpu.VMEM((2 * count, width), LOW),
                pltpu.VMEM((width // replicas, 2 * count), LOW),
            ],
        ),
        out_shape=(
            shaped((width // replicas, size), LOW),
            shaped((size // replicas, width), LOW),
            MARK,
        ),
    )(mine, after, *rows, *acts, *hidden)


def logits_kernel(
    after, back, tokens, params, grads, dispatch, combine, left, right, local, mark,
    tokens_v, grads_v, wide, sems, grad_sems,
):
    del after, mark
    images, slots, _ = dispatch.shape
    grad_copies = start_copies(grads, grads_v, grad_sems)
    copies = start_copies(tokens, tokens_v, sems)
    load_rows(wide, back[...])
    stride = KINDS * images
    parts = []
    for image in range(images):
        slot_out = take(wide, KINDS * image, slots, stride).astype(LOW)
        weights = combine[image]
        grad_copies[image].wait()
        d_combine = dot(slot_out, grads_v[image], 1, 1)
        parts.append(
            weights * (d_combine - jnp.sum(weights * d_combine, axis=0, keepdims=True))
        )
    total = jnp.zeros(params.shape, WIDE)
    for image in range(images):
        d_slot_in = take(wide, KINDS * image + 1, slots, stride).astype(LOW)
        right[image, :slots, :] = d_slot_in
        right[image, slots:, :] = params[...]
        weights = dispatch[image]
        copies[image].wait()
        d_dispatch = dot(d_slot_in, tokens_v[image], 1, 1)
        d_logits = parts[image] + weights * (
            d_dispatch - jnp.sum(weights * d_dispatch, axis=1, keepdims=True)
        )
        low = d_logits.astype(LOW)
        left[image, :slots, :] = weights.astype(LOW)
        left[image, slots:, :] = low
        total += dot(low, tokens_v[image], 1, 0)
    pieces, _, size = local.shape
    for slot in range(slots):
        for piece in range(pieces // slots):
            local[slot * (pieces // slots) + piece] = total[
                slot : slot + 1, piece * size : (piece + 1) * size
            ]


def logits_grads(after, back, tokens, params, grads, dispatch, combine, pieces):
    images, length, width = tokens.shape
    slots = params.shape[0]
    return call(
        logits_kernel,
        "logits_grads",
        SHARED,
        6 * images * slots * length * width,
        4 * images * length * width,
        out_shape=(
            shaped((images, 2 * slots, length), LOW),
            shaped((images, 2 * slots, width), LOW),
            shaped((pieces, 1, slots * width // pieces), WIDE),
            MARK,
        ),
        in_specs=[PLACE, WHOLE, PLACE, WHOLE, PLACE, WHOLE, WHOLE],
        out_specs=(WHOLE, WHOLE, WHOLE, PLACE),
        scratch_shapes=[
            pltpu.VMEM(tokens.shape, LOW),
            pltpu.VMEM(grads.shape, LOW),
            scratch_rows(back.shape),
            pltpu.SemaphoreType.DMA((images,)),
            pltpu.SemaphoreType.DMA((images,)),
        ],
    )(after, back, tokens, params, grads, dispatch, combine)


def tokens_kernel(after, left, right, out):
    del after
    out[0] = dot(left[0], right[0], 0, 0).astype(LOW)


def tokens_grads(after, left, right):
    images, deep, length = left.shape
    width = right.shape[2]
    return call(
        tokens_kernel,
        "tokens_grads",
        SHARED,
        2 * images * deep * length * width,
        2 * images * length * width,
        grid=(images,),
        out_shape=shaped((images, length, width), LOW),
        in_specs=[
            PLACE,
            pl.BlockSpec((1, deep, length), lambda i: (i, 0, 0)),
            pl.BlockSpec((1, deep, width), lambda i: (i, 0, 0)),
        ],
        out_specs=pl.BlockSpec((1, length, width), lambda i: (i, 0, 0)),
    )(after, left, right)


def share_kernel(after, pieces, out, mark):
    del after, mark
    out[...] = jnp.broadcast_to(jnp.sum(pieces[...], axis=0, keepdims=True), out.shape)


def share_of_sum(after, pieces):
    return call(
        share_kernel,
        "share_of_sum",
        SHARED,
        pieces.size,
        8 * pieces.size,
        out_shape=(shaped(pieces.shape, WIDE), MARK),
        in_specs=[PLACE, WHOLE],
        out_specs=(WHOLE, PLACE),
    )(after, pieces)


def exchange(rows, axes):
    return lax.all_to_all(rows, axes, split_axis=0, concat_axis=0, tiled=True)


def body(tokens, slot_params, expert_in, expert_out, grad_out):
    params = slot_params.T
    weights = (expert_in[0], expert_out[0])
    replicas = lax.axis_size("rep")
    everyone = ("rep", "exp")
    mine = lax.axis_index("rep").astype(jnp.int32).reshape(1)

    sent, dispatch, combine = gather(tokens, params, grad_out)
    rows = exchange(sent, "exp")
    other_rows = lax.ppermute(rows, "rep", [(i, (i + 1) % replicas) for i in range(replicas)])
    back, acts, hidden, after_expert = expert(rows, *weights, 512)
    other_acts, other_hidden, after_others = others_hidden(
        after_expert, other_rows, *weights, 512
    )
    back = exchange(back, "exp")
    left, right, local, after_logits = logits_grads(
        after_others, back, tokens, params, grad_out, dispatch, combine, lax.axis_size(everyone)
    )
    grad_expert_in, grad_expert_out, after_weights = weight_grads(
        mine,
        after_logits,
        (rows, other_rows),
        (acts, other_acts),
        (hidden, other_hidden),
        5,
        replicas,
    )
    share, after_share = share_of_sum(after_weights, exchange(local, everyone))
    grad_params = exchange(share, everyone)
    grad_tokens = tokens_grads(after_share, left, right)
    return (
        grad_tokens,
        grad_params.reshape(params.shape).T,
        grad_expert_in[None],
        grad_expert_out[None],
    )


def solution(mesh):
    in_specs = (
        P(("rep", "exp"), None, None),
        P(),
        P("exp", None, None),
        P("exp", None, None),
        P(("rep", "exp"), None, None),
    )
    out_specs = (P(("rep", "exp"), None, None), P(), P("exp", "rep", None), P("exp", "rep", None))
    return jax.shard_map(body, mesh=mesh, in_specs=in_specs, out_specs=out_specs, check_vma=False)
```

```python
import math

import jax
import jax.numpy as jnp
from jax import lax
from jax.experimental import pallas as pl
from jax.experimental.pallas import tpu as pltpu
from jax.sharding import PartitionSpec as P

GELU_C = math.sqrt(2.0 / math.pi)
CUBIC = 0.044715
LOW = jnp.bfloat16
WIDE = jnp.float32
LANES = 128
KINDS = 2
SHARED = 52 * 1024 * 1024
WHOLE = pl.BlockSpec(memory_space=pltpu.VMEM)
PLACE = pl.BlockSpec(memory_space=pl.ANY)


def call(kernel, name, grant, flops, nbytes, exps=0, **kwargs):
    return pl.pallas_call(
        kernel,
        name=name,
        compiler_params=pltpu.CompilerParams(vmem_limit_bytes=grant),
        cost_estimate=pl.CostEstimate(
            flops=flops, bytes_accessed=nbytes, transcendentals=exps
        ),
        **kwargs,
    )


def shaped(shape, dtype):
    return jax.ShapeDtypeStruct(shape, dtype)


MARK = shaped((8, LANES), WIDE)


def gelu_parts(values):
    square = values * values
    tangent = jnp.tanh(GELU_C * (values + CUBIC * square * values))
    half = 0.5 * (1.0 + tangent)
    slope = half + 0.5 * values * (1.0 - tangent * tangent) * GELU_C * (1.0 + 3.0 * CUBIC * square)
    return values * half, slope


def dot(left, right, over_left, over_right):
    return lax.dot_general(
        left, right, (((over_left,), (over_right,)), ((), ())), preferred_element_type=WIDE
    )


def softmax(values, axis):
    raised = jnp.exp(values - jnp.max(values, axis=axis, keepdims=True))
    return raised / jnp.sum(raised, axis=axis, keepdims=True)


def scratch_rows(shape):
    return pltpu.VMEM((shape[1] // LANES, shape[0], LANES), WIDE)


def load_rows(ref, array):
    for tile in range(ref.shape[0]):
        ref[tile] = array[:, tile * LANES : (tile + 1) * LANES].astype(WIDE)


def packed(ref):
    return jnp.concatenate([ref[tile] for tile in range(ref.shape[0])], axis=1).astype(LOW)


def take(ref, start, count, stride, first=0, tiles=None):
    tiles = ref.shape[0] if tiles is None else tiles
    picked = [ref[first + tile, pl.ds(start, count, stride=stride), :] for tile in range(tiles)]
    return jnp.concatenate(picked, axis=1)


def put(ref, start, count, stride, array):
    for tile in range(ref.shape[0]):
        ref[tile, pl.ds(start, count, stride=stride), :] = array[
            :, tile * LANES : (tile + 1) * LANES
        ]


def start_copies(source, target, sems):
    copies = []
    for index in range(source.shape[0]):
        copy = pltpu.make_async_copy(source.at[index], target.at[index], sems.at[index])
        copy.start()
        copies.append(copy)
    return copies


def gather_kernel(
    tokens, params, grads, sent, dispatch, combine, tokens_v, grads_v, rows, sems, grad_sems
):
    images = tokens.shape[0]
    slots = params.shape[0]
    stride = KINDS * images
    copies = start_copies(tokens, tokens_v, sems)
    grad_copies = start_copies(grads, grads_v, grad_sems)
    logits = []
    for image in range(images):
        copies[image].wait()
        logits.append(dot(params[...], tokens_v[image], 1, 1))
    over_slots = []
    for image in range(images):
        over_tokens = softmax(logits[image], 1)
        dispatch[image] = over_tokens
        put(
            rows, KINDS * image, slots, stride, dot(over_tokens.astype(LOW), tokens_v[image], 1, 0)
        )
        over_slots.append(softmax(logits[image], 0))
        combine[image] = over_slots[image]
    for image in range(images):
        grad_copies[image].wait()
        value = dot(over_slots[image].astype(LOW), grads_v[image], 1, 0)
        put(rows, KINDS * image + 1, slots, stride, value)
    sent[...] = packed(rows)


def gather(tokens, params, grads):
    images, length, width = tokens.shape
    slots = params.shape[0]
    weights = shaped((images, slots, length), WIDE)
    rows = (slots * images * KINDS, width)
    return call(
        gather_kernel,
        "gather_slots",
        SHARED,
        6 * images * slots * length * width,
        4 * images * length * width,
        2 * images * slots * length,
        out_shape=(shaped(rows, LOW), weights, weights),
        in_specs=[PLACE, WHOLE, PLACE],
        out_specs=(WHOLE, WHOLE, WHOLE),
        scratch_shapes=[
            pltpu.VMEM(tokens.shape, LOW),
            pltpu.VMEM(grads.shape, LOW),
            scratch_rows(rows),
            pltpu.SemaphoreType.DMA((images,)),
            pltpu.SemaphoreType.DMA((images,)),
        ],
    )(tokens, params, grads)


def start_weights(w_in, w_out, w_in_v, w_out_v, sems):
    chunks, tile = w_out_v.shape[:2]
    copies = []
    for chunk in range(chunks):
        units = pl.ds(chunk * tile, tile)
        pair = (
            pltpu.make_async_copy(w_in.at[:, units], w_in_v.at[chunk], sems.at[0, chunk]),
            pltpu.make_async_copy(w_out.at[units, :], w_out_v.at[chunk], sems.at[1, chunk]),
        )
        for copy in pair:
            copy.start()
        copies.append(pair)
    return copies


def weight_scratch(width, hidden, tile):
    chunks = hidden // tile
    return [
        pltpu.VMEM((chunks, width, tile), LOW),
        pltpu.VMEM((chunks, tile, width), LOW),
        pltpu.SemaphoreType.DMA((2, chunks)),
    ]


def expert_kernel(rows, w_in, w_out, back, acts, hidden, mark, w_in_v, w_out_v, sems, wide):
    del mark
    copies = start_weights(w_in, w_out, w_in_v, w_out_v, sems)
    count = rows.shape[0] // KINDS
    chunks, tile = w_out_v.shape[:2]
    load_rows(wide, rows[...])
    rows_in = take(wide, 0, count, KINDS).astype(LOW)
    rows_grad = take(wide, 1, count, KINDS).astype(LOW)
    out = d_in = None
    for chunk in range(chunks):
        units = slice(chunk * tile, (chunk + 1) * tile)
        copies[chunk][0].wait()
        preact = dot(rows_in, w_in_v[chunk], 1, 0)
        copies[chunk][1].wait()
        d_acts = dot(rows_grad, w_out_v[chunk], 1, 1)
        values, slope = gelu_parts(preact)
        values = values.astype(LOW)
        d_hidden = (d_acts * slope).astype(LOW)
        acts[:, units] = values
        hidden[:, units] = d_hidden
        out_part = dot(values, w_out_v[chunk], 1, 0)
        d_in_part = dot(d_hidden, w_in_v[chunk], 1, 1)
        out = out_part if chunk == 0 else out + out_part
        d_in = d_in_part if chunk == 0 else d_in + d_in_part
    put(wide, 0, count, KINDS, out)
    put(wide, 1, count, KINDS, d_in)
    back[...] = packed(wide)


def expert(rows, w_in, w_out, tile):
    total, width = rows.shape
    hidden = w_in.shape[1]
    count = total // KINDS
    kept = shaped((count, hidden), LOW)
    return call(
        expert_kernel,
        "expert_rows",
        SHARED,
        8 * count * hidden * width,
        4 * hidden * width,
        count * hidden,
        out_shape=(shaped(rows.shape, LOW), kept, kept, MARK),
        in_specs=[WHOLE, PLACE, PLACE],
        out_specs=(WHOLE, WHOLE, WHOLE, PLACE),
        scratch_shapes=[*weight_scratch(width, hidden, tile), scratch_rows(rows.shape)],
    )(rows, w_in, w_out)


def others_kernel(after, rows, w_in, w_out, acts, hidden, mark, w_in_v, w_out_v, sems, wide):
    del after, mark
    copies = start_weights(w_in, w_out, w_in_v, w_out_v, sems)
    count = rows.shape[0] // KINDS
    chunks, tile = w_out_v.shape[:2]
    load_rows(wide, rows[...])
    rows_in = take(wide, 0, count, KINDS).astype(LOW)
    rows_grad = take(wide, 1, count, KINDS).astype(LOW)
    for chunk in range(chunks):
        units = slice(chunk * tile, (chunk + 1) * tile)
        copies[chunk][0].wait()
        values, slope = gelu_parts(dot(rows_in, w_in_v[chunk], 1, 0))
        acts[:, units] = values.astype(LOW)
        copies[chunk][1].wait()
        d_acts = dot(rows_grad, w_out_v[chunk], 1, 1)
        hidden[:, units] = (d_acts * slope).astype(LOW)


def others_hidden(after, rows, w_in, w_out, tile):
    total, width = rows.shape
    hidden = w_in.shape[1]
    count = total // KINDS
    kept = shaped((count, hidden), LOW)
    return call(
        others_kernel,
        "others_hidden",
        SHARED,
        64 * count * hidden * width,
        32 * hidden * width,
        count * hidden,
        out_shape=(kept, kept, MARK),
        in_specs=[PLACE, WHOLE, PLACE, PLACE],
        out_specs=(WHOLE, WHOLE, PLACE),
        scratch_shapes=[*weight_scratch(width, hidden, tile), scratch_rows(rows.shape)],
    )(after, rows, w_in, w_out)


def weights_kernel(
    mine, after, rows, other_rows, acts, other_acts, hidden, other_hidden, grad_in, grad_out, mark,
    wide, grads, turned,
):
    del after, mark
    count = rows.shape[0] // KINDS

    @pl.when(pl.program_id(0) == 0)
    def _():
        left, right = [], []
        tiles = turned.shape[0] // LANES
        for source in (rows, other_rows):
            load_rows(wide, source[...])
            left.append(take(wide, 0, count, KINDS, mine[0] * tiles, tiles))
            right.append(take(wide, 1, count, KINDS))
        turned[...] = jnp.concatenate(left, axis=0).T.astype(LOW)
        grads[...] = jnp.concatenate(right, axis=0).astype(LOW)

    all_hidden = jnp.concatenate([hidden[...], other_hidden[...]], axis=0)
    grad_in[...] = dot(turned[...], all_hidden, 1, 0).astype(LOW)
    all_acts = jnp.concatenate([acts[...], other_acts[...]], axis=0)
    grad_out[...] = dot(all_acts, grads[...], 0, 0).astype(LOW)


def weight_grads(mine, after, rows, acts, hidden, steps, replicas):
    total, width = rows[0].shape
    size = acts[0].shape[1]
    count = total // KINDS
    in_tile, out_tile = size // steps, size // replicas // steps
    whole_rows = pl.BlockSpec((total, width), lambda i, mine: (0, 0))
    acts_spec = pl.BlockSpec((count, out_tile), lambda i, mine: (0, mine[0] * steps + i))
    hidden_spec = pl.BlockSpec((count, in_tile), lambda i, mine: (0, i))
    return call(
        weights_kernel,
        "weight_grads",
        SHARED,
        8 * count * size * width // replicas,
        4 * size * width // replicas,
        grid_spec=pltpu.PrefetchScalarGridSpec(
            num_scalar_prefetch=1,
            grid=(steps,),
            in_specs=[PLACE] + [whole_rows] * 2 + [acts_spec] * 2 + [hidden_spec] * 2,
            out_specs=(
                pl.BlockSpec((width // replicas, in_tile), lambda i, mine: (0, i)),
                pl.BlockSpec((out_tile, width), lambda i, mine: (i, 0)),
                PLACE,
            ),
            scratch_shapes=[
                scratch_rows((total, width)),
                pltpu.VMEM((2 * count, width), LOW),
                pltpu.VMEM((width // replicas, 2 * count), LOW),
            ],
        ),
        out_shape=(
            shaped((width // replicas, size), LOW),
            shaped((size // replicas, width), LOW),
            MARK,
        ),
    )(mine, after, *rows, *acts, *hidden)


def logits_kernel(
    after, back, tokens, params, grads, dispatch, combine, left, right, local, mark,
    tokens_v, grads_v, wide, sems, grad_sems,
):
    del after, mark
    images, slots, _ = dispatch.shape
    grad_copies = start_copies(grads, grads_v, grad_sems)
    copies = start_copies(tokens, tokens_v, sems)
    load_rows(wide, back[...])
    stride = KINDS * images
    parts = []
    for image in range(images):
        slot_out = take(wide, KINDS * image, slots, stride).astype(LOW)
        weights = combine[image]
        grad_copies[image].wait()
        d_combine = dot(slot_out, grads_v[image], 1, 1)
        parts.append(
            weights * (d_combine - jnp.sum(weights * d_combine, axis=0, keepdims=True))
        )
    total = jnp.zeros(params.shape, WIDE)
    for image in range(images):
        d_slot_in = take(wide, KINDS * image + 1, slots, stride).astype(LOW)
        right[image, :slots, :] = d_slot_in
        right[image, slots:, :] = params[...]
        weights = dispatch[image]
        copies[image].wait()
        d_dispatch = dot(d_slot_in, tokens_v[image], 1, 1)
        d_logits = parts[image] + weights * (
            d_dispatch - jnp.sum(weights * d_dispatch, axis=1, keepdims=True)
        )
        low = d_logits.astype(LOW)
        left[image, :slots, :] = weights.astype(LOW)
        left[image, slots:, :] = low
        total += dot(low, tokens_v[image], 1, 0)
    pieces, _, size = local.shape
    for slot in range(slots):
        for piece in range(pieces // slots):
            local[slot * (pieces // slots) + piece] = total[
                slot : slot + 1, piece * size : (piece + 1) * size
            ]


def logits_grads(after, back, tokens, params, grads, dispatch, combine, pieces):
    images, length, width = tokens.shape
    slots = params.shape[0]
    return call(
        logits_kernel,
        "logits_grads",
        SHARED,
        6 * images * slots * length * width,
        4 * images * length * width,
        out_shape=(
            shaped((images, 2 * slots, length), LOW),
            shaped((images, 2 * slots, width), LOW),
            shaped((pieces, 1, slots * width // pieces), WIDE),
            MARK,
        ),
        in_specs=[PLACE, WHOLE, PLACE, WHOLE, PLACE, WHOLE, WHOLE],
        out_specs=(WHOLE, WHOLE, WHOLE, PLACE),
        scratch_shapes=[
            pltpu.VMEM(tokens.shape, LOW),
            pltpu.VMEM(grads.shape, LOW),
            scratch_rows(back.shape),
            pltpu.SemaphoreType.DMA((images,)),
            pltpu.SemaphoreType.DMA((images,)),
        ],
    )(after, back, tokens, params, grads, dispatch, combine)


def tokens_kernel(after, left, right, out):
    del after
    out[0] = dot(left[0], right[0], 0, 0).astype(LOW)


def tokens_grads(after, left, right):
    images, deep, length = left.shape
    width = right.shape[2]
    return call(
        tokens_kernel,
        "tokens_grads",
        SHARED,
        2 * images * deep * length * width,
        2 * images * length * width,
        grid=(images,),
        out_shape=shaped((images, length, width), LOW),
        in_specs=[
            PLACE,
            pl.BlockSpec((1, deep, length), lambda i: (i, 0, 0)),
            pl.BlockSpec((1, deep, width), lambda i: (i, 0, 0)),
        ],
        out_specs=pl.BlockSpec((1, length, width), lambda i: (i, 0, 0)),
    )(after, left, right)


def share_kernel(after, pieces, out, mark):
    del after, mark
    out[...] = jnp.broadcast_to(jnp.sum(pieces[...], axis=0, keepdims=True), out.shape)


def share_of_sum(after, pieces):
    return call(
        share_kernel,
        "share_of_sum",
        SHARED,
        pieces.size,
        8 * pieces.size,
        out_shape=(shaped(pieces.shape, WIDE), MARK),
        in_specs=[PLACE, WHOLE],
        out_specs=(WHOLE, PLACE),
    )(after, pieces)


def exchange(rows, axes):
    return lax.all_to_all(rows, axes, split_axis=0, concat_axis=0, tiled=True)


def body(tokens, slot_params, expert_in, expert_out, grad_out):
    params = slot_params.T
    weights = (expert_in[0], expert_out[0])
    replicas = lax.axis_size("rep")
    everyone = ("rep", "exp")
    mine = lax.axis_index("rep").astype(jnp.int32).reshape(1)

    sent, dispatch, combine = gather(tokens, params, grad_out)
    rows = exchange(sent, "exp")
    other_rows = lax.ppermute(rows, "rep", [(i, (i + 1) % replicas) for i in range(replicas)])
    back, acts, hidden, after_expert = expert(rows, *weights, 512)
    other_acts, other_hidden, after_others = others_hidden(
        after_expert, other_rows, *weights, 512
    )
    back = exchange(back, "exp")
    left, right, local, after_logits = logits_grads(
        after_others, back, tokens, params, grad_out, dispatch, combine, lax.axis_size(everyone)
    )
    grad_expert_in, grad_expert_out, after_weights = weight_grads(
        mine,
        after_logits,
        (rows, other_rows),
        (acts, other_acts),
        (hidden, other_hidden),
        5,
        replicas,
    )
    share, after_share = share_of_sum(after_weights, exchange(local, everyone))
    grad_params = exchange(share, everyone)
    grad_tokens = tokens_grads(after_share, left, right)
    return (
        grad_tokens,
        grad_params.reshape(params.shape).T,
        grad_expert_in[None],
        grad_expert_out[None],
    )


def solution(mesh):
    in_specs = (
        P(("rep", "exp"), None, None),
        P(),
        P("exp", None, None),
        P("exp", None, None),
        P(("rep", "exp"), None, None),
    )
    out_specs = (P(("rep", "exp"), None, None), P(), P("exp", "rep", None), P("exp", "rep", None))
    return jax.shard_map(body, mesh=mesh, in_specs=in_specs, out_specs=out_specs, check_vma=False)
```

```python
import math

import jax
import jax.numpy as jnp
from jax import lax
from jax.experimental import pallas as pl
from jax.experimental.pallas import tpu as pltpu
from jax.sharding import PartitionSpec as P

GELU_C = math.sqrt(2.0 / math.pi)
CUBIC = 0.044715
LOW = jnp.bfloat16
WIDE = jnp.float32
LANES = 128
TILE = 8
KINDS = 2
SHARED = 52 * 1024 * 1024
WHOLE = pl.BlockSpec(memory_space=pltpu.VMEM)
PLACE = pl.BlockSpec(memory_space=pl.ANY)


def call(kernel, name, grant, flops, nbytes, exps=0, **kwargs):
    return pl.pallas_call(
        kernel,
        name=name,
        compiler_params=pltpu.CompilerParams(vmem_limit_bytes=grant),
        cost_estimate=pl.CostEstimate(
            flops=flops, bytes_accessed=nbytes, transcendentals=exps
        ),
        **kwargs,
    )


def shaped(shape, dtype):
    return jax.ShapeDtypeStruct(shape, dtype)


MARK = shaped((8, LANES), WIDE)


def gelu_parts(values):
    square = values * values
    tangent = jnp.tanh(GELU_C * (values + CUBIC * square * values))
    half = 0.5 * (1.0 + tangent)
    slope = half + 0.5 * values * (1.0 - tangent * tangent) * GELU_C * (1.0 + 3.0 * CUBIC * square)
    return values * half, slope


def dot(left, right, over_left, over_right):
    return lax.dot_general(
        left, right, (((over_left,), (over_right,)), ((), ())), preferred_element_type=WIDE
    )


def softmax(values, axis):
    raised = jnp.exp(values - jnp.max(values, axis=axis, keepdims=True))
    return raised / jnp.sum(raised, axis=axis, keepdims=True)


def scratch_rows(shape):
    return pltpu.VMEM((shape[1] // LANES, shape[0], LANES), WIDE)


def load_rows(ref, array):
    for tile in range(ref.shape[0]):
        ref[tile] = array[:, tile * LANES : (tile + 1) * LANES].astype(WIDE)


def packed(ref):
    return jnp.concatenate([ref[tile] for tile in range(ref.shape[0])], axis=1).astype(LOW)


def take(ref, start, count, stride, first=0, tiles=None):
    tiles = ref.shape[0] if tiles is None else tiles
    picked = [ref[first + tile, pl.ds(start, count, stride=stride), :] for tile in range(tiles)]
    return jnp.concatenate(picked, axis=1)


def put(ref, start, count, stride, array):
    for tile in range(ref.shape[0]):
        ref[tile, pl.ds(start, count, stride=stride), :] = array[
            :, tile * LANES : (tile + 1) * LANES
        ]


def start_copy(source, target, sem):
    copy = pltpu.make_async_copy(source, target, sem)
    copy.start()
    return copy


def gather_kernel(
    tokens, params, grads, sent, dispatch, combine, tokens_v, grads_v, rows, sems
):
    images = tokens.shape[0]
    slots = params.shape[0]
    stride = KINDS * images
    tokens_copy = start_copy(tokens, tokens_v, sems.at[0])
    grads_copy = start_copy(grads, grads_v, sems.at[1])
    tokens_copy.wait()
    logits = [dot(params[...], tokens_v[image], 1, 1) for image in range(images)]
    over_slots = []
    for image in range(images):
        over_tokens = softmax(logits[image], 1)
        dispatch[image] = over_tokens
        put(
            rows, KINDS * image, slots, stride, dot(over_tokens.astype(LOW), tokens_v[image], 1, 0)
        )
        over_slots.append(softmax(logits[image], 0))
        combine[image] = over_slots[image]
    grads_copy.wait()
    for image in range(images):
        value = dot(over_slots[image].astype(LOW), grads_v[image], 1, 0)
        put(rows, KINDS * image + 1, slots, stride, value)
    sent[...] = packed(rows)


def gather(tokens, params, grads):
    images, length, width = tokens.shape
    slots = params.shape[0]
    weights = shaped((images, slots, length), WIDE)
    rows = (slots * images * KINDS, width)
    return call(
        gather_kernel,
        "gather_slots",
        SHARED,
        6 * images * slots * length * width,
        4 * images * length * width,
        2 * images * slots * length,
        out_shape=(shaped(rows, LOW), weights, weights),
        in_specs=[PLACE, WHOLE, PLACE],
        out_specs=(WHOLE, WHOLE, WHOLE),
        scratch_shapes=[
            pltpu.VMEM(tokens.shape, LOW),
            pltpu.VMEM(grads.shape, LOW),
            scratch_rows(rows),
            pltpu.SemaphoreType.DMA((2,)),
        ],
    )(tokens, params, grads)


def start_weights(w_in, w_out, w_in_v, w_out_v, sems):
    chunks, tile = w_out_v.shape[:2]
    copies = []
    for chunk in range(chunks):
        units = pl.ds(chunk * tile, tile)
        pair = (
            pltpu.make_async_copy(w_in.at[:, units], w_in_v.at[chunk], sems.at[0, chunk]),
            pltpu.make_async_copy(w_out.at[units, :], w_out_v.at[chunk], sems.at[1, chunk]),
        )
        for copy in pair:
            copy.start()
        copies.append(pair)
    return copies


def weight_scratch(width, hidden, tile):
    chunks = hidden // tile
    return [
        pltpu.VMEM((chunks, width, tile), LOW),
        pltpu.VMEM((chunks, tile, width), LOW),
        pltpu.SemaphoreType.DMA((2, chunks)),
    ]


def expert_kernel(rows, w_in, w_out, back, acts, hidden, mark, w_in_v, w_out_v, sems, wide):
    del mark
    copies = start_weights(w_in, w_out, w_in_v, w_out_v, sems)
    count = rows.shape[0] // KINDS
    chunks, tile = w_out_v.shape[:2]
    load_rows(wide, rows[...])
    rows_in = take(wide, 0, count, KINDS).astype(LOW)
    rows_grad = take(wide, 1, count, KINDS).astype(LOW)
    out = d_in = None
    held = None
    for chunk in range(chunks + 1):
        if chunk < chunks:
            for copy in copies[chunk]:
                copy.wait()
            preact = dot(rows_in, w_in_v[chunk], 1, 0)
            d_acts = dot(rows_grad, w_out_v[chunk], 1, 1)
        if chunk > 0:
            out_part = dot(held[0], w_out_v[chunk - 1], 1, 0)
            d_in_part = dot(held[1], w_in_v[chunk - 1], 1, 1)
            out = out_part if chunk == 1 else out + out_part
            d_in = d_in_part if chunk == 1 else d_in + d_in_part
        if chunk < chunks:
            units = slice(chunk * tile, (chunk + 1) * tile)
            values, slope = gelu_parts(preact)
            held = (values.astype(LOW), (d_acts * slope).astype(LOW))
            acts[:, units], hidden[:, units] = held
    put(wide, 0, count, KINDS, out)
    put(wide, 1, count, KINDS, d_in)
    back[...] = packed(wide)


def expert(rows, w_in, w_out, tile):
    total, width = rows.shape
    hidden = w_in.shape[1]
    count = total // KINDS
    kept = shaped((count, hidden), LOW)
    return call(
        expert_kernel,
        "expert_rows",
        SHARED,
        8 * count * hidden * width,
        4 * hidden * width,
        count * hidden,
        out_shape=(shaped(rows.shape, LOW), kept, kept, MARK),
        in_specs=[WHOLE, PLACE, PLACE],
        out_specs=(WHOLE, WHOLE, WHOLE, PLACE),
        scratch_shapes=[*weight_scratch(width, hidden, tile), scratch_rows(rows.shape)],
    )(rows, w_in, w_out)


def others_kernel(after, rows, w_in, w_out, acts, hidden, mark, w_in_v, w_out_v, sems, wide):
    del after, mark
    copies = start_weights(w_in, w_out, w_in_v, w_out_v, sems)
    count = rows.shape[0] // KINDS
    chunks, tile = w_out_v.shape[:2]
    load_rows(wide, rows[...])
    rows_in = take(wide, 0, count, KINDS).astype(LOW)
    rows_grad = take(wide, 1, count, KINDS).astype(LOW)
    for chunk in range(chunks):
        units = slice(chunk * tile, (chunk + 1) * tile)
        copies[chunk][0].wait()
        values, slope = gelu_parts(dot(rows_in, w_in_v[chunk], 1, 0))
        acts[:, units] = values.astype(LOW)
        copies[chunk][1].wait()
        d_acts = dot(rows_grad, w_out_v[chunk], 1, 1)
        hidden[:, units] = (d_acts * slope).astype(LOW)


def others_hidden(after, rows, w_in, w_out, tile):
    total, width = rows.shape
    hidden = w_in.shape[1]
    count = total // KINDS
    kept = shaped((count, hidden), LOW)
    return call(
        others_kernel,
        "others_hidden",
        SHARED,
        64 * count * hidden * width,
        32 * hidden * width,
        count * hidden,
        out_shape=(kept, kept, MARK),
        in_specs=[PLACE, WHOLE, PLACE, PLACE],
        out_specs=(WHOLE, WHOLE, PLACE),
        scratch_shapes=[*weight_scratch(width, hidden, tile), scratch_rows(rows.shape)],
    )(after, rows, w_in, w_out)


def weights_kernel(
    mine, after, rows, other_rows, acts, other_acts, hidden, other_hidden, grad_in, grad_out, mark,
    wide, grads, turned,
):
    del after, mark
    count = rows.shape[0] // KINDS

    @pl.when(pl.program_id(0) == 0)
    def _():
        left, right = [], []
        tiles = turned.shape[0] // LANES
        for source in (rows, other_rows):
            load_rows(wide, source[...])
            left.append(take(wide, 0, count, KINDS, mine[0] * tiles, tiles))
            right.append(take(wide, 1, count, KINDS))
        turned[...] = jnp.concatenate(left, axis=0).T.astype(LOW)
        grads[...] = jnp.concatenate(right, axis=0).astype(LOW)

    all_hidden = jnp.concatenate([hidden[...], other_hidden[...]], axis=0)
    grad_in[...] = dot(turned[...], all_hidden, 1, 0).astype(LOW)
    all_acts = jnp.concatenate([acts[...], other_acts[...]], axis=0)
    grad_out[...] = dot(all_acts, grads[...], 0, 0).astype(LOW)


def weight_grads(mine, after, rows, acts, hidden, steps, replicas):
    total, width = rows[0].shape
    size = acts[0].shape[1]
    count = total // KINDS
    in_tile, out_tile = size // steps, size // replicas // steps
    whole_rows = pl.BlockSpec((total, width), lambda i, mine: (0, 0))
    acts_spec = pl.BlockSpec((count, out_tile), lambda i, mine: (0, mine[0] * steps + i))
    hidden_spec = pl.BlockSpec((count, in_tile), lambda i, mine: (0, i))
    return call(
        weights_kernel,
        "weight_grads",
        SHARED,
        8 * count * size * width // replicas,
        4 * size * width // replicas,
        grid_spec=pltpu.PrefetchScalarGridSpec(
            num_scalar_prefetch=1,
            grid=(steps,),
            in_specs=[PLACE] + [whole_rows] * 2 + [acts_spec] * 2 + [hidden_spec] * 2,
            out_specs=(
                pl.BlockSpec((width // replicas, in_tile), lambda i, mine: (0, i)),
                pl.BlockSpec((out_tile, width), lambda i, mine: (i, 0)),
                PLACE,
            ),
            scratch_shapes=[
                scratch_rows((total, width)),
                pltpu.VMEM((2 * count, width), LOW),
                pltpu.VMEM((width // replicas, 2 * count), LOW),
            ],
        ),
        out_shape=(
            shaped((width // replicas, size), LOW),
            shaped((size // replicas, width), LOW),
            MARK,
        ),
    )(mine, after, *rows, *acts, *hidden)


def logits_kernel(
    after, back, tokens, params, grads, dispatch, combine, left, right, local, mark,
    tokens_v, grads_v, wide, sems,
):
    del after, mark
    images, slots, _ = dispatch.shape
    grads_copy = start_copy(grads, grads_v, sems.at[0])
    tokens_copy = start_copy(tokens, tokens_v, sems.at[1])
    load_rows(wide, back[...])
    stride = KINDS * images
    d_slot_in = []
    for image in range(images):
        d_slot_in.append(take(wide, KINDS * image + 1, slots, stride).astype(LOW))
        right[image, :slots, :] = d_slot_in[image]
        right[image, slots:, :] = params[...]
        left[image, :slots, :] = dispatch[image].astype(LOW)
    local[...] = jnp.zeros_like(local)
    grads_copy.wait()
    parts = []
    for image in range(images):
        slot_out = take(wide, KINDS * image, slots, stride).astype(LOW)
        weights = combine[image]
        d_combine = dot(slot_out, grads_v[image], 1, 1)
        parts.append(
            weights * (d_combine - jnp.sum(weights * d_combine, axis=0, keepdims=True))
        )
    tokens_copy.wait()
    total = None
    for image in range(images):
        weights = dispatch[image]
        d_dispatch = dot(d_slot_in[image], tokens_v[image], 1, 1)
        d_logits = parts[image] + weights * (
            d_dispatch - jnp.sum(weights * d_dispatch, axis=1, keepdims=True)
        )
        low = d_logits.astype(LOW)
        left[image, slots:, :] = low
        part = dot(low, tokens_v[image], 1, 0)
        total = part if image == 0 else total + part
    for tile, (start, step) in enumerate(piece_rows(local, *params.shape)):
        local[pl.ds(start, slots, stride=step), :] = total[:, tile * LANES : (tile + 1) * LANES]


def piece_rows(pieces, slots, width):
    per_slot = pieces.shape[0] // TILE // slots
    used = width // LANES // per_slot
    step = per_slot * TILE
    return [(tile // used * TILE + tile % used, step) for tile in range(width // LANES)]


def logits_grads(after, back, tokens, params, grads, dispatch, combine, pieces):
    images, length, width = tokens.shape
    slots = params.shape[0]
    return call(
        logits_kernel,
        "logits_grads",
        SHARED,
        6 * images * slots * length * width,
        4 * images * length * width,
        out_shape=(
            shaped((images, 2 * slots, length), LOW),
            shaped((images, 2 * slots, width), LOW),
            shaped((pieces * TILE, LANES), WIDE),
            MARK,
        ),
        in_specs=[PLACE, WHOLE, PLACE, WHOLE, PLACE, WHOLE, WHOLE],
        out_specs=(WHOLE, WHOLE, WHOLE, PLACE),
        scratch_shapes=[
            pltpu.VMEM(tokens.shape, LOW),
            pltpu.VMEM(grads.shape, LOW),
            scratch_rows(back.shape),
            pltpu.SemaphoreType.DMA((2,)),
        ],
    )(after, back, tokens, params, grads, dispatch, combine)


def tokens_kernel(after, left, right, out):
    del after
    out[0] = dot(left[0], right[0], 0, 0).astype(LOW)


def tokens_grads(after, left, right):
    images, deep, length = left.shape
    width = right.shape[2]
    return call(
        tokens_kernel,
        "tokens_grads",
        SHARED,
        2 * images * deep * length * width,
        2 * images * length * width,
        grid=(images,),
        out_shape=shaped((images, length, width), LOW),
        in_specs=[
            PLACE,
            pl.BlockSpec((1, deep, length), lambda i: (i, 0, 0)),
            pl.BlockSpec((1, deep, width), lambda i: (i, 0, 0)),
        ],
        out_specs=pl.BlockSpec((1, length, width), lambda i: (i, 0, 0)),
    )(after, left, right)


def share_kernel(after, pieces, out, mark):
    del after, mark
    rows = pieces.shape[0]
    total = pieces[:TILE, :]
    for row in range(TILE, rows, TILE):
        total = total + pieces[row : row + TILE, :]
    for row in range(0, rows, TILE):
        out[row : row + TILE, :] = total


def share_of_sum(after, pieces):
    return call(
        share_kernel,
        "share_of_sum",
        SHARED,
        pieces.size,
        8 * pieces.size,
        out_shape=(shaped(pieces.shape, WIDE), MARK),
        in_specs=[PLACE, WHOLE],
        out_specs=(WHOLE, PLACE),
    )(after, pieces)


def unpack_kernel(pieces, out):
    slots, width = out.shape
    for tile, (start, step) in enumerate(piece_rows(pieces, slots, width)):
        out[:, tile * LANES : (tile + 1) * LANES] = pieces[pl.ds(start, slots, stride=step), :]


def unpack(pieces, shape):
    return call(
        unpack_kernel,
        "unpack_sum",
        SHARED,
        0,
        8 * pieces.size,
        out_shape=shaped(shape, WIDE),
        in_specs=[WHOLE],
        out_specs=WHOLE,
    )(pieces)


def exchange(rows, axes):
    return lax.all_to_all(rows, axes, split_axis=0, concat_axis=0, tiled=True)


def body(tokens, slot_params, expert_in, expert_out, grad_out):
    params = slot_params.T
    weights = (expert_in[0], expert_out[0])
    replicas = lax.axis_size("rep")
    everyone = ("rep", "exp")
    mine = lax.axis_index("rep").astype(jnp.int32).reshape(1)

    sent, dispatch, combine = gather(tokens, params, grad_out)
    rows = exchange(sent, "exp")
    other_rows = lax.ppermute(rows, "rep", [(i, (i + 1) % replicas) for i in range(replicas)])
    back, acts, hidden, after_expert = expert(rows, *weights, 512)
    other_acts, other_hidden, after_others = others_hidden(
        after_expert, other_rows, *weights, 512
    )
    back = exchange(back, "exp")
    left, right, local, after_logits = logits_grads(
        after_others, back, tokens, params, grad_out, dispatch, combine, lax.axis_size(everyone)
    )
    grad_expert_in, grad_expert_out, after_weights = weight_grads(
        mine,
        after_logits,
        (rows, other_rows),
        (acts, other_acts),
        (hidden, other_hidden),
        5,
        replicas,
    )
    share, after_share = share_of_sum(after_weights, exchange(local, everyone))
    grad_params = unpack(exchange(share, everyone), params.shape).T
    grad_tokens = tokens_grads(after_share, left, right)
    return (
        grad_tokens,
        grad_params,
        grad_expert_in[None],
        grad_expert_out[None],
    )


def solution(mesh):
    in_specs = (
        P(("rep", "exp"), None, None),
        P(),
        P("exp", None, None),
        P("exp", None, None),
        P(("rep", "exp"), None, None),
    )
    out_specs = (P(("rep", "exp"), None, None), P(), P("exp", "rep", None), P("exp", "rep", None))
    return jax.shard_map(body, mesh=mesh, in_specs=in_specs, out_specs=out_specs, check_vma=False)
```

```python
import functools
import math

import jax
import jax.numpy as jnp
from jax import lax
from jax.experimental import pallas as pl
from jax.experimental.pallas import tpu as pltpu
from jax.sharding import PartitionSpec as P

GELU_C = math.sqrt(2.0 / math.pi)
CUBIC = 0.044715
LOW = jnp.bfloat16
WIDE = jnp.float32
LANES = 128
KINDS = 2
SHARED = 52 * 1024 * 1024
WHOLE = pl.BlockSpec(memory_space=pltpu.VMEM)
PLACE = pl.BlockSpec(memory_space=pl.ANY)


def call(kernel, name, grant, flops, nbytes, exps=0, **kwargs):
    return pl.pallas_call(
        kernel,
        name=name,
        compiler_params=pltpu.CompilerParams(vmem_limit_bytes=grant),
        cost_estimate=pl.CostEstimate(
            flops=flops, bytes_accessed=nbytes, transcendentals=exps
        ),
        **kwargs,
    )


def shaped(shape, dtype):
    return jax.ShapeDtypeStruct(shape, dtype)


MARK = shaped((8, LANES), WIDE)


def gelu_parts(values):
    square = values * values
    tangent = jnp.tanh(GELU_C * (values + CUBIC * square * values))
    half = 0.5 * (1.0 + tangent)
    slope = half + 0.5 * values * (1.0 - tangent * tangent) * GELU_C * (1.0 + 3.0 * CUBIC * square)
    return values * half, slope


def dot(left, right, over_left, over_right):
    return lax.dot_general(
        left, right, (((over_left,), (over_right,)), ((), ())), preferred_element_type=WIDE
    )


def softmax(values, axis):
    raised = jnp.exp(values - jnp.max(values, axis=axis, keepdims=True))
    return raised / jnp.sum(raised, axis=axis, keepdims=True)


def scratch_rows(shape):
    return pltpu.VMEM((shape[1] // LANES, shape[0], LANES), WIDE)


def load_rows(ref, array):
    for tile in range(ref.shape[0]):
        ref[tile] = array[:, tile * LANES : (tile + 1) * LANES].astype(WIDE)


def packed(ref):
    return jnp.concatenate([ref[tile] for tile in range(ref.shape[0])], axis=1).astype(LOW)


def take(ref, start, count, stride, first=0, tiles=None):
    tiles = ref.shape[0] if tiles is None else tiles
    picked = [ref[first + tile, pl.ds(start, count, stride=stride), :] for tile in range(tiles)]
    return jnp.concatenate(picked, axis=1)


def put(ref, start, count, stride, array):
    for tile in range(ref.shape[0]):
        ref[tile, pl.ds(start, count, stride=stride), :] = array[
            :, tile * LANES : (tile + 1) * LANES
        ]


def start_copy(source, target, sem):
    copy = pltpu.make_async_copy(source, target, sem)
    copy.start()
    return copy


def gather_kernel(
    tokens, params, grads, sent, dispatch, combine, tokens_v, grads_v, rows, sems
):
    images = tokens.shape[0]
    slots = params.shape[0]
    stride = KINDS * images
    tokens_copy = start_copy(tokens, tokens_v, sems.at[0])
    grads_copy = start_copy(grads, grads_v, sems.at[1])
    tokens_copy.wait()
    logits = [dot(params[...], tokens_v[image], 1, 1) for image in range(images)]
    over_slots = []
    for image in range(images):
        over_tokens = softmax(logits[image], 1)
        dispatch[image] = over_tokens
        put(
            rows, KINDS * image, slots, stride, dot(over_tokens.astype(LOW), tokens_v[image], 1, 0)
        )
        over_slots.append(softmax(logits[image], 0))
        combine[image] = over_slots[image]
    grads_copy.wait()
    for image in range(images):
        value = dot(over_slots[image].astype(LOW), grads_v[image], 1, 0)
        put(rows, KINDS * image + 1, slots, stride, value)
    sent[...] = packed(rows)


def gather(tokens, params, grads):
    images, length, width = tokens.shape
    slots = params.shape[0]
    weights = shaped((images, slots, length), WIDE)
    rows = (slots * images * KINDS, width)
    return call(
        gather_kernel,
        "gather_slots",
        SHARED,
        6 * images * slots * length * width,
        4 * images * length * width,
        2 * images * slots * length,
        out_shape=(shaped(rows, LOW), weights, weights),
        in_specs=[PLACE, WHOLE, PLACE],
        out_specs=(WHOLE, WHOLE, WHOLE),
        scratch_shapes=[
            pltpu.VMEM(tokens.shape, LOW),
            pltpu.VMEM(grads.shape, LOW),
            scratch_rows(rows),
            pltpu.SemaphoreType.DMA((2,)),
        ],
    )(tokens, params, grads)


def chunks_of(hidden, tile):
    edges = [0, *range(tile // 2, hidden, tile), hidden]
    return [slice(first, last) for first, last in zip(edges, edges[1:])]


def start_weights(w_in, w_out, w_in_v, w_out_v, sems, tile):
    copies = []
    for chunk, units in enumerate(chunks_of(w_in.shape[1], tile)):
        copies.append(
            (
                start_copy(w_in.at[:, units], w_in_v.at[:, units], sems.at[0, chunk]),
                start_copy(w_out.at[units, :], w_out_v.at[units, :], sems.at[1, chunk]),
            )
        )
    return copies


def weight_scratch(width, hidden, tile):
    return [
        pltpu.VMEM((width, hidden), LOW),
        pltpu.VMEM((hidden, width), LOW),
        pltpu.SemaphoreType.DMA((2, len(chunks_of(hidden, tile)))),
    ]


def expert_kernel(
    tile, rows, w_in, w_out, back, acts, hidden, mark, w_in_v, w_out_v, sems, wide
):
    del mark
    copies = start_weights(w_in, w_out, w_in_v, w_out_v, sems, tile)
    count = rows.shape[0] // KINDS
    load_rows(wide, rows[...])
    rows_in = take(wide, 0, count, KINDS).astype(LOW)
    rows_grad = take(wide, 1, count, KINDS).astype(LOW)
    out = d_in = held = before = None
    for pair, units in zip([*copies, None], [*chunks_of(w_in.shape[1], tile), None]):
        if pair is not None:
            for copy in pair:
                copy.wait()
            preact = dot(rows_in, w_in_v[:, units], 1, 0)
            d_acts = dot(rows_grad, w_out_v[units, :], 1, 1)
        if before is not None:
            out_part = dot(held[0], w_out_v[before, :], 1, 0)
            d_in_part = dot(held[1], w_in_v[:, before], 1, 1)
            out = out_part if out is None else out + out_part
            d_in = d_in_part if d_in is None else d_in + d_in_part
        if pair is not None:
            values, slope = gelu_parts(preact)
            held = (values.astype(LOW), (d_acts * slope).astype(LOW))
            acts[:, units], hidden[:, units] = held
        before = units
    put(wide, 0, count, KINDS, out)
    put(wide, 1, count, KINDS, d_in)
    back[...] = packed(wide)


def expert(rows, w_in, w_out, tile):
    total, width = rows.shape
    hidden = w_in.shape[1]
    count = total // KINDS
    kept = shaped((count, hidden), LOW)
    return call(
        functools.partial(expert_kernel, tile),
        "expert_rows",
        SHARED,
        8 * count * hidden * width,
        4 * hidden * width,
        count * hidden,
        out_shape=(shaped(rows.shape, LOW), kept, kept, MARK),
        in_specs=[WHOLE, PLACE, PLACE],
        out_specs=(WHOLE, WHOLE, WHOLE, PLACE),
        scratch_shapes=[*weight_scratch(width, hidden, tile), scratch_rows(rows.shape)],
    )(rows, w_in, w_out)


def others_kernel(
    tile, after, rows, w_in, w_out, acts, hidden, mark, w_in_v, w_out_v, sems, wide
):
    del after, mark
    copies = start_weights(w_in, w_out, w_in_v, w_out_v, sems, tile)
    count = rows.shape[0] // KINDS
    load_rows(wide, rows[...])
    rows_in = take(wide, 0, count, KINDS).astype(LOW)
    rows_grad = take(wide, 1, count, KINDS).astype(LOW)
    for pair, units in zip(copies, chunks_of(w_in.shape[1], tile)):
        for copy in pair:
            copy.wait()
        values, slope = gelu_parts(dot(rows_in, w_in_v[:, units], 1, 0))
        acts[:, units] = values.astype(LOW)
        d_acts = dot(rows_grad, w_out_v[units, :], 1, 1)
        hidden[:, units] = (d_acts * slope).astype(LOW)


def others_hidden(after, rows, w_in, w_out, tile):
    total, width = rows.shape
    hidden = w_in.shape[1]
    count = total // KINDS
    kept = shaped((count, hidden), LOW)
    return call(
        functools.partial(others_kernel, tile),
        "others_hidden",
        SHARED,
        64 * count * hidden * width,
        32 * hidden * width,
        count * hidden,
        out_shape=(kept, kept, MARK),
        in_specs=[PLACE, WHOLE, PLACE, PLACE],
        out_specs=(WHOLE, WHOLE, PLACE),
        scratch_shapes=[*weight_scratch(width, hidden, tile), scratch_rows(rows.shape)],
    )(after, rows, w_in, w_out)


def weights_kernel(
    mine, after, rows, other_rows, acts, other_acts, hidden, other_hidden, grad_in, grad_out, mark,
    wide, grads, turned,
):
    del after, mark
    count = rows.shape[0] // KINDS

    @pl.when(pl.program_id(0) == 0)
    def _():
        left, right = [], []
        tiles = turned.shape[0] // LANES
        for source in (rows, other_rows):
            load_rows(wide, source[...])
            left.append(take(wide, 0, count, KINDS, mine[0] * tiles, tiles))
            right.append(take(wide, 1, count, KINDS))
        turned[...] = jnp.concatenate(left, axis=0).T.astype(LOW)
        grads[...] = jnp.concatenate(right, axis=0).astype(LOW)

    all_hidden = jnp.concatenate([hidden[...], other_hidden[...]], axis=0)
    grad_in[...] = dot(turned[...], all_hidden, 1, 0).astype(LOW)
    all_acts = jnp.concatenate([acts[...], other_acts[...]], axis=0)
    grad_out[...] = dot(all_acts, grads[...], 0, 0).astype(LOW)


def weight_grads(mine, after, rows, acts, hidden, steps, replicas):
    total, width = rows[0].shape
    size = acts[0].shape[1]
    count = total // KINDS
    in_tile, out_tile = size // steps, size // replicas // steps
    whole_rows = pl.BlockSpec((total, width), lambda i, mine: (0, 0))
    acts_spec = pl.BlockSpec((count, out_tile), lambda i, mine: (0, mine[0] * steps + i))
    hidden_spec = pl.BlockSpec((count, in_tile), lambda i, mine: (0, i))
    return call(
        weights_kernel,
        "weight_grads",
        SHARED,
        8 * count * size * width // replicas,
        4 * size * width // replicas,
        grid_spec=pltpu.PrefetchScalarGridSpec(
            num_scalar_prefetch=1,
            grid=(steps,),
            in_specs=[PLACE] + [whole_rows] * 2 + [acts_spec] * 2 + [hidden_spec] * 2,
            out_specs=(
                pl.BlockSpec((width // replicas, in_tile), lambda i, mine: (0, i)),
                pl.BlockSpec((out_tile, width), lambda i, mine: (i, 0)),
                PLACE,
            ),
            scratch_shapes=[
                scratch_rows((total, width)),
                pltpu.VMEM((2 * count, width), LOW),
                pltpu.VMEM((width // replicas, 2 * count), LOW),
            ],
        ),
        out_shape=(
            shaped((width // replicas, size), LOW),
            shaped((size // replicas, width), LOW),
            MARK,
        ),
    )(mine, after, *rows, *acts, *hidden)


def logits_kernel(
    after, back, tokens, params, grads, dispatch, combine, left, right, local, mark,
    tokens_v, grads_v, wide, sems,
):
    del after, mark
    images, slots, _ = dispatch.shape
    grads_copy = start_copy(grads, grads_v, sems.at[0])
    tokens_copy = start_copy(tokens, tokens_v, sems.at[1])
    load_rows(wide, back[...])
    stride = KINDS * images
    d_slot_in = []
    for image in range(images):
        d_slot_in.append(take(wide, KINDS * image + 1, slots, stride).astype(LOW))
        right[image, :slots, :] = d_slot_in[image]
        right[image, slots:, :] = params[...]
        left[image, :slots, :] = dispatch[image].astype(LOW)
    grads_copy.wait()
    parts = []
    for image in range(images):
        slot_out = take(wide, KINDS * image, slots, stride).astype(LOW)
        weights = combine[image]
        d_combine = dot(slot_out, grads_v[image], 1, 1)
        parts.append(
            weights * (d_combine - jnp.sum(weights * d_combine, axis=0, keepdims=True))
        )
    tokens_copy.wait()
    total = None
    for image in range(images):
        weights = dispatch[image]
        d_dispatch = dot(d_slot_in[image], tokens_v[image], 1, 1)
        d_logits = parts[image] + weights * (
            d_dispatch - jnp.sum(weights * d_dispatch, axis=1, keepdims=True)
        )
        low = d_logits.astype(LOW)
        left[image, slots:, :] = low
        part = dot(low, tokens_v[image], 1, 0)
        total = part if image == 0 else total + part
    for row in range(slots):
        local[row] = total[row : row + 1, :]


def logits_grads(after, back, tokens, params, grads, dispatch, combine):
    images, length, width = tokens.shape
    slots = params.shape[0]
    return call(
        logits_kernel,
        "logits_grads",
        SHARED,
        6 * images * slots * length * width,
        4 * images * length * width,
        out_shape=(
            shaped((images, 2 * slots, length), LOW),
            shaped((images, 2 * slots, width), LOW),
            shaped((slots, 1, width), WIDE),
            MARK,
        ),
        in_specs=[PLACE, WHOLE, PLACE, WHOLE, PLACE, WHOLE, WHOLE],
        out_specs=(WHOLE, WHOLE, WHOLE, PLACE),
        scratch_shapes=[
            pltpu.VMEM(tokens.shape, LOW),
            pltpu.VMEM(grads.shape, LOW),
            scratch_rows(back.shape),
            pltpu.SemaphoreType.DMA((2,)),
        ],
    )(after, back, tokens, params, grads, dispatch, combine)


def tokens_kernel(after, left, right, out):
    del after
    out[0] = dot(left[0], right[0], 0, 0).astype(LOW)


def tokens_grads(after, left, right):
    images, deep, length = left.shape
    width = right.shape[2]
    return call(
        tokens_kernel,
        "tokens_grads",
        SHARED,
        2 * images * deep * length * width,
        2 * images * length * width,
        grid=(images,),
        out_shape=shaped((images, length, width), LOW),
        in_specs=[
            PLACE,
            pl.BlockSpec((1, deep, length), lambda i: (i, 0, 0)),
            pl.BlockSpec((1, deep, width), lambda i: (i, 0, 0)),
        ],
        out_specs=pl.BlockSpec((1, length, width), lambda i: (i, 0, 0)),
    )(after, left, right)


def share_kernel(after, parts, out, mark):
    del after, mark
    total = jnp.sum(parts[...], axis=0, keepdims=True)
    out[...] = jnp.broadcast_to(total, out.shape)


def share_of_sum(after, parts, copies):
    shape = (copies, *parts.shape[1:])
    return call(
        share_kernel,
        "share_of_sum",
        SHARED,
        parts.size,
        8 * parts.size,
        out_shape=(shaped(shape, WIDE), MARK),
        in_specs=[PLACE, WHOLE],
        out_specs=(WHOLE, PLACE),
    )(after, parts)


def total_kernel(shares, out):
    slots = out.shape[0]
    for slot in range(slots):
        total = shares[slot]
        for replica in range(1, shares.shape[0] // slots):
            total = total + shares[replica * slots + slot]
        out[slot : slot + 1, :] = total


def total_of_shares(shares, shape):
    return call(
        total_kernel,
        "total_of_shares",
        SHARED,
        shares.size,
        8 * shares.size,
        out_shape=shaped(shape, WIDE),
        in_specs=[WHOLE],
        out_specs=WHOLE,
    )(shares)


def copy_kernel(after, source, target):
    del after
    target[...] = source[...]


def copy_after(after, array):
    return call(
        copy_kernel,
        "copy_after",
        SHARED,
        0,
        4 * array.size,
        out_shape=shaped(array.shape, array.dtype),
        in_specs=[PLACE, WHOLE],
        out_specs=WHOLE,
    )(after, array)


def exchange(rows, axes):
    return lax.all_to_all(rows, axes, split_axis=0, concat_axis=0, tiled=True)


def body(tokens, slot_params, expert_in, expert_out, grad_out):
    params = slot_params.T
    weights = (expert_in[0], expert_out[0])
    replicas = lax.axis_size("rep")
    everyone = ("rep", "exp")
    mine = lax.axis_index("rep").astype(jnp.int32).reshape(1)

    sent, dispatch, combine = gather(tokens, params, grad_out)
    rows = exchange(sent, "exp")
    back, acts, hidden, after_expert = expert(rows, *weights, 512)
    back = exchange(back, "exp")
    other_rows = lax.ppermute(
        copy_after(after_expert, rows), "rep", [(i, (i + 1) % replicas) for i in range(replicas)]
    )
    left, right, local, after_logits = logits_grads(
        after_expert, back, tokens, params, grad_out, dispatch, combine
    )
    other_acts, other_hidden, after_others = others_hidden(
        after_logits, other_rows, *weights, 512
    )
    share, after_share = share_of_sum(
        after_others, exchange(local, "exp"), lax.axis_size(everyone)
    )
    grad_expert_in, grad_expert_out, _ = weight_grads(
        mine,
        after_share,
        (rows, other_rows),
        (acts, other_acts),
        (hidden, other_hidden),
        5,
        replicas,
    )
    grad_params = total_of_shares(exchange(share, everyone), params.shape).T
    grad_tokens = tokens_grads(after_share, left, right)
    return (
        grad_tokens,
        grad_params,
        grad_expert_in[None],
        grad_expert_out[None],
    )


def solution(mesh):
    in_specs = (
        P(("rep", "exp"), None, None),
        P(),
        P("exp", None, None),
        P("exp", None, None),
        P(("rep", "exp"), None, None),
    )
    out_specs = (P(("rep", "exp"), None, None), P(), P("exp", "rep", None), P("exp", "rep", None))
    return jax.shard_map(body, mesh=mesh, in_specs=in_specs, out_specs=out_specs, check_vma=False)
```

```python
import functools
import math

import jax
import jax.numpy as jnp
from jax import lax
from jax.experimental import pallas as pl
from jax.experimental.pallas import tpu as pltpu
from jax.sharding import PartitionSpec as P

GELU_C = math.sqrt(2.0 / math.pi)
CUBIC = 0.044715
LOW = jnp.bfloat16
WIDE = jnp.float32
LANES = 128
KINDS = 2
SHARED = 52 * 1024 * 1024
WHOLE = pl.BlockSpec(memory_space=pltpu.VMEM)
PLACE = pl.BlockSpec(memory_space=pl.ANY)


def call(kernel, name, grant, flops, nbytes, exps=0, **kwargs):
    return pl.pallas_call(
        kernel,
        name=name,
        compiler_params=pltpu.CompilerParams(vmem_limit_bytes=grant),
        cost_estimate=pl.CostEstimate(
            flops=flops, bytes_accessed=nbytes, transcendentals=exps
        ),
        **kwargs,
    )


def shaped(shape, dtype):
    return jax.ShapeDtypeStruct(shape, dtype)


MARK = shaped((8, LANES), WIDE)


def gelu_parts(values):
    square = values * values
    tangent = jnp.tanh(GELU_C * (values + CUBIC * square * values))
    half = 0.5 * (1.0 + tangent)
    slope = half + 0.5 * values * (1.0 - tangent * tangent) * GELU_C * (1.0 + 3.0 * CUBIC * square)
    return values * half, slope


def dot(left, right, over_left, over_right):
    return lax.dot_general(
        left, right, (((over_left,), (over_right,)), ((), ())), preferred_element_type=WIDE
    )


def softmax(values, axis):
    raised = jnp.exp(values - jnp.max(values, axis=axis, keepdims=True))
    return raised / jnp.sum(raised, axis=axis, keepdims=True)


def scratch_rows(shape):
    return pltpu.VMEM((shape[1] // LANES, shape[0], LANES), WIDE)


def load_rows(ref, array):
    for tile in range(ref.shape[0]):
        ref[tile] = array[:, tile * LANES : (tile + 1) * LANES].astype(WIDE)


def packed(ref):
    return jnp.concatenate([ref[tile] for tile in range(ref.shape[0])], axis=1).astype(LOW)


def take(ref, start, count, stride, first=0, tiles=None):
    tiles = ref.shape[0] if tiles is None else tiles
    picked = [ref[first + tile, pl.ds(start, count, stride=stride), :] for tile in range(tiles)]
    return jnp.concatenate(picked, axis=1)


def put(ref, start, count, stride, array):
    for tile in range(ref.shape[0]):
        ref[tile, pl.ds(start, count, stride=stride), :] = array[
            :, tile * LANES : (tile + 1) * LANES
        ]


def start_copy(source, target, sem):
    copy = pltpu.make_async_copy(source, target, sem)
    copy.start()
    return copy


def start_halves(source, target, sems):
    images = source.shape[0]
    parts = []
    for index, (first, last) in enumerate(((0, images // 2), (images // 2, images))):
        part = pl.ds(first, last - first)
        copy = start_copy(source.at[part], target.at[part], sems.at[index])
        parts.append((copy, range(first, last)))
    return parts


def gather_kernel(
    tokens, params, grads, sent, dispatch, combine, mark, tokens_v, grads_v, rows, sems
):
    del mark
    images = tokens.shape[0]
    slots = params.shape[0]
    stride = KINDS * images
    halves = start_halves(tokens, tokens_v, sems)
    grads_copy = start_copy(grads, grads_v, sems.at[2])
    logits = []
    for copy, half in halves:
        copy.wait()
        logits += [dot(params[...], tokens_v[image], 1, 1) for image in half]
    over_slots = []
    for image in range(images):
        over_tokens = softmax(logits[image], 1)
        dispatch[image] = over_tokens
        put(
            rows, KINDS * image, slots, stride, dot(over_tokens.astype(LOW), tokens_v[image], 1, 0)
        )
        over_slots.append(softmax(logits[image], 0))
        combine[image] = over_slots[image]
    grads_copy.wait()
    for image in range(images):
        value = dot(over_slots[image].astype(LOW), grads_v[image], 1, 0)
        put(rows, KINDS * image + 1, slots, stride, value)
    sent[...] = packed(rows)


def gather(tokens, params, grads):
    images, length, width = tokens.shape
    slots = params.shape[0]
    weights = shaped((images, slots, length), WIDE)
    rows = (slots * images * KINDS, width)
    return call(
        gather_kernel,
        "gather_slots",
        SHARED,
        6 * images * slots * length * width,
        4 * images * length * width,
        2 * images * slots * length,
        out_shape=(shaped(rows, LOW), weights, weights, MARK),
        in_specs=[PLACE, WHOLE, PLACE],
        out_specs=(WHOLE, WHOLE, WHOLE, PLACE),
        scratch_shapes=[
            pltpu.VMEM(tokens.shape, LOW),
            pltpu.VMEM(grads.shape, LOW),
            scratch_rows(rows),
            pltpu.SemaphoreType.DMA((3,)),
        ],
    )(tokens, params, grads)


def chunks_of(first, hidden, tile):
    edges = [*range(first, hidden, tile), hidden]
    return [slice(low, high) for low, high in zip(edges, edges[1:])]


def start_weights(w_in, w_out, w_in_v, w_out_v, sems, chunks):
    copies = []
    for chunk, units in enumerate(chunks):
        copies.append(
            (
                start_copy(w_in.at[:, units], w_in_v.at[:, units], sems.at[0, chunk]),
                start_copy(w_out.at[units, :], w_out_v.at[units, :], sems.at[1, chunk]),
            )
        )
    return copies


def weight_scratch(width, hidden, chunks):
    return [
        pltpu.VMEM((width, hidden), LOW),
        pltpu.VMEM((hidden, width), LOW),
        pltpu.SemaphoreType.DMA((2, len(chunks))),
    ]


def fetch_kernel(after, w_in, w_out, first_in, first_out, sems):
    del after
    units = slice(0, first_out.shape[0])
    copies = (
        start_copy(w_in.at[:, units], first_in, sems.at[0]),
        start_copy(w_out.at[units, :], first_out, sems.at[1]),
    )
    for copy in copies:
        copy.wait()


def fetch_first(after, w_in, w_out, count):
    width = w_in.shape[0]
    return call(
        fetch_kernel,
        "fetch_first",
        SHARED,
        0,
        8 * count * width,
        out_shape=(shaped((width, count), LOW), shaped((count, width), LOW)),
        in_specs=[PLACE] * 3,
        out_specs=(WHOLE,) * 2,
        scratch_shapes=[pltpu.SemaphoreType.DMA((2,))],
    )(after, w_in, w_out)


def expert_kernel(
    chunks, rows, first_in, first_out, w_in, w_out, back, acts, hidden, mark,
    w_in_v, w_out_v, sems, wide,
):
    del mark
    copies = start_weights(w_in, w_out, w_in_v, w_out_v, sems, chunks)
    count = rows.shape[0] // KINDS
    load_rows(wide, rows[...])
    rows_in = take(wide, 0, count, KINDS).astype(LOW)
    rows_grad = take(wide, 1, count, KINDS).astype(LOW)

    def first_products(weight_in, weight_out):
        return dot(rows_in, weight_in, 1, 0), dot(rows_grad, weight_out, 1, 1)

    def second_products(held, weight_in, weight_out):
        return dot(held[0], weight_out, 1, 0), dot(held[1], weight_in, 1, 1)

    def hold(preact, d_acts, units):
        values, slope = gelu_parts(preact)
        held = (values.astype(LOW), (d_acts * slope).astype(LOW))
        acts[:, units], hidden[:, units] = held
        return held

    held = hold(
        *first_products(first_in[...], first_out[...]), slice(0, first_out.shape[0])
    )
    out, d_in = second_products(held, first_in[...], first_out[...])
    before = None
    for pair, units in zip([*copies, None], [*chunks, None]):
        if pair is not None:
            for copy in pair:
                copy.wait()
            products = first_products(w_in_v[:, units], w_out_v[units, :])
        if before is not None:
            parts = second_products(held, w_in_v[:, before], w_out_v[before, :])
            out, d_in = out + parts[0], d_in + parts[1]
        if pair is not None:
            held = hold(*products, units)
        before = units
    put(wide, 0, count, KINDS, out)
    put(wide, 1, count, KINDS, d_in)
    back[...] = packed(wide)


def expert(rows, first_in, first_out, w_in, w_out, tile):
    total, width = rows.shape
    hidden = w_in.shape[1]
    count = total // KINDS
    kept = shaped((count, hidden), LOW)
    chunks = chunks_of(first_out.shape[0], hidden, tile)
    return call(
        functools.partial(expert_kernel, chunks),
        "expert_rows",
        50 * 1024 * 1024,
        8 * count * hidden * width,
        4 * hidden * width,
        count * hidden,
        out_shape=(shaped(rows.shape, LOW), kept, kept, MARK),
        in_specs=[WHOLE, WHOLE, WHOLE, PLACE, PLACE],
        out_specs=(WHOLE, WHOLE, WHOLE, PLACE),
        scratch_shapes=[*weight_scratch(width, hidden, chunks), scratch_rows(rows.shape)],
    )(rows, first_in, first_out, w_in, w_out)


def others_kernel(
    chunks, after, rows, w_in, w_out, acts, hidden, mark, w_in_v, w_out_v, sems, wide
):
    del after, mark
    copies = start_weights(w_in, w_out, w_in_v, w_out_v, sems, chunks)
    count = rows.shape[0] // KINDS
    load_rows(wide, rows[...])
    rows_in = take(wide, 0, count, KINDS).astype(LOW)
    rows_grad = take(wide, 1, count, KINDS).astype(LOW)
    for pair, units in zip(copies, chunks):
        for copy in pair:
            copy.wait()
        values, slope = gelu_parts(dot(rows_in, w_in_v[:, units], 1, 0))
        acts[:, units] = values.astype(LOW)
        d_acts = dot(rows_grad, w_out_v[units, :], 1, 1)
        hidden[:, units] = (d_acts * slope).astype(LOW)


def others_hidden(after, rows, w_in, w_out, tile):
    total, width = rows.shape
    hidden = w_in.shape[1]
    count = total // KINDS
    kept = shaped((count, hidden), LOW)
    chunks = chunks_of(0, hidden, tile)
    return call(
        functools.partial(others_kernel, chunks),
        "others_hidden",
        SHARED,
        64 * count * hidden * width,
        32 * hidden * width,
        count * hidden,
        out_shape=(kept, kept, MARK),
        in_specs=[PLACE, WHOLE, PLACE, PLACE],
        out_specs=(WHOLE, WHOLE, PLACE),
        scratch_shapes=[*weight_scratch(width, hidden, chunks), scratch_rows(rows.shape)],
    )(after, rows, w_in, w_out)


def weights_kernel(
    mine, after, rows, other_rows, acts, other_acts, hidden, other_hidden, grad_in, grad_out, mark,
    wide, grads, turned,
):
    del after, mark
    count = rows.shape[0] // KINDS

    @pl.when(pl.program_id(0) == 0)
    def _():
        left, right = [], []
        tiles = turned.shape[0] // LANES
        for source in (rows, other_rows):
            load_rows(wide, source[...])
            left.append(take(wide, 0, count, KINDS, mine[0] * tiles, tiles))
            right.append(take(wide, 1, count, KINDS))
        turned[...] = jnp.concatenate(left, axis=0).T.astype(LOW)
        grads[...] = jnp.concatenate(right, axis=0).astype(LOW)

    all_hidden = jnp.concatenate([hidden[...], other_hidden[...]], axis=0)
    grad_in[...] = dot(turned[...], all_hidden, 1, 0).astype(LOW)
    all_acts = jnp.concatenate([acts[...], other_acts[...]], axis=0)
    grad_out[...] = dot(all_acts, grads[...], 0, 0).astype(LOW)


def weight_grads(mine, after, rows, acts, hidden, steps, replicas):
    total, width = rows[0].shape
    size = acts[0].shape[1]
    count = total // KINDS
    in_tile, out_tile = size // steps, size // replicas // steps
    whole_rows = pl.BlockSpec((total, width), lambda i, mine: (0, 0))
    acts_spec = pl.BlockSpec((count, out_tile), lambda i, mine: (0, mine[0] * steps + i))
    hidden_spec = pl.BlockSpec((count, in_tile), lambda i, mine: (0, i))
    return call(
        weights_kernel,
        "weight_grads",
        SHARED,
        8 * count * size * width // replicas,
        4 * size * width // replicas,
        grid_spec=pltpu.PrefetchScalarGridSpec(
            num_scalar_prefetch=1,
            grid=(steps,),
            in_specs=[PLACE] + [whole_rows] * 2 + [acts_spec] * 2 + [hidden_spec] * 2,
            out_specs=(
                pl.BlockSpec((width // replicas, in_tile), lambda i, mine: (0, i)),
                pl.BlockSpec((out_tile, width), lambda i, mine: (i, 0)),
                PLACE,
            ),
            scratch_shapes=[
                scratch_rows((total, width)),
                pltpu.VMEM((2 * count, width), LOW),
                pltpu.VMEM((width // replicas, 2 * count), LOW),
            ],
        ),
        out_shape=(
            shaped((width // replicas, size), LOW),
            shaped((size // replicas, width), LOW),
            MARK,
        ),
    )(mine, after, *rows, *acts, *hidden)


def put_pieces(pieces, array):
    size = pieces.shape[2]
    per_row = array.shape[1] // size
    for piece in range(pieces.shape[0]):
        row, at = piece // per_row, piece % per_row * size
        pieces[piece] = array[row : row + 1, at : at + size]


def logits_kernel(
    after, back, tokens, params, grads, dispatch, combine, left, right, local, mark,
    tokens_v, grads_v, wide, sems,
):
    del after, mark
    images, slots, _ = dispatch.shape
    halves = start_halves(tokens, tokens_v, sems)
    grads_copy = start_copy(grads, grads_v, sems.at[2])
    load_rows(wide, back[...])
    stride = KINDS * images
    d_slot_in = []
    for image in range(images):
        d_slot_in.append(take(wide, KINDS * image + 1, slots, stride).astype(LOW))
        right[image, :slots, :] = d_slot_in[image]
        right[image, slots:, :] = params[...]
        left[image, :slots, :] = dispatch[image].astype(LOW)
    parts = []
    for copy, half in halves:
        copy.wait()
        for image in half:
            weights = dispatch[image]
            d_dispatch = dot(d_slot_in[image], tokens_v[image], 1, 1)
            parts.append(
                weights * (d_dispatch - jnp.sum(weights * d_dispatch, axis=1, keepdims=True))
            )
    grads_copy.wait()
    total = None
    for image in range(images):
        slot_out = take(wide, KINDS * image, slots, stride).astype(LOW)
        weights = combine[image]
        d_combine = dot(slot_out, grads_v[image], 1, 1)
        d_logits = parts[image] + weights * (
            d_combine - jnp.sum(weights * d_combine, axis=0, keepdims=True)
        )
        low = d_logits.astype(LOW)
        left[image, slots:, :] = low
        part = dot(low, tokens_v[image], 1, 0)
        total = part if image == 0 else total + part
    put_pieces(local, total)


def logits_grads(after, back, tokens, params, grads, dispatch, combine, pieces):
    images, length, width = tokens.shape
    slots = params.shape[0]
    return call(
        logits_kernel,
        "logits_grads",
        SHARED,
        6 * images * slots * length * width,
        4 * images * length * width,
        out_shape=(
            shaped((images, 2 * slots, length), LOW),
            shaped((images, 2 * slots, width), LOW),
            shaped((pieces, 1, slots * width // pieces), WIDE),
            MARK,
        ),
        in_specs=[PLACE, WHOLE, PLACE, WHOLE, PLACE, WHOLE, WHOLE],
        out_specs=(WHOLE, WHOLE, WHOLE, PLACE),
        scratch_shapes=[
            pltpu.VMEM(tokens.shape, LOW),
            pltpu.VMEM(grads.shape, LOW),
            scratch_rows(back.shape),
            pltpu.SemaphoreType.DMA((3,)),
        ],
    )(after, back, tokens, params, grads, dispatch, combine)


def tokens_kernel(after, left, right, out):
    del after
    out[0] = dot(left[0], right[0], 0, 0).astype(LOW)


def tokens_grads(after, left, right):
    images, deep, length = left.shape
    width = right.shape[2]
    return call(
        tokens_kernel,
        "tokens_grads",
        SHARED,
        2 * images * deep * length * width,
        2 * images * length * width,
        grid=(images,),
        out_shape=shaped((images, length, width), LOW),
        in_specs=[
            PLACE,
            pl.BlockSpec((1, deep, length), lambda i: (i, 0, 0)),
            pl.BlockSpec((1, deep, width), lambda i: (i, 0, 0)),
        ],
        out_specs=pl.BlockSpec((1, length, width), lambda i: (i, 0, 0)),
    )(after, left, right)


def share_kernel(after, parts, out, mark):
    del after, mark
    total = jnp.sum(parts[...], axis=0, keepdims=True)
    out[...] = jnp.broadcast_to(total, out.shape)


def share_of_sum(after, parts):
    return call(
        share_kernel,
        "share_of_sum",
        SHARED,
        parts.size,
        8 * parts.size,
        out_shape=(shaped(parts.shape, WIDE), MARK),
        in_specs=[PLACE, WHOLE],
        out_specs=(WHOLE, PLACE),
    )(after, parts)


def join_kernel(pieces, out):
    size = pieces.shape[2]
    per_row = out.shape[1] // size
    for piece in range(pieces.shape[0]):
        row, at = piece // per_row, piece % per_row * size
        out[row : row + 1, at : at + size] = pieces[piece]


def join(pieces, shape):
    return call(
        join_kernel,
        "join_pieces",
        SHARED,
        0,
        8 * pieces.size,
        out_shape=shaped(shape, WIDE),
        in_specs=[WHOLE],
        out_specs=WHOLE,
    )(pieces)


def copy_kernel(after, source, target):
    del after
    target[...] = source[...]


def copy_after(after, array):
    return call(
        copy_kernel,
        "copy_after",
        SHARED,
        0,
        4 * array.size,
        out_shape=shaped(array.shape, array.dtype),
        in_specs=[PLACE, WHOLE],
        out_specs=WHOLE,
    )(after, array)


def exchange(rows, axes):
    return lax.all_to_all(rows, axes, split_axis=0, concat_axis=0, tiled=True)


def body(tokens, slot_params, expert_in, expert_out, grad_out):
    params = slot_params.T
    weights = (expert_in[0], expert_out[0])
    replicas = lax.axis_size("rep")
    everyone = ("rep", "exp")
    mine = lax.axis_index("rep").astype(jnp.int32).reshape(1)

    sent, dispatch, combine, after_gather = gather(tokens, params, grad_out)
    rows = exchange(sent, "exp")
    first = fetch_first(after_gather, *weights, 256)
    back, acts, hidden, after_expert = expert(rows, *first, *weights, 512)
    back = exchange(back, "exp")
    other_rows = lax.ppermute(
        copy_after(after_expert, rows), "rep", [(i, (i + 1) % replicas) for i in range(replicas)]
    )
    left, right, local, after_logits = logits_grads(
        after_expert, back, tokens, params, grad_out, dispatch, combine, lax.axis_size(everyone)
    )
    other_acts, other_hidden, after_others = others_hidden(
        after_logits, other_rows, *weights, 512
    )
    share, after_share = share_of_sum(after_others, exchange(local, everyone))
    grad_expert_in, grad_expert_out, _ = weight_grads(
        mine,
        after_share,
        (rows, other_rows),
        (acts, other_acts),
        (hidden, other_hidden),
        5,
        replicas,
    )
    grad_params = join(exchange(share, everyone), params.shape).T
    grad_tokens = tokens_grads(after_share, left, right)
    return (
        grad_tokens,
        grad_params,
        grad_expert_in[None],
        grad_expert_out[None],
    )


def solution(mesh):
    in_specs = (
        P(("rep", "exp"), None, None),
        P(),
        P("exp", None, None),
        P("exp", None, None),
        P(("rep", "exp"), None, None),
    )
    out_specs = (P(("rep", "exp"), None, None), P(), P("exp", "rep", None), P("exp", "rep", None))
    return jax.shard_map(body, mesh=mesh, in_specs=in_specs, out_specs=out_specs, check_vma=False)
```

```python
import functools
import math

import jax
import jax.numpy as jnp
from jax import lax
from jax.experimental import pallas as pl
from jax.experimental.pallas import tpu as pltpu
from jax.sharding import PartitionSpec as P

GELU_C = math.sqrt(2.0 / math.pi)
CUBIC = 0.044715
LOW = jnp.bfloat16
WIDE = jnp.float32
LANES = 128
KINDS = 2
SHARED = 52 * 1024 * 1024
WHOLE = pl.BlockSpec(memory_space=pltpu.VMEM)
PLACE = pl.BlockSpec(memory_space=pl.ANY)


def call(kernel, name, grant, flops, nbytes, exps=0, **kwargs):
    return pl.pallas_call(
        kernel,
        name=name,
        compiler_params=pltpu.CompilerParams(vmem_limit_bytes=grant),
        cost_estimate=pl.CostEstimate(
            flops=flops, bytes_accessed=nbytes, transcendentals=exps
        ),
        **kwargs,
    )


def shaped(shape, dtype):
    return jax.ShapeDtypeStruct(shape, dtype)


MARK = shaped((8, LANES), WIDE)


def gelu_parts(values):
    square = values * values
    tangent = jnp.tanh(GELU_C * (values + CUBIC * square * values))
    half = 0.5 * (1.0 + tangent)
    slope = half + 0.5 * values * (1.0 - tangent * tangent) * GELU_C * (1.0 + 3.0 * CUBIC * square)
    return values * half, slope


def dot(left, right, over_left, over_right):
    return lax.dot_general(
        left, right, (((over_left,), (over_right,)), ((), ())), preferred_element_type=WIDE
    )


def softmax(values, axis):
    raised = jnp.exp(values - jnp.max(values, axis=axis, keepdims=True))
    return raised / jnp.sum(raised, axis=axis, keepdims=True)


def scratch_rows(shape):
    return pltpu.VMEM((shape[1] // LANES, shape[0], LANES), WIDE)


def load_rows(ref, array):
    for tile in range(ref.shape[0]):
        ref[tile] = array[:, tile * LANES : (tile + 1) * LANES].astype(WIDE)


def packed(ref):
    return jnp.concatenate([ref[tile] for tile in range(ref.shape[0])], axis=1).astype(LOW)


def take(ref, start, count, stride, first=0, tiles=None):
    tiles = ref.shape[0] if tiles is None else tiles
    picked = [ref[first + tile, pl.ds(start, count, stride=stride), :] for tile in range(tiles)]
    return jnp.concatenate(picked, axis=1)


def put(ref, start, count, stride, array):
    for tile in range(ref.shape[0]):
        ref[tile, pl.ds(start, count, stride=stride), :] = array[
            :, tile * LANES : (tile + 1) * LANES
        ]


def start_copy(source, target, sem):
    copy = pltpu.make_async_copy(source, target, sem)
    copy.start()
    return copy


def start_halves(source, target, sems):
    images = source.shape[0]
    parts = []
    for index, (first, last) in enumerate(((0, images // 2), (images // 2, images))):
        part = pl.ds(first, last - first)
        copy = start_copy(source.at[part], target.at[part], sems.at[index])
        parts.append((copy, range(first, last)))
    return parts


def gather_kernel(
    tokens, params, grads, sent, dispatch, combine, mark, tokens_v, grads_v, rows, sems
):
    del mark
    images = tokens.shape[0]
    slots = params.shape[0]
    stride = KINDS * images
    halves = start_halves(tokens, tokens_v, sems)
    grads_copy = start_copy(grads, grads_v, sems.at[2])
    logits = []
    for copy, half in halves:
        copy.wait()
        logits += [dot(params[...], tokens_v[image], 1, 1) for image in half]
    over_slots = []
    for image in range(images):
        over_tokens = softmax(logits[image], 1)
        dispatch[image] = over_tokens
        put(
            rows, KINDS * image, slots, stride, dot(over_tokens.astype(LOW), tokens_v[image], 1, 0)
        )
        over_slots.append(softmax(logits[image], 0))
        combine[image] = over_slots[image]
    grads_copy.wait()
    for image in range(images):
        value = dot(over_slots[image].astype(LOW), grads_v[image], 1, 0)
        put(rows, KINDS * image + 1, slots, stride, value)
    sent[...] = packed(rows)


def gather(tokens, params, grads):
    images, length, width = tokens.shape
    slots = params.shape[0]
    weights = shaped((images, slots, length), WIDE)
    rows = (slots * images * KINDS, width)
    return call(
        gather_kernel,
        "gather_slots",
        SHARED,
        6 * images * slots * length * width,
        4 * images * length * width,
        2 * images * slots * length,
        out_shape=(shaped(rows, LOW), weights, weights, MARK),
        in_specs=[PLACE, WHOLE, PLACE],
        out_specs=(WHOLE, WHOLE, WHOLE, PLACE),
        scratch_shapes=[
            pltpu.VMEM(tokens.shape, LOW),
            pltpu.VMEM(grads.shape, LOW),
            scratch_rows(rows),
            pltpu.SemaphoreType.DMA((3,)),
        ],
    )(tokens, params, grads)


def chunks_of(first, hidden, tile):
    edges = [*range(first, hidden, tile), hidden]
    return [slice(low, high) for low, high in zip(edges, edges[1:])]


def start_weights(w_in, w_out, w_in_v, w_out_v, sems, chunks):
    copies = []
    for chunk, units in enumerate(chunks):
        copies.append(
            (
                start_copy(w_in.at[:, units], w_in_v.at[:, units], sems.at[0, chunk]),
                start_copy(w_out.at[units, :], w_out_v.at[units, :], sems.at[1, chunk]),
            )
        )
    return copies


def weight_scratch(width, hidden, chunks):
    return [
        pltpu.VMEM((width, hidden), LOW),
        pltpu.VMEM((hidden, width), LOW),
        pltpu.SemaphoreType.DMA((2, len(chunks))),
    ]


def fetch_kernel(after, w_in, w_out, first_in, first_out, sems):
    del after
    units = slice(0, first_out.shape[0])
    copies = (
        start_copy(w_in.at[:, units], first_in, sems.at[0]),
        start_copy(w_out.at[units, :], first_out, sems.at[1]),
    )
    for copy in copies:
        copy.wait()


def fetch_first(after, w_in, w_out, count):
    width = w_in.shape[0]
    return call(
        fetch_kernel,
        "fetch_first",
        SHARED,
        0,
        8 * count * width,
        out_shape=(shaped((width, count), LOW), shaped((count, width), LOW)),
        in_specs=[PLACE] * 3,
        out_specs=(WHOLE,) * 2,
        scratch_shapes=[pltpu.SemaphoreType.DMA((2,))],
    )(after, w_in, w_out)


def expert_kernel(
    chunks, rows, first_in, first_out, w_in, w_out, back, acts, hidden, mark,
    w_in_v, w_out_v, sems, wide,
):
    del mark
    copies = start_weights(w_in, w_out, w_in_v, w_out_v, sems, chunks)
    count = rows.shape[0] // KINDS
    load_rows(wide, rows[...])
    rows_in = take(wide, 0, count, KINDS).astype(LOW)
    rows_grad = take(wide, 1, count, KINDS).astype(LOW)

    def first_products(weight_in, weight_out):
        return dot(rows_in, weight_in, 1, 0), dot(rows_grad, weight_out, 1, 1)

    def second_products(held, weight_in, weight_out):
        return dot(held[0], weight_out, 1, 0), dot(held[1], weight_in, 1, 1)

    def hold(preact, d_acts, units):
        values, slope = gelu_parts(preact)
        held = (values.astype(LOW), (d_acts * slope).astype(LOW))
        acts[:, units], hidden[:, units] = held
        return held

    held = hold(
        *first_products(first_in[...], first_out[...]), slice(0, first_out.shape[0])
    )
    out, d_in = second_products(held, first_in[...], first_out[...])
    before = None
    for pair, units in zip([*copies, None], [*chunks, None]):
        if pair is not None:
            for copy in pair:
                copy.wait()
            products = first_products(w_in_v[:, units], w_out_v[units, :])
        if before is not None:
            parts = second_products(held, w_in_v[:, before], w_out_v[before, :])
            out, d_in = out + parts[0], d_in + parts[1]
        if pair is not None:
            held = hold(*products, units)
        before = units
    put(wide, 0, count, KINDS, out)
    put(wide, 1, count, KINDS, d_in)
    back[...] = packed(wide)


def expert(rows, first_in, first_out, w_in, w_out, tile):
    total, width = rows.shape
    hidden = w_in.shape[1]
    count = total // KINDS
    kept = shaped((count, hidden), LOW)
    chunks = chunks_of(first_out.shape[0], hidden, tile)
    return call(
        functools.partial(expert_kernel, chunks),
        "expert_rows",
        50 * 1024 * 1024,
        8 * count * hidden * width,
        4 * hidden * width,
        count * hidden,
        out_shape=(shaped(rows.shape, LOW), kept, kept, MARK),
        in_specs=[WHOLE, WHOLE, WHOLE, PLACE, PLACE],
        out_specs=(WHOLE, WHOLE, WHOLE, PLACE),
        scratch_shapes=[*weight_scratch(width, hidden, chunks), scratch_rows(rows.shape)],
    )(rows, first_in, first_out, w_in, w_out)


def others_kernel(
    chunks, after, rows, w_in, w_out, acts, hidden, mark, w_in_v, w_out_v, sems, wide
):
    del after, mark
    copies = start_weights(w_in, w_out, w_in_v, w_out_v, sems, chunks)
    count = rows.shape[0] // KINDS
    load_rows(wide, rows[...])
    rows_in = take(wide, 0, count, KINDS).astype(LOW)
    rows_grad = take(wide, 1, count, KINDS).astype(LOW)
    for pair, units in zip(copies, chunks):
        for copy in pair:
            copy.wait()
        values, slope = gelu_parts(dot(rows_in, w_in_v[:, units], 1, 0))
        acts[:, units] = values.astype(LOW)
        d_acts = dot(rows_grad, w_out_v[units, :], 1, 1)
        hidden[:, units] = (d_acts * slope).astype(LOW)


def others_hidden(after, rows, w_in, w_out, tile):
    total, width = rows.shape
    hidden = w_in.shape[1]
    count = total // KINDS
    kept = shaped((count, hidden), LOW)
    chunks = chunks_of(0, hidden, tile)
    return call(
        functools.partial(others_kernel, chunks),
        "others_hidden",
        SHARED,
        64 * count * hidden * width,
        32 * hidden * width,
        count * hidden,
        out_shape=(kept, kept, MARK),
        in_specs=[PLACE, WHOLE, PLACE, PLACE],
        out_specs=(WHOLE, WHOLE, PLACE),
        scratch_shapes=[*weight_scratch(width, hidden, chunks), scratch_rows(rows.shape)],
    )(after, rows, w_in, w_out)


def grad_in_kernel(mine, rows, other_rows, hidden, other_hidden, grad, mark, wide, turned):
    del mark
    count = rows.shape[0] // KINDS

    @pl.when(pl.program_id(0) == 0)
    def _():
        left = []
        tiles = turned.shape[0] // LANES
        for source in (rows, other_rows):
            load_rows(wide, source[...])
            left.append(take(wide, 0, count, KINDS, mine[0] * tiles, tiles))
        turned[...] = jnp.concatenate(left, axis=0).T.astype(LOW)

    all_hidden = jnp.concatenate([hidden[...], other_hidden[...]], axis=0)
    grad[...] = dot(turned[...], all_hidden, 1, 0).astype(LOW)


def grad_expert_in(mine, rows, hidden, steps, replicas):
    total, width = rows[0].shape
    size = hidden[0].shape[1]
    count = total // KINDS
    whole_rows = pl.BlockSpec((total, width), lambda i, mine: (0, 0))
    units = pl.BlockSpec((count, size // steps), lambda i, mine: (0, i))
    return call(
        grad_in_kernel,
        "grad_expert_in",
        SHARED,
        4 * count * size * width // replicas,
        2 * size * width // replicas,
        grid_spec=pltpu.PrefetchScalarGridSpec(
            num_scalar_prefetch=1,
            grid=(steps,),
            in_specs=[whole_rows] * 2 + [units] * 2,
            out_specs=(
                pl.BlockSpec((width // replicas, size // steps), lambda i, mine: (0, i)),
                PLACE,
            ),
            scratch_shapes=[
                scratch_rows((total, width)),
                pltpu.VMEM((width // replicas, 2 * count), LOW),
            ],
        ),
        out_shape=(shaped((width // replicas, size), LOW), MARK),
    )(mine, *rows, *hidden)


def grad_out_kernel(mine, after, rows, other_rows, acts, other_acts, grad, wide, grads):
    del mine, after
    count = rows.shape[0] // KINDS

    @pl.when(pl.program_id(0) == 0)
    def _():
        right = []
        for source in (rows, other_rows):
            load_rows(wide, source[...])
            right.append(take(wide, 1, count, KINDS))
        grads[...] = jnp.concatenate(right, axis=0).astype(LOW)

    all_acts = jnp.concatenate([acts[...], other_acts[...]], axis=0)
    grad[...] = dot(all_acts, grads[...], 0, 0).astype(LOW)


def grad_expert_out(mine, after, rows, acts, steps, replicas):
    total, width = rows[0].shape
    size = acts[0].shape[1] // replicas
    count = total // KINDS
    whole_rows = pl.BlockSpec((total, width), lambda i, mine: (0, 0))
    units = pl.BlockSpec((count, size // steps), lambda i, mine: (0, mine[0] * steps + i))
    return call(
        grad_out_kernel,
        "grad_expert_out",
        SHARED,
        4 * count * size * width,
        2 * size * width,
        grid_spec=pltpu.PrefetchScalarGridSpec(
            num_scalar_prefetch=1,
            grid=(steps,),
            in_specs=[PLACE] + [whole_rows] * 2 + [units] * 2,
            out_specs=pl.BlockSpec((size // steps, width), lambda i, mine: (i, 0)),
            scratch_shapes=[
                scratch_rows((total, width)),
                pltpu.VMEM((2 * count, width), LOW),
            ],
        ),
        out_shape=shaped((size, width), LOW),
    )(mine, after, *rows, *acts)


def logits_kernel(
    after, back, tokens, params, grads, dispatch, combine, left, right, local, mark,
    tokens_v, grads_v, wide, sems,
):
    del after, mark
    images, slots, _ = dispatch.shape
    halves = start_halves(tokens, tokens_v, sems)
    grads_copy = start_copy(grads, grads_v, sems.at[2])
    load_rows(wide, back[...])
    stride = KINDS * images
    d_slot_in = []
    for image in range(images):
        d_slot_in.append(take(wide, KINDS * image + 1, slots, stride).astype(LOW))
        right[image, :slots, :] = d_slot_in[image]
        right[image, slots:, :] = params[...]
        left[image, :slots, :] = dispatch[image].astype(LOW)
    parts = []
    for copy, half in halves:
        copy.wait()
        for image in half:
            weights = dispatch[image]
            d_dispatch = dot(d_slot_in[image], tokens_v[image], 1, 1)
            parts.append(
                weights * (d_dispatch - jnp.sum(weights * d_dispatch, axis=1, keepdims=True))
            )
    grads_copy.wait()
    total = None
    for image in range(images):
        slot_out = take(wide, KINDS * image, slots, stride).astype(LOW)
        weights = combine[image]
        d_combine = dot(slot_out, grads_v[image], 1, 1)
        d_logits = parts[image] + weights * (
            d_combine - jnp.sum(weights * d_combine, axis=0, keepdims=True)
        )
        low = d_logits.astype(LOW)
        left[image, slots:, :] = low
        part = dot(low, tokens_v[image], 1, 0)
        total = part if image == 0 else total + part
    local[...] = total.astype(LOW)


def logits_grads(after, back, tokens, params, grads, dispatch, combine):
    images, length, width = tokens.shape
    slots = params.shape[0]
    return call(
        logits_kernel,
        "logits_grads",
        SHARED,
        6 * images * slots * length * width,
        4 * images * length * width,
        out_shape=(
            shaped((images, 2 * slots, length), LOW),
            shaped((images, 2 * slots, width), LOW),
            shaped(params.shape, LOW),
            MARK,
        ),
        in_specs=[PLACE, WHOLE, PLACE, WHOLE, PLACE, WHOLE, WHOLE],
        out_specs=(WHOLE, WHOLE, WHOLE, PLACE),
        scratch_shapes=[
            pltpu.VMEM(tokens.shape, LOW),
            pltpu.VMEM(grads.shape, LOW),
            scratch_rows(back.shape),
            pltpu.SemaphoreType.DMA((3,)),
        ],
    )(after, back, tokens, params, grads, dispatch, combine)


def tokens_kernel(after, left, right, out):
    del after
    out[0] = dot(left[0], right[0], 0, 0).astype(LOW)


def tokens_grads(after, left, right):
    images, deep, length = left.shape
    width = right.shape[2]
    return call(
        tokens_kernel,
        "tokens_grads",
        SHARED,
        2 * images * deep * length * width,
        2 * images * length * width,
        grid=(images,),
        out_shape=shaped((images, length, width), LOW),
        in_specs=[
            PLACE,
            pl.BlockSpec((1, deep, length), lambda i: (i, 0, 0)),
            pl.BlockSpec((1, deep, width), lambda i: (i, 0, 0)),
        ],
        out_specs=pl.BlockSpec((1, length, width), lambda i: (i, 0, 0)),
    )(after, left, right)


def exchange(rows, axes):
    return lax.all_to_all(rows, axes, split_axis=0, concat_axis=0, tiled=True)


def body(tokens, slot_params, expert_in, expert_out, grad_out):
    params = slot_params.T
    weights = (expert_in[0], expert_out[0])
    replicas = lax.axis_size("rep")
    mine = lax.axis_index("rep").astype(jnp.int32).reshape(1)

    sent, dispatch, combine, after_gather = gather(tokens, params, grad_out)
    rows = exchange(sent, "exp")
    first = fetch_first(after_gather, *weights, 256)
    other_rows = lax.ppermute(rows, "rep", [(i, (i + 1) % replicas) for i in range(replicas)])
    back, acts, hidden, after_expert = expert(rows, *first, *weights, 512)
    back = exchange(back, "exp")
    other_acts, other_hidden, _ = others_hidden(after_expert, other_rows, *weights, 512)
    grad_in, after_grad = grad_expert_in(
        mine, (rows, other_rows), (hidden, other_hidden), 5, replicas
    )
    left, right, local, after_logits = logits_grads(
        after_grad, back, tokens, params, grad_out, dispatch, combine
    )
    grad_params = lax.psum(local, ("rep", "exp")).astype(WIDE).T
    grad_outer = grad_expert_out(
        mine, after_logits, (rows, other_rows), (acts, other_acts), 5, replicas
    )
    grad_tokens = tokens_grads(after_logits, left, right)
    return (grad_tokens, grad_params, grad_in[None], grad_outer[None])


def solution(mesh):
    in_specs = (
        P(("rep", "exp"), None, None),
        P(),
        P("exp", None, None),
        P("exp", None, None),
        P(("rep", "exp"), None, None),
    )
    out_specs = (P(("rep", "exp"), None, None), P(), P("exp", "rep", None), P("exp", "rep", None))
    return jax.shard_map(body, mesh=mesh, in_specs=in_specs, out_specs=out_specs, check_vma=False)
```

```python
import functools
import math

import jax
import jax.numpy as jnp
from jax import lax
from jax.experimental import pallas as pl
from jax.experimental.pallas import tpu as pltpu
from jax.sharding import PartitionSpec as P

GELU_C = math.sqrt(2.0 / math.pi)
CUBIC = 0.044715
LOW = jnp.bfloat16
WIDE = jnp.float32
LANES = 128
KINDS = 2
SHARED = 52 * 1024 * 1024
WHOLE = pl.BlockSpec(memory_space=pltpu.VMEM)
PLACE = pl.BlockSpec(memory_space=pl.ANY)


def call(kernel, name, grant, flops, nbytes, exps=0, **kwargs):
    return pl.pallas_call(
        kernel,
        name=name,
        compiler_params=pltpu.CompilerParams(vmem_limit_bytes=grant),
        cost_estimate=pl.CostEstimate(
            flops=flops, bytes_accessed=nbytes, transcendentals=exps
        ),
        **kwargs,
    )


def shaped(shape, dtype):
    return jax.ShapeDtypeStruct(shape, dtype)


MARK = shaped((8, LANES), WIDE)


def gelu_parts(values):
    square = values * values
    tangent = jnp.tanh(GELU_C * (values + CUBIC * square * values))
    half = 0.5 * (1.0 + tangent)
    slope = half + 0.5 * values * (1.0 - tangent * tangent) * GELU_C * (1.0 + 3.0 * CUBIC * square)
    return values * half, slope


def dot(left, right, over_left, over_right):
    return lax.dot_general(
        left, right, (((over_left,), (over_right,)), ((), ())), preferred_element_type=WIDE
    )


def softmax(values, axis):
    raised = jnp.exp(values - jnp.max(values, axis=axis, keepdims=True))
    return raised / jnp.sum(raised, axis=axis, keepdims=True)


def scratch_rows(shape):
    return pltpu.VMEM((shape[1] // LANES, shape[0], LANES), WIDE)


def load_rows(ref, array):
    for tile in range(ref.shape[0]):
        ref[tile] = array[:, tile * LANES : (tile + 1) * LANES].astype(WIDE)


def packed(ref):
    return jnp.concatenate([ref[tile] for tile in range(ref.shape[0])], axis=1).astype(LOW)


def take(ref, start, count, stride, first=0, tiles=None):
    tiles = ref.shape[0] if tiles is None else tiles
    picked = [ref[first + tile, pl.ds(start, count, stride=stride), :] for tile in range(tiles)]
    return jnp.concatenate(picked, axis=1)


def put(ref, start, count, stride, array):
    for tile in range(ref.shape[0]):
        ref[tile, pl.ds(start, count, stride=stride), :] = array[
            :, tile * LANES : (tile + 1) * LANES
        ]


def start_copy(source, target, sem):
    copy = pltpu.make_async_copy(source, target, sem)
    copy.start()
    return copy


def start_halves(source, target, sems):
    images = source.shape[0]
    parts = []
    for index, (first, last) in enumerate(((0, images // 2), (images // 2, images))):
        part = pl.ds(first, last - first)
        copy = start_copy(source.at[part], target.at[part], sems.at[index])
        parts.append((copy, range(first, last)))
    return parts


def gather_kernel(
    tokens, params, grads, sent, dispatch, combine, tokens_v, grads_v, rows, sems
):
    images = tokens.shape[0]
    slots = params.shape[0]
    stride = KINDS * images
    halves = start_halves(tokens, tokens_v, sems)
    grads_copy = start_copy(grads, grads_v, sems.at[2])
    logits = []
    for copy, half in halves:
        copy.wait()
        logits += [dot(params[...], tokens_v[image], 1, 1) for image in half]
    over_slots = []
    for image in range(images):
        over_tokens = softmax(logits[image], 1)
        dispatch[image] = over_tokens
        put(
            rows, KINDS * image, slots, stride, dot(over_tokens.astype(LOW), tokens_v[image], 1, 0)
        )
        over_slots.append(softmax(logits[image], 0))
        combine[image] = over_slots[image]
    grads_copy.wait()
    for image in range(images):
        value = dot(over_slots[image].astype(LOW), grads_v[image], 1, 0)
        put(rows, KINDS * image + 1, slots, stride, value)
    sent[...] = packed(rows)


def gather(tokens, params, grads):
    images, length, width = tokens.shape
    slots = params.shape[0]
    weights = shaped((images, slots, length), WIDE)
    rows = (slots * images * KINDS, width)
    return call(
        gather_kernel,
        "gather_slots",
        SHARED,
        6 * images * slots * length * width,
        4 * images * length * width,
        2 * images * slots * length,
        out_shape=(shaped(rows, LOW), weights, weights),
        in_specs=[PLACE, WHOLE, PLACE],
        out_specs=(WHOLE, WHOLE, WHOLE),
        scratch_shapes=[
            pltpu.VMEM(tokens.shape, LOW),
            pltpu.VMEM(grads.shape, LOW),
            scratch_rows(rows),
            pltpu.SemaphoreType.DMA((3,)),
        ],
    )(tokens, params, grads)


def chunks_of(first, hidden, tile):
    edges = [*range(first, hidden, tile), hidden]
    return [slice(low, high) for low, high in zip(edges, edges[1:])]


def start_weights(w_in, w_out, w_in_v, w_out_v, sems, chunks):
    copies = []
    for chunk, units in enumerate(chunks):
        copies.append(
            (
                start_copy(w_in.at[:, units], w_in_v.at[:, units], sems.at[0, chunk]),
                start_copy(w_out.at[units, :], w_out_v.at[units, :], sems.at[1, chunk]),
            )
        )
    return copies


def weight_scratch(width, hidden, chunks):
    return [
        pltpu.VMEM((width, hidden), LOW),
        pltpu.VMEM((hidden, width), LOW),
        pltpu.SemaphoreType.DMA((2, len(chunks))),
    ]


def expert_kernel(
    chunks, rows, w_in, w_out, back, acts, hidden, mark, w_in_v, w_out_v, sems, wide
):
    del mark
    copies = start_weights(w_in, w_out, w_in_v, w_out_v, sems, chunks)
    count = rows.shape[0] // KINDS
    load_rows(wide, rows[...])
    rows_in = take(wide, 0, count, KINDS).astype(LOW)
    rows_grad = take(wide, 1, count, KINDS).astype(LOW)
    out = d_in = held = before = None
    for pair, units in zip([*copies, None], [*chunks, None]):
        if pair is not None:
            for copy in pair:
                copy.wait()
            preact = dot(rows_in, w_in_v[:, units], 1, 0)
            d_acts = dot(rows_grad, w_out_v[units, :], 1, 1)
        if before is not None:
            out_part = dot(held[0], w_out_v[before, :], 1, 0)
            d_in_part = dot(held[1], w_in_v[:, before], 1, 1)
            out = out_part if out is None else out + out_part
            d_in = d_in_part if d_in is None else d_in + d_in_part
        if pair is not None:
            values, slope = gelu_parts(preact)
            held = (values.astype(LOW), (d_acts * slope).astype(LOW))
            acts[:, units], hidden[:, units] = held
        before = units
    put(wide, 0, count, KINDS, out)
    put(wide, 1, count, KINDS, d_in)
    back[...] = packed(wide)


def expert(rows, w_in, w_out, tile):
    total, width = rows.shape
    hidden = w_in.shape[1]
    count = total // KINDS
    kept = shaped((count, hidden), LOW)
    chunks = chunks_of(0, hidden, tile)
    return call(
        functools.partial(expert_kernel, chunks),
        "expert_rows",
        SHARED,
        8 * count * hidden * width,
        4 * hidden * width,
        count * hidden,
        out_shape=(shaped(rows.shape, LOW), kept, kept, MARK),
        in_specs=[WHOLE, PLACE, PLACE],
        out_specs=(WHOLE, WHOLE, WHOLE, PLACE),
        scratch_shapes=[*weight_scratch(width, hidden, chunks), scratch_rows(rows.shape)],
    )(rows, w_in, w_out)


def others_kernel(
    chunks, after, rows, w_in, w_out, acts, hidden, mark, w_in_v, w_out_v, sems, wide
):
    del after, mark
    copies = start_weights(w_in, w_out, w_in_v, w_out_v, sems, chunks)
    count = rows.shape[0] // KINDS
    load_rows(wide, rows[...])
    rows_in = take(wide, 0, count, KINDS).astype(LOW)
    rows_grad = take(wide, 1, count, KINDS).astype(LOW)
    for pair, units in zip(copies, chunks):
        for copy in pair:
            copy.wait()
        values, slope = gelu_parts(dot(rows_in, w_in_v[:, units], 1, 0))
        acts[:, units] = values.astype(LOW)
        d_acts = dot(rows_grad, w_out_v[units, :], 1, 1)
        hidden[:, units] = (d_acts * slope).astype(LOW)


def others_hidden(after, rows, w_in, w_out, tile):
    total, width = rows.shape
    hidden = w_in.shape[1]
    count = total // KINDS
    kept = shaped((count, hidden), LOW)
    chunks = chunks_of(0, hidden, tile)
    return call(
        functools.partial(others_kernel, chunks),
        "others_hidden",
        SHARED,
        64 * count * hidden * width,
        32 * hidden * width,
        count * hidden,
        out_shape=(kept, kept, MARK),
        in_specs=[PLACE, WHOLE, PLACE, PLACE],
        out_specs=(WHOLE, WHOLE, PLACE),
        scratch_shapes=[*weight_scratch(width, hidden, chunks), scratch_rows(rows.shape)],
    )(after, rows, w_in, w_out)


def weights_kernel(
    mine, after, rows, other_rows, acts, other_acts, hidden, other_hidden, grad_in, grad_out, mark,
    wide, grads, turned,
):
    del after, mark
    count = rows.shape[0] // KINDS

    @pl.when(pl.program_id(0) == 0)
    def _():
        left, right = [], []
        tiles = turned.shape[0] // LANES
        for source in (rows, other_rows):
            load_rows(wide, source[...])
            left.append(take(wide, 0, count, KINDS, mine[0] * tiles, tiles))
            right.append(take(wide, 1, count, KINDS))
        turned[...] = jnp.concatenate(left, axis=0).T.astype(LOW)
        grads[...] = jnp.concatenate(right, axis=0).astype(LOW)

    all_hidden = jnp.concatenate([hidden[...], other_hidden[...]], axis=0)
    grad_in[...] = dot(turned[...], all_hidden, 1, 0).astype(LOW)
    all_acts = jnp.concatenate([acts[...], other_acts[...]], axis=0)
    grad_out[...] = dot(all_acts, grads[...], 0, 0).astype(LOW)


def weight_grads(mine, after, rows, acts, hidden, steps, replicas):
    total, width = rows[0].shape
    size = acts[0].shape[1]
    count = total // KINDS
    in_tile, out_tile = size // steps, size // replicas // steps
    whole_rows = pl.BlockSpec((total, width), lambda i, mine: (0, 0))
    acts_spec = pl.BlockSpec((count, out_tile), lambda i, mine: (0, mine[0] * steps + i))
    hidden_spec = pl.BlockSpec((count, in_tile), lambda i, mine: (0, i))
    return call(
        weights_kernel,
        "weight_grads",
        SHARED,
        8 * count * size * width // replicas,
        4 * size * width // replicas,
        grid_spec=pltpu.PrefetchScalarGridSpec(
            num_scalar_prefetch=1,
            grid=(steps,),
            in_specs=[PLACE] + [whole_rows] * 2 + [acts_spec] * 2 + [hidden_spec] * 2,
            out_specs=(
                pl.BlockSpec((width // replicas, in_tile), lambda i, mine: (0, i)),
                pl.BlockSpec((out_tile, width), lambda i, mine: (i, 0)),
                PLACE,
            ),
            scratch_shapes=[
                scratch_rows((total, width)),
                pltpu.VMEM((2 * count, width), LOW),
                pltpu.VMEM((width // replicas, 2 * count), LOW),
            ],
        ),
        out_shape=(
            shaped((width // replicas, size), LOW),
            shaped((size // replicas, width), LOW),
            MARK,
        ),
    )(mine, after, *rows, *acts, *hidden)


def logits_kernel(
    after, back, tokens, params, grads, dispatch, combine, left, right, local, mark,
    tokens_v, grads_v, wide, sems,
):
    del after, mark
    images, slots, _ = dispatch.shape
    halves = start_halves(tokens, tokens_v, sems)
    grads_copy = start_copy(grads, grads_v, sems.at[2])
    load_rows(wide, back[...])
    stride = KINDS * images
    d_slot_in = []
    for image in range(images):
        d_slot_in.append(take(wide, KINDS * image + 1, slots, stride).astype(LOW))
        right[image, :slots, :] = d_slot_in[image]
        right[image, slots:, :] = params[...]
        left[image, :slots, :] = dispatch[image].astype(LOW)
    parts = []
    for copy, half in halves:
        copy.wait()
        for image in half:
            weights = dispatch[image]
            d_dispatch = dot(d_slot_in[image], tokens_v[image], 1, 1)
            parts.append(
                weights * (d_dispatch - jnp.sum(weights * d_dispatch, axis=1, keepdims=True))
            )
    grads_copy.wait()
    total = None
    for image in range(images):
        slot_out = take(wide, KINDS * image, slots, stride).astype(LOW)
        weights = combine[image]
        d_combine = dot(slot_out, grads_v[image], 1, 1)
        d_logits = parts[image] + weights * (
            d_combine - jnp.sum(weights * d_combine, axis=0, keepdims=True)
        )
        low = d_logits.astype(LOW)
        left[image, slots:, :] = low
        part = dot(low, tokens_v[image], 1, 0)
        total = part if image == 0 else total + part
    local[...] = total.astype(LOW)


def logits_grads(after, back, tokens, params, grads, dispatch, combine):
    images, length, width = tokens.shape
    slots = params.shape[0]
    return call(
        logits_kernel,
        "logits_grads",
        SHARED,
        6 * images * slots * length * width,
        4 * images * length * width,
        out_shape=(
            shaped((images, 2 * slots, length), LOW),
            shaped((images, 2 * slots, width), LOW),
            shaped(params.shape, LOW),
            MARK,
        ),
        in_specs=[PLACE, WHOLE, PLACE, WHOLE, PLACE, WHOLE, WHOLE],
        out_specs=(WHOLE, WHOLE, WHOLE, PLACE),
        scratch_shapes=[
            pltpu.VMEM(tokens.shape, LOW),
            pltpu.VMEM(grads.shape, LOW),
            scratch_rows(back.shape),
            pltpu.SemaphoreType.DMA((3,)),
        ],
    )(after, back, tokens, params, grads, dispatch, combine)


def tokens_kernel(after, left, right, out, mark):
    del after, mark
    out[0] = dot(left[0], right[0], 0, 0).astype(LOW)


def tokens_grads(after, left, right):
    images, deep, length = left.shape
    width = right.shape[2]
    return call(
        tokens_kernel,
        "tokens_grads",
        SHARED,
        2 * images * deep * length * width,
        2 * images * length * width,
        grid=(images,),
        out_shape=(shaped((images, length, width), LOW), MARK),
        in_specs=[
            PLACE,
            pl.BlockSpec((1, deep, length), lambda i: (i, 0, 0)),
            pl.BlockSpec((1, deep, width), lambda i: (i, 0, 0)),
        ],
        out_specs=(pl.BlockSpec((1, length, width), lambda i: (i, 0, 0)), PLACE),
    )(after, left, right)


def add_kernel(after, *refs):
    del after
    terms = [ref[...].astype(WIDE) for ref in refs[:-2]]
    while len(terms) > 1:
        terms = [left + right for left, right in zip(terms[::2], terms[1::2])]
    refs[-2][...] = terms[0].astype(refs[-2].dtype)


def add(after, terms, dtype):
    return call(
        add_kernel,
        "add_terms",
        SHARED,
        len(terms) * terms[0].size,
        2 * len(terms) * terms[0].size,
        out_shape=(shaped(terms[0].shape, dtype), MARK),
        in_specs=[PLACE] + [WHOLE] * len(terms),
        out_specs=(WHOLE, PLACE),
    )(after, *terms)


def terms_of_group(array, axis, distances):
    count = lax.axis_size(axis)
    return [array] + [
        lax.ppermute(array, axis, [(i, i ^ distance) for i in range(count)])
        for distance in distances
    ]


def copy_kernel(after, source, target):
    del after
    target[...] = source[...]


def copy_after(after, array):
    return call(
        copy_kernel,
        "copy_after",
        SHARED,
        0,
        4 * array.size,
        out_shape=shaped(array.shape, array.dtype),
        in_specs=[PLACE, WHOLE],
        out_specs=WHOLE,
    )(after, array)


def exchange(rows, axes):
    return lax.all_to_all(rows, axes, split_axis=0, concat_axis=0, tiled=True)


def body(tokens, slot_params, expert_in, expert_out, grad_out):
    params = slot_params.T
    weights = (expert_in[0], expert_out[0])
    replicas = lax.axis_size("rep")
    mine = lax.axis_index("rep").astype(jnp.int32).reshape(1)

    sent, dispatch, combine = gather(tokens, params, grad_out)
    rows = exchange(sent, "exp")
    back, acts, hidden, after_expert = expert(rows, *weights, 512)
    back = exchange(back, "exp")
    other_rows = lax.ppermute(
        copy_after(after_expert, rows), "rep", [(i, (i + 1) % replicas) for i in range(replicas)]
    )
    left, right, local, after = logits_grads(
        after_expert, back, tokens, params, grad_out, dispatch, combine
    )
    bits = lax.axis_size("exp").bit_length() - 1
    groups = [(1 << bit, 2 << bit, 3 << bit) for bit in range(0, bits - 1, 2)]
    if bits % 2:
        groups.append((1 << (bits - 1),))
    terms = terms_of_group(local, "exp", groups[0])
    grad_tokens, after = tokens_grads(after, left, right)
    local, after = add(after, terms, LOW)
    terms = terms_of_group(local, "exp", groups[1])
    other_acts, other_hidden, after = others_hidden(after, other_rows, *weights, 512)
    local, after = add(after, terms, LOW)
    for distances in groups[2:]:
        local, after = add(after, terms_of_group(local, "exp", distances), LOW)
    terms = terms_of_group(local, "rep", (1,))
    grad_expert_in, grad_expert_out, after = weight_grads(
        mine,
        after,
        (rows, other_rows),
        (acts, other_acts),
        (hidden, other_hidden),
        5,
        replicas,
    )
    grad_params, _ = add(after, terms, WIDE)
    return (grad_tokens, grad_params.T, grad_expert_in[None], grad_expert_out[None])


def solution(mesh):
    in_specs = (
        P(("rep", "exp"), None, None),
        P(),
        P("exp", None, None),
        P("exp", None, None),
        P(("rep", "exp"), None, None),
    )
    out_specs = (P(("rep", "exp"), None, None), P(), P("exp", "rep", None), P("exp", "rep", None))
    return jax.shard_map(body, mesh=mesh, in_specs=in_specs, out_specs=out_specs, check_vma=False)
```

```python
import functools
import math

import jax
import jax.numpy as jnp
from jax import lax
from jax.experimental import pallas as pl
from jax.experimental.pallas import tpu as pltpu
from jax.sharding import PartitionSpec as P

GELU_C = math.sqrt(2.0 / math.pi)
CUBIC = 0.044715
LOW = jnp.bfloat16
WIDE = jnp.float32
LANES = 128
KINDS = 2
SHARED = 52 * 1024 * 1024
WHOLE = pl.BlockSpec(memory_space=pltpu.VMEM)
PLACE = pl.BlockSpec(memory_space=pl.ANY)


def call(kernel, name, grant, flops, nbytes, exps=0, **kwargs):
    return pl.pallas_call(
        kernel,
        name=name,
        compiler_params=pltpu.CompilerParams(vmem_limit_bytes=grant),
        cost_estimate=pl.CostEstimate(
            flops=flops, bytes_accessed=nbytes, transcendentals=exps
        ),
        **kwargs,
    )


def shaped(shape, dtype):
    return jax.ShapeDtypeStruct(shape, dtype)


MARK = shaped((8, LANES), WIDE)


def gelu_parts(values):
    square = values * values
    tangent = jnp.tanh(GELU_C * (values + CUBIC * square * values))
    half = 0.5 * (1.0 + tangent)
    slope = half + 0.5 * values * (1.0 - tangent * tangent) * GELU_C * (1.0 + 3.0 * CUBIC * square)
    return values * half, slope


def dot(left, right, over_left, over_right):
    return lax.dot_general(
        left, right, (((over_left,), (over_right,)), ((), ())), preferred_element_type=WIDE
    )


def softmax(values, axis):
    raised = jnp.exp(values - jnp.max(values, axis=axis, keepdims=True))
    return raised / jnp.sum(raised, axis=axis, keepdims=True)


def scratch_rows(shape):
    return pltpu.VMEM((shape[1] // LANES, shape[0], LANES), WIDE)


def load_rows(ref, array):
    for tile in range(ref.shape[0]):
        ref[tile] = array[:, tile * LANES : (tile + 1) * LANES].astype(WIDE)


def packed(ref):
    return jnp.concatenate([ref[tile] for tile in range(ref.shape[0])], axis=1).astype(LOW)


def take(ref, start, count, stride, first=0, tiles=None):
    tiles = ref.shape[0] if tiles is None else tiles
    picked = [ref[first + tile, pl.ds(start, count, stride=stride), :] for tile in range(tiles)]
    return jnp.concatenate(picked, axis=1)


def put(ref, start, count, stride, array):
    for tile in range(ref.shape[0]):
        ref[tile, pl.ds(start, count, stride=stride), :] = array[
            :, tile * LANES : (tile + 1) * LANES
        ]


def start_copy(source, target, sem):
    copy = pltpu.make_async_copy(source, target, sem)
    copy.start()
    return copy


def start_halves(source, target, sems):
    images = source.shape[0]
    parts = []
    for index, (first, last) in enumerate(((0, images // 2), (images // 2, images))):
        part = pl.ds(first, last - first)
        copy = start_copy(source.at[part], target.at[part], sems.at[index])
        parts.append((copy, range(first, last)))
    return parts


def gather_kernel(
    tokens, params, grads, sent, dispatch, combine, tokens_v, grads_v, rows, sems
):
    images = tokens.shape[0]
    slots = params.shape[0]
    stride = KINDS * images
    halves = start_halves(tokens, tokens_v, sems)
    grads_copy = start_copy(grads, grads_v, sems.at[2])
    logits = []
    for copy, half in halves:
        copy.wait()
        logits += [dot(params[...], tokens_v[image], 1, 1) for image in half]
    over_slots = []
    for image in range(images):
        over_tokens = softmax(logits[image], 1)
        dispatch[image] = over_tokens
        put(
            rows, KINDS * image, slots, stride, dot(over_tokens.astype(LOW), tokens_v[image], 1, 0)
        )
        over_slots.append(softmax(logits[image], 0))
        combine[image] = over_slots[image]
    grads_copy.wait()
    for image in range(images):
        value = dot(over_slots[image].astype(LOW), grads_v[image], 1, 0)
        put(rows, KINDS * image + 1, slots, stride, value)
    sent[...] = packed(rows)


def gather(tokens, params, grads):
    images, length, width = tokens.shape
    slots = params.shape[0]
    weights = shaped((images, slots, length), WIDE)
    rows = (slots * images * KINDS, width)
    return call(
        gather_kernel,
        "gather_slots",
        SHARED,
        6 * images * slots * length * width,
        4 * images * length * width,
        2 * images * slots * length,
        out_shape=(shaped(rows, LOW), weights, weights),
        in_specs=[PLACE, WHOLE, PLACE],
        out_specs=(WHOLE, WHOLE, WHOLE),
        scratch_shapes=[
            pltpu.VMEM(tokens.shape, LOW),
            pltpu.VMEM(grads.shape, LOW),
            scratch_rows(rows),
            pltpu.SemaphoreType.DMA((3,)),
        ],
    )(tokens, params, grads)


def chunks_of(first, hidden, tile):
    edges = [*range(first, hidden, tile), hidden]
    return [slice(low, high) for low, high in zip(edges, edges[1:])]


def start_weights(w_in, w_out, w_in_v, w_out_v, sems, chunks):
    copies = []
    for chunk, units in enumerate(chunks):
        copies.append(
            (
                start_copy(w_in.at[:, units], w_in_v.at[:, units], sems.at[0, chunk]),
                start_copy(w_out.at[units, :], w_out_v.at[units, :], sems.at[1, chunk]),
            )
        )
    return copies


def weight_scratch(width, hidden, chunks):
    return [
        pltpu.VMEM((width, hidden), LOW),
        pltpu.VMEM((hidden, width), LOW),
        pltpu.SemaphoreType.DMA((2, len(chunks))),
    ]


def expert_kernel(
    chunks, rows, w_in, w_out, back, acts, hidden, mark, w_in_v, w_out_v, sems, wide
):
    del mark
    copies = start_weights(w_in, w_out, w_in_v, w_out_v, sems, chunks)
    count = rows.shape[0] // KINDS
    load_rows(wide, rows[...])
    rows_in = take(wide, 0, count, KINDS).astype(LOW)
    rows_grad = take(wide, 1, count, KINDS).astype(LOW)
    out = d_in = held = before = None
    for pair, units in zip([*copies, None], [*chunks, None]):
        if pair is not None:
            for copy in pair:
                copy.wait()
            preact = dot(rows_in, w_in_v[:, units], 1, 0)
            d_acts = dot(rows_grad, w_out_v[units, :], 1, 1)
        if before is not None:
            out_part = dot(held[0], w_out_v[before, :], 1, 0)
            d_in_part = dot(held[1], w_in_v[:, before], 1, 1)
            out = out_part if out is None else out + out_part
            d_in = d_in_part if d_in is None else d_in + d_in_part
        if pair is not None:
            values, slope = gelu_parts(preact)
            held = (values.astype(LOW), (d_acts * slope).astype(LOW))
            acts[:, units], hidden[:, units] = held
        before = units
    put(wide, 0, count, KINDS, out)
    put(wide, 1, count, KINDS, d_in)
    back[...] = packed(wide)


def expert(rows, w_in, w_out, tile):
    total, width = rows.shape
    hidden = w_in.shape[1]
    count = total // KINDS
    kept = shaped((count, hidden), LOW)
    chunks = chunks_of(0, hidden, tile)
    return call(
        functools.partial(expert_kernel, chunks),
        "expert_rows",
        SHARED,
        8 * count * hidden * width,
        4 * hidden * width,
        count * hidden,
        out_shape=(shaped(rows.shape, LOW), kept, kept, MARK),
        in_specs=[WHOLE, PLACE, PLACE],
        out_specs=(WHOLE, WHOLE, WHOLE, PLACE),
        scratch_shapes=[*weight_scratch(width, hidden, chunks), scratch_rows(rows.shape)],
    )(rows, w_in, w_out)


def replica_kernel(
    chunks, mine, after, rows, other_rows, acts, hidden, w_in, w_out, grad_in, grad_out, mark,
    w_in_v, w_out_v, grad_in_v, grad_out_v, wide, grads, turned, sems, in_sems, out_sems,
):
    del after, mark
    count = rows.shape[0] // KINDS
    size = w_in.shape[1]
    half = grad_out.shape[0]
    spans, copies = [], []
    for chunk, units in enumerate(chunks):
        start = pl.multiple_of(lax.rem(mine[0] * half + units.start, size), LANES)
        span = pl.ds(start, units.stop - units.start)
        spans.append(span)
        copies.append(
            (
                start_copy(w_in.at[:, span], w_in_v.at[:, units], sems.at[0, chunk]),
                start_copy(w_out.at[span, :], w_out_v.at[units, :], sems.at[1, chunk]),
            )
        )
    left, right = [], []
    tiles = turned.shape[0] // LANES
    for source in (rows, other_rows):
        load_rows(wide, source[...])
        left.append(take(wide, 0, count, KINDS, mine[0] * tiles, tiles))
        right.append(take(wide, 1, count, KINDS))
    turned[...] = jnp.concatenate(left, axis=0).T.astype(LOW)
    grads[...] = jnp.concatenate(right, axis=0).astype(LOW)
    rows_in = take(wide, 0, count, KINDS).astype(LOW)
    rows_grad = right[1].astype(LOW)
    results = []
    before = None
    for chunk in range(len(chunks) + 1):
        if chunk < len(chunks):
            units = chunks[chunk]
            for copy in copies[chunk]:
                copy.wait()
            preact = dot(rows_in, w_in_v[:, units], 1, 0)
            d_acts = dot(rows_grad, w_out_v[units, :], 1, 1)
        if before is not None:
            past, span, all_acts, all_hidden = before
            grad_in_v[:, past] = dot(turned[...], all_hidden, 1, 0).astype(LOW)
            results.append(
                start_copy(grad_in_v.at[:, past], grad_in.at[:, span], in_sems.at[chunk - 1])
            )
            if past.stop <= half:
                grad_out_v[past, :] = dot(all_acts, grads[...], 0, 0).astype(LOW)
                results.append(
                    start_copy(
                        grad_out_v.at[past, :], grad_out.at[past, :], out_sems.at[chunk - 1]
                    )
                )
        if chunk < len(chunks):
            span = spans[chunk]
            values, slope = gelu_parts(preact)
            all_acts = jnp.concatenate([acts[:, span], values.astype(LOW)], axis=0)
            all_hidden = jnp.concatenate(
                [hidden[:, span], (d_acts * slope).astype(LOW)], axis=0
            )
            before = (units, span, all_acts, all_hidden)
    for copy in results:
        copy.wait()


def replica_grads(mine, after, rows, other_rows, acts, hidden, w_in, w_out, replicas, tile):
    total, width = rows.shape
    size = w_in.shape[1]
    half = size // replicas
    count = total // KINDS
    chunks = [
        slice(part * half + units.start, part * half + units.stop)
        for part in range(replicas)
        for units in chunks_of(0, half, tile)
    ]
    return call(
        functools.partial(replica_kernel, chunks),
        "replica_grads",
        SHARED,
        64 * count * size * width,
        32 * size * width,
        count * size,
        out_shape=(
            shaped((width // replicas, size), LOW),
            shaped((half, width), LOW),
            MARK,
        ),
        in_specs=[pl.BlockSpec(memory_space=pltpu.SMEM), PLACE]
        + [WHOLE] * 4
        + [PLACE] * 2,
        out_specs=(PLACE,) * 3,
        scratch_shapes=[
            *weight_scratch(width, size, chunks)[:2],
            pltpu.VMEM((width // replicas, size), LOW),
            pltpu.VMEM((half, width), LOW),
            scratch_rows((total, width)),
            pltpu.VMEM((2 * count, width), LOW),
            pltpu.VMEM((width // replicas, 2 * count), LOW),
            pltpu.SemaphoreType.DMA((2, len(chunks))),
            pltpu.SemaphoreType.DMA((len(chunks),)),
            pltpu.SemaphoreType.DMA((len(chunks),)),
        ],
    )(mine, after, rows, other_rows, acts, hidden, w_in, w_out)


def logits_kernel(
    after, back, tokens, params, grads, dispatch, combine, left, right, local, mark,
    tokens_v, grads_v, wide, sems,
):
    del after, mark
    images, slots, _ = dispatch.shape
    halves = start_halves(tokens, tokens_v, sems)
    grads_copy = start_copy(grads, grads_v, sems.at[2])
    load_rows(wide, back[...])
    stride = KINDS * images
    d_slot_in = []
    for image in range(images):
        d_slot_in.append(take(wide, KINDS * image + 1, slots, stride).astype(LOW))
        right[image, :slots, :] = d_slot_in[image]
        right[image, slots:, :] = params[...]
        left[image, :slots, :] = dispatch[image].astype(LOW)
    parts = []
    for copy, half in halves:
        copy.wait()
        for image in half:
            weights = dispatch[image]
            d_dispatch = dot(d_slot_in[image], tokens_v[image], 1, 1)
            parts.append(
                weights * (d_dispatch - jnp.sum(weights * d_dispatch, axis=1, keepdims=True))
            )
    grads_copy.wait()
    total = None
    for image in range(images):
        slot_out = take(wide, KINDS * image, slots, stride).astype(LOW)
        weights = combine[image]
        d_combine = dot(slot_out, grads_v[image], 1, 1)
        d_logits = parts[image] + weights * (
            d_combine - jnp.sum(weights * d_combine, axis=0, keepdims=True)
        )
        low = d_logits.astype(LOW)
        left[image, slots:, :] = low
        part = dot(low, tokens_v[image], 1, 0)
        total = part if image == 0 else total + part
    local[...] = total.astype(LOW)


def logits_grads(after, back, tokens, params, grads, dispatch, combine):
    images, length, width = tokens.shape
    slots = params.shape[0]
    return call(
        logits_kernel,
        "logits_grads",
        SHARED,
        6 * images * slots * length * width,
        4 * images * length * width,
        out_shape=(
            shaped((images, 2 * slots, length), LOW),
            shaped((images, 2 * slots, width), LOW),
            shaped(params.shape, LOW),
            MARK,
        ),
        in_specs=[PLACE, WHOLE, PLACE, WHOLE, PLACE, WHOLE, WHOLE],
        out_specs=(WHOLE, WHOLE, WHOLE, PLACE),
        scratch_shapes=[
            pltpu.VMEM(tokens.shape, LOW),
            pltpu.VMEM(grads.shape, LOW),
            scratch_rows(back.shape),
            pltpu.SemaphoreType.DMA((3,)),
        ],
    )(after, back, tokens, params, grads, dispatch, combine)


def tokens_kernel(after, left, right, out, mark):
    del after, mark
    out[0] = dot(left[0], right[0], 0, 0).astype(LOW)


def tokens_grads(after, left, right):
    images, deep, length = left.shape
    width = right.shape[2]
    return call(
        tokens_kernel,
        "tokens_grads",
        SHARED,
        2 * images * deep * length * width,
        2 * images * length * width,
        grid=(images,),
        out_shape=(shaped((images, length, width), LOW), MARK),
        in_specs=[
            PLACE,
            pl.BlockSpec((1, deep, length), lambda i: (i, 0, 0)),
            pl.BlockSpec((1, deep, width), lambda i: (i, 0, 0)),
        ],
        out_specs=(pl.BlockSpec((1, length, width), lambda i: (i, 0, 0)), PLACE),
    )(after, left, right)


def add_kernel(after, *refs):
    del after
    terms = [ref[...].astype(WIDE) for ref in refs[:-2]]
    while len(terms) > 1:
        terms = [left + right for left, right in zip(terms[::2], terms[1::2])]
    refs[-2][...] = terms[0].astype(refs[-2].dtype)


def add(after, terms, dtype):
    return call(
        add_kernel,
        "add_terms",
        SHARED,
        len(terms) * terms[0].size,
        2 * len(terms) * terms[0].size,
        out_shape=(shaped(terms[0].shape, dtype), MARK),
        in_specs=[PLACE] + [WHOLE] * len(terms),
        out_specs=(WHOLE, PLACE),
    )(after, *terms)


def terms_of_group(array, axis, distances):
    count = lax.axis_size(axis)
    return [array] + [
        lax.ppermute(array, axis, [(i, i ^ distance) for i in range(count)])
        for distance in distances
    ]


def exchange(rows, axes):
    return lax.all_to_all(rows, axes, split_axis=0, concat_axis=0, tiled=True)


def body(tokens, slot_params, expert_in, expert_out, grad_out):
    params = slot_params.T
    weights = (expert_in[0], expert_out[0])
    replicas = lax.axis_size("rep")
    mine = lax.axis_index("rep").astype(jnp.int32).reshape(1)

    sent, dispatch, combine = gather(tokens, params, grad_out)
    rows = exchange(sent, "exp")
    other_rows = lax.ppermute(rows, "rep", [(i, (i + 1) % replicas) for i in range(replicas)])
    back, acts, hidden, after = expert(rows, *weights, 512)
    back = exchange(back, "exp")
    grad_in, grad_outer, after = replica_grads(
        mine, after, rows, other_rows, acts, hidden, *weights, replicas, 512
    )
    left, right, local, after = logits_grads(
        after, back, tokens, params, grad_out, dispatch, combine
    )
    bits = lax.axis_size("exp").bit_length() - 1
    groups = [(1 << bit, 2 << bit, 3 << bit) for bit in range(0, bits - 1, 2)]
    if bits % 2:
        groups.append((1 << (bits - 1),))
    terms = terms_of_group(local, "exp", groups[0])
    grad_tokens, after = tokens_grads(after, left, right)
    local, after = add(after, terms, LOW)
    for distances in groups[1:]:
        local, after = add(after, terms_of_group(local, "exp", distances), LOW)
    grad_params, _ = add(after, terms_of_group(local, "rep", (1,)), WIDE)
    return (grad_tokens, grad_params.T, grad_in[None], grad_outer[None])


def solution(mesh):
    in_specs = (
        P(("rep", "exp"), None, None),
        P(),
        P("exp", None, None),
        P("exp", None, None),
        P(("rep", "exp"), None, None),
    )
    out_specs = (P(("rep", "exp"), None, None), P(), P("exp", "rep", None), P("exp", "rep", None))
    return jax.shard_map(body, mesh=mesh, in_specs=in_specs, out_specs=out_specs, check_vma=False)
```

```python
import functools
import math

import jax
import jax.numpy as jnp
from jax import lax
from jax.experimental import pallas as pl
from jax.experimental.pallas import tpu as pltpu
from jax.sharding import PartitionSpec as P

GELU_C = math.sqrt(2.0 / math.pi)
CUBIC = 0.044715
LOW = jnp.bfloat16
WIDE = jnp.float32
LANES = 128
KINDS = 2
SHARED = 52 * 1024 * 1024
ROOMY = 50 * 1024 * 1024
WHOLE = pl.BlockSpec(memory_space=pltpu.VMEM)
PLACE = pl.BlockSpec(memory_space=pl.ANY)


def call(kernel, name, grant, flops, nbytes, exps=0, **kwargs):
    return pl.pallas_call(
        kernel,
        name=name,
        compiler_params=pltpu.CompilerParams(vmem_limit_bytes=grant),
        cost_estimate=pl.CostEstimate(
            flops=flops, bytes_accessed=nbytes, transcendentals=exps
        ),
        **kwargs,
    )


def shaped(shape, dtype):
    return jax.ShapeDtypeStruct(shape, dtype)


MARK = shaped((8, LANES), WIDE)


def gelu_parts(values):
    square = values * values
    tangent = jnp.tanh(GELU_C * (values + CUBIC * square * values))
    half = 0.5 * (1.0 + tangent)
    slope = half + 0.5 * values * (1.0 - tangent * tangent) * GELU_C * (1.0 + 3.0 * CUBIC * square)
    return values * half, slope


def dot(left, right, over_left, over_right):
    return lax.dot_general(
        left, right, (((over_left,), (over_right,)), ((), ())), preferred_element_type=WIDE
    )


def softmax(values, axis):
    raised = jnp.exp(values - jnp.max(values, axis=axis, keepdims=True))
    return raised / jnp.sum(raised, axis=axis, keepdims=True)


def scratch_rows(shape):
    return pltpu.VMEM((shape[1] // LANES, shape[0], LANES), WIDE)


def load_rows(ref, array):
    for tile in range(ref.shape[0]):
        ref[tile] = array[:, tile * LANES : (tile + 1) * LANES].astype(WIDE)


def packed(ref):
    return jnp.concatenate([ref[tile] for tile in range(ref.shape[0])], axis=1).astype(LOW)


def take(ref, start, count, stride, first=0, tiles=None):
    tiles = ref.shape[0] if tiles is None else tiles
    picked = [ref[first + tile, pl.ds(start, count, stride=stride), :] for tile in range(tiles)]
    return jnp.concatenate(picked, axis=1)


def put(ref, start, count, stride, array):
    for tile in range(ref.shape[0]):
        ref[tile, pl.ds(start, count, stride=stride), :] = array[
            :, tile * LANES : (tile + 1) * LANES
        ]


def start_copy(source, target, sem):
    copy = pltpu.make_async_copy(source, target, sem)
    copy.start()
    return copy


def start_halves(source, target, sems):
    images = source.shape[0]
    parts = []
    for index, (first, last) in enumerate(((0, images // 2), (images // 2, images))):
        part = pl.ds(first, last - first)
        copy = start_copy(source.at[part], target.at[part], sems.at[index])
        parts.append((copy, range(first, last)))
    return parts


def gather_kernel(
    tokens, params, grads, w_in, w_out, sent, dispatch, combine, first_in, first_out,
    tokens_v, grads_v, rows, sems,
):
    images = tokens.shape[0]
    slots = params.shape[0]
    stride = KINDS * images
    halves = start_halves(tokens, tokens_v, sems)
    grads_copy = start_copy(grads, grads_v, sems.at[2])
    units = slice(0, first_out.shape[0])
    weight_copies = (
        start_copy(w_in.at[:, units], first_in, sems.at[3]),
        start_copy(w_out.at[units, :], first_out, sems.at[4]),
    )
    logits = []
    for copy, half in halves:
        copy.wait()
        logits += [dot(params[...], tokens_v[image], 1, 1) for image in half]
    over_slots = []
    for image in range(images):
        over_tokens = softmax(logits[image], 1)
        dispatch[image] = over_tokens
        put(
            rows, KINDS * image, slots, stride, dot(over_tokens.astype(LOW), tokens_v[image], 1, 0)
        )
        over_slots.append(softmax(logits[image], 0))
        combine[image] = over_slots[image]
    grads_copy.wait()
    for image in range(images):
        value = dot(over_slots[image].astype(LOW), grads_v[image], 1, 0)
        put(rows, KINDS * image + 1, slots, stride, value)
    sent[...] = packed(rows)
    for copy in weight_copies:
        copy.wait()


def gather(tokens, params, grads, w_in, w_out, first):
    images, length, width = tokens.shape
    slots = params.shape[0]
    weights = shaped((images, slots, length), WIDE)
    rows = (slots * images * KINDS, width)
    return call(
        gather_kernel,
        "gather_slots",
        ROOMY,
        6 * images * slots * length * width,
        4 * images * length * width,
        2 * images * slots * length,
        out_shape=(
            shaped(rows, LOW),
            weights,
            weights,
            shaped((width, first), LOW),
            shaped((first, width), LOW),
        ),
        in_specs=[PLACE, WHOLE, PLACE, PLACE, PLACE],
        out_specs=(WHOLE,) * 5,
        scratch_shapes=[
            pltpu.VMEM(tokens.shape, LOW),
            pltpu.VMEM(grads.shape, LOW),
            scratch_rows(rows),
            pltpu.SemaphoreType.DMA((5,)),
        ],
    )(tokens, params, grads, w_in, w_out)


def chunks_of(first, hidden, tile):
    edges = [*range(first, hidden, tile), hidden]
    return [slice(low, high) for low, high in zip(edges, edges[1:])]


def start_weights(w_in, w_out, w_in_v, w_out_v, sems, chunks):
    copies = []
    for chunk, units in enumerate(chunks):
        copies.append(
            (
                start_copy(w_in.at[:, units], w_in_v.at[:, units], sems.at[0, chunk]),
                start_copy(w_out.at[units, :], w_out_v.at[units, :], sems.at[1, chunk]),
            )
        )
    return copies


def weight_scratch(width, hidden, chunks):
    return [
        pltpu.VMEM((width, hidden), LOW),
        pltpu.VMEM((hidden, width), LOW),
        pltpu.SemaphoreType.DMA((2, len(chunks))),
    ]


def expert_kernel(
    chunks, rows, first_in, first_out, w_in, w_out, back, acts, hidden, mark,
    w_in_v, w_out_v, sems, wide,
):
    del mark
    copies = start_weights(w_in, w_out, w_in_v, w_out_v, sems, chunks)
    count = rows.shape[0] // KINDS
    load_rows(wide, rows[...])
    rows_in = take(wide, 0, count, KINDS).astype(LOW)
    rows_grad = take(wide, 1, count, KINDS).astype(LOW)

    def first_products(weight_in, weight_out):
        return dot(rows_in, weight_in, 1, 0), dot(rows_grad, weight_out, 1, 1)

    def second_products(held, weight_in, weight_out):
        return dot(held[0], weight_out, 1, 0), dot(held[1], weight_in, 1, 1)

    def hold(preact, d_acts, units):
        values, slope = gelu_parts(preact)
        held = (values.astype(LOW), (d_acts * slope).astype(LOW))
        acts[:, units], hidden[:, units] = held
        return held

    held = hold(
        *first_products(first_in[...], first_out[...]), slice(0, first_out.shape[0])
    )
    out, d_in = second_products(held, first_in[...], first_out[...])
    before = None
    for pair, units in zip([*copies, None], [*chunks, None]):
        if pair is not None:
            for copy in pair:
                copy.wait()
            products = first_products(w_in_v[:, units], w_out_v[units, :])
        if before is not None:
            parts = second_products(held, w_in_v[:, before], w_out_v[before, :])
            out, d_in = out + parts[0], d_in + parts[1]
        if pair is not None:
            held = hold(*products, units)
        before = units
    put(wide, 0, count, KINDS, out)
    put(wide, 1, count, KINDS, d_in)
    back[...] = packed(wide)


def expert(rows, first_in, first_out, w_in, w_out, tile):
    total, width = rows.shape
    hidden = w_in.shape[1]
    count = total // KINDS
    kept = shaped((count, hidden), LOW)
    chunks = chunks_of(first_out.shape[0], hidden, tile)
    return call(
        functools.partial(expert_kernel, chunks),
        "expert_rows",
        ROOMY,
        8 * count * hidden * width,
        4 * hidden * width,
        count * hidden,
        out_shape=(shaped(rows.shape, LOW), kept, kept, MARK),
        in_specs=[WHOLE, WHOLE, WHOLE, PLACE, PLACE],
        out_specs=(WHOLE, WHOLE, WHOLE, PLACE),
        scratch_shapes=[*weight_scratch(width, hidden, chunks), scratch_rows(rows.shape)],
    )(rows, first_in, first_out, w_in, w_out)


def replica_kernel(
    chunks, mine, after, rows, other_rows, acts, hidden, w_in, w_out, grad_in, grad_out, mark,
    w_in_v, w_out_v, grad_in_v, grad_out_v, wide, grads, turned, sems, in_sems, out_sems,
):
    del after, mark
    count = rows.shape[0] // KINDS
    size = w_in.shape[1]
    half = grad_out.shape[0]
    spans, copies = [], []
    for chunk, units in enumerate(chunks):
        start = pl.multiple_of(lax.rem(mine[0] * half + units.start, size), LANES)
        span = pl.ds(start, units.stop - units.start)
        spans.append(span)
        copies.append(
            (
                start_copy(w_in.at[:, span], w_in_v.at[:, units], sems.at[0, chunk]),
                start_copy(w_out.at[span, :], w_out_v.at[units, :], sems.at[1, chunk]),
            )
        )
    left, right = [], []
    tiles = turned.shape[0] // LANES
    for source in (rows, other_rows):
        load_rows(wide, source[...])
        left.append(take(wide, 0, count, KINDS, mine[0] * tiles, tiles))
        right.append(take(wide, 1, count, KINDS))
    turned[...] = jnp.concatenate(left, axis=0).T.astype(LOW)
    grads[...] = jnp.concatenate(right, axis=0).astype(LOW)
    rows_in = take(wide, 0, count, KINDS).astype(LOW)
    rows_grad = right[1].astype(LOW)
    results = []
    before = None
    for chunk in range(len(chunks) + 1):
        if chunk < len(chunks):
            units = chunks[chunk]
            for copy in copies[chunk]:
                copy.wait()
            preact = dot(rows_in, w_in_v[:, units], 1, 0)
            d_acts = dot(rows_grad, w_out_v[units, :], 1, 1)
        if before is not None:
            past, span, all_acts, all_hidden = before
            grad_in_v[:, past] = dot(turned[...], all_hidden, 1, 0).astype(LOW)
            results.append(
                start_copy(grad_in_v.at[:, past], grad_in.at[:, span], in_sems.at[chunk - 1])
            )
            if past.stop <= half:
                grad_out_v[past, :] = dot(all_acts, grads[...], 0, 0).astype(LOW)
                results.append(
                    start_copy(
                        grad_out_v.at[past, :], grad_out.at[past, :], out_sems.at[chunk - 1]
                    )
                )
        if chunk < len(chunks):
            span = spans[chunk]
            values, slope = gelu_parts(preact)
            all_acts = jnp.concatenate([acts[:, span], values.astype(LOW)], axis=0)
            all_hidden = jnp.concatenate(
                [hidden[:, span], (d_acts * slope).astype(LOW)], axis=0
            )
            before = (units, span, all_acts, all_hidden)
    for copy in results:
        copy.wait()


def replica_grads(mine, after, rows, other_rows, acts, hidden, w_in, w_out, replicas, tile):
    total, width = rows.shape
    size = w_in.shape[1]
    half = size // replicas
    count = total // KINDS
    chunks = [
        slice(part * half + units.start, part * half + units.stop)
        for part in range(replicas)
        for units in chunks_of(0, half, tile)
    ]
    return call(
        functools.partial(replica_kernel, chunks),
        "replica_grads",
        SHARED,
        64 * count * size * width,
        32 * size * width,
        count * size,
        out_shape=(
            shaped((width // replicas, size), LOW),
            shaped((half, width), LOW),
            MARK,
        ),
        in_specs=[pl.BlockSpec(memory_space=pltpu.SMEM), PLACE]
        + [WHOLE] * 4
        + [PLACE] * 2,
        out_specs=(PLACE,) * 3,
        scratch_shapes=[
            *weight_scratch(width, size, chunks)[:2],
            pltpu.VMEM((width // replicas, size), LOW),
            pltpu.VMEM((half, width), LOW),
            scratch_rows((total, width)),
            pltpu.VMEM((2 * count, width), LOW),
            pltpu.VMEM((width // replicas, 2 * count), LOW),
            pltpu.SemaphoreType.DMA((2, len(chunks))),
            pltpu.SemaphoreType.DMA((len(chunks),)),
            pltpu.SemaphoreType.DMA((len(chunks),)),
        ],
    )(mine, after, rows, other_rows, acts, hidden, w_in, w_out)


def logits_kernel(
    after, back, tokens, params, grads, dispatch, combine, left, right, local, mark,
    tokens_v, grads_v, wide, sems,
):
    del after, mark
    images, slots, _ = dispatch.shape
    halves = start_halves(tokens, tokens_v, sems)
    grads_copy = start_copy(grads, grads_v, sems.at[2])
    load_rows(wide, back[...])
    stride = KINDS * images
    d_slot_in = []
    for image in range(images):
        d_slot_in.append(take(wide, KINDS * image + 1, slots, stride).astype(LOW))
        right[image, :slots, :] = d_slot_in[image]
        right[image, slots:, :] = params[...]
        left[image, :slots, :] = dispatch[image].astype(LOW)
    parts = []
    for copy, half in halves:
        copy.wait()
        for image in half:
            weights = dispatch[image]
            d_dispatch = dot(d_slot_in[image], tokens_v[image], 1, 1)
            parts.append(
                weights * (d_dispatch - jnp.sum(weights * d_dispatch, axis=1, keepdims=True))
            )
    grads_copy.wait()
    total = None
    for image in range(images):
        slot_out = take(wide, KINDS * image, slots, stride).astype(LOW)
        weights = combine[image]
        d_combine = dot(slot_out, grads_v[image], 1, 1)
        d_logits = parts[image] + weights * (
            d_combine - jnp.sum(weights * d_combine, axis=0, keepdims=True)
        )
        low = d_logits.astype(LOW)
        left[image, slots:, :] = low
        part = dot(low, tokens_v[image], 1, 0)
        total = part if image == 0 else total + part
    local[...] = total.astype(LOW)


def logits_grads(after, back, tokens, params, grads, dispatch, combine):
    images, length, width = tokens.shape
    slots = params.shape[0]
    return call(
        logits_kernel,
        "logits_grads",
        SHARED,
        6 * images * slots * length * width,
        4 * images * length * width,
        out_shape=(
            shaped((images, 2 * slots, length), LOW),
            shaped((images, 2 * slots, width), LOW),
            shaped(params.shape, LOW),
            MARK,
        ),
        in_specs=[PLACE, WHOLE, PLACE, WHOLE, PLACE, WHOLE, WHOLE],
        out_specs=(WHOLE, WHOLE, WHOLE, PLACE),
        scratch_shapes=[
            pltpu.VMEM(tokens.shape, LOW),
            pltpu.VMEM(grads.shape, LOW),
            scratch_rows(back.shape),
            pltpu.SemaphoreType.DMA((3,)),
        ],
    )(after, back, tokens, params, grads, dispatch, combine)


def tokens_kernel(after, left, right, out, mark):
    del after, mark
    out[0] = dot(left[0], right[0], 0, 0).astype(LOW)


def tokens_grads(after, left, right):
    images, deep, length = left.shape
    width = right.shape[2]
    return call(
        tokens_kernel,
        "tokens_grads",
        SHARED,
        2 * images * deep * length * width,
        2 * images * length * width,
        grid=(images,),
        out_shape=(shaped((images, length, width), LOW), MARK),
        in_specs=[
            PLACE,
            pl.BlockSpec((1, deep, length), lambda i: (i, 0, 0)),
            pl.BlockSpec((1, deep, width), lambda i: (i, 0, 0)),
        ],
        out_specs=(pl.BlockSpec((1, length, width), lambda i: (i, 0, 0)), PLACE),
    )(after, left, right)


def add_kernel(after, *refs):
    del after
    terms = [ref[...].astype(WIDE) for ref in refs[:-2]]
    while len(terms) > 1:
        terms = [left + right for left, right in zip(terms[::2], terms[1::2])]
    refs[-2][...] = terms[0].astype(refs[-2].dtype)


def add(after, terms, dtype):
    return call(
        add_kernel,
        "add_terms",
        SHARED,
        len(terms) * terms[0].size,
        2 * len(terms) * terms[0].size,
        out_shape=(shaped(terms[0].shape, dtype), MARK),
        in_specs=[PLACE] + [WHOLE] * len(terms),
        out_specs=(WHOLE, PLACE),
    )(after, *terms)


def terms_of_group(array, axis, distances):
    count = lax.axis_size(axis)
    return [array] + [
        lax.ppermute(array, axis, [(i, i ^ distance) for i in range(count)])
        for distance in distances
    ]


def exchange(rows, axes):
    return lax.all_to_all(rows, axes, split_axis=0, concat_axis=0, tiled=True)


def body(tokens, slot_params, expert_in, expert_out, grad_out):
    params = slot_params.T
    weights = (expert_in[0], expert_out[0])
    replicas = lax.axis_size("rep")
    mine = lax.axis_index("rep").astype(jnp.int32).reshape(1)

    sent, dispatch, combine, *first = gather(tokens, params, grad_out, *weights, 512)
    rows = exchange(sent, "exp")
    other_rows = lax.ppermute(rows, "rep", [(i, (i + 1) % replicas) for i in range(replicas)])
    back, acts, hidden, after = expert(rows, *first, *weights, 512)
    back = exchange(back, "exp")
    grad_in, grad_outer, after = replica_grads(
        mine, after, rows, other_rows, acts, hidden, *weights, replicas, 512
    )
    left, right, local, after = logits_grads(
        after, back, tokens, params, grad_out, dispatch, combine
    )
    bits = lax.axis_size("exp").bit_length() - 1
    groups = [(1 << bit, 2 << bit, 3 << bit) for bit in range(0, bits - 1, 2)]
    if bits % 2:
        groups.append((1 << (bits - 1),))
    terms = terms_of_group(local, "exp", groups[0])
    grad_tokens, after = tokens_grads(after, left, right)
    local, after = add(after, terms, LOW)
    for distances in groups[1:]:
        local, after = add(after, terms_of_group(local, "exp", distances), LOW)
    grad_params, _ = add(after, terms_of_group(local, "rep", (1,)), WIDE)
    return (grad_tokens, grad_params.T, grad_in[None], grad_outer[None])


def solution(mesh):
    in_specs = (
        P(("rep", "exp"), None, None),
        P(),
        P("exp", None, None),
        P("exp", None, None),
        P(("rep", "exp"), None, None),
    )
    out_specs = (P(("rep", "exp"), None, None), P(), P("exp", "rep", None), P("exp", "rep", None))
    return jax.shard_map(body, mesh=mesh, in_specs=in_specs, out_specs=out_specs, check_vma=False)
```

```python
import functools
import math

import jax
import jax.numpy as jnp
from jax import lax
from jax.experimental import pallas as pl
from jax.experimental.pallas import tpu as pltpu
from jax.sharding import PartitionSpec as P

GELU_C = math.sqrt(2.0 / math.pi)
CUBIC = 0.044715
LOW = jnp.bfloat16
WIDE = jnp.float32
LANES = 128
KINDS = 2
SHARED = 52 * 1024 * 1024
ROOMY = 50 * 1024 * 1024
WHOLE = pl.BlockSpec(memory_space=pltpu.VMEM)
PLACE = pl.BlockSpec(memory_space=pl.ANY)


def call(kernel, name, grant, flops, nbytes, exps=0, **kwargs):
    return pl.pallas_call(
        kernel,
        name=name,
        compiler_params=pltpu.CompilerParams(vmem_limit_bytes=grant),
        cost_estimate=pl.CostEstimate(
            flops=flops, bytes_accessed=nbytes, transcendentals=exps
        ),
        **kwargs,
    )


def shaped(shape, dtype):
    return jax.ShapeDtypeStruct(shape, dtype)


MARK = shaped((8, LANES), WIDE)


def gelu_parts(values):
    square = values * values
    tangent = jnp.tanh(GELU_C * (values + CUBIC * square * values))
    half = 0.5 * (1.0 + tangent)
    slope = half + 0.5 * values * (1.0 - tangent * tangent) * GELU_C * (1.0 + 3.0 * CUBIC * square)
    return values * half, slope


def dot(left, right, over_left, over_right):
    return lax.dot_general(
        left, right, (((over_left,), (over_right,)), ((), ())), preferred_element_type=WIDE
    )


def softmax(values, axis):
    raised = jnp.exp(values - jnp.max(values, axis=axis, keepdims=True))
    return raised / jnp.sum(raised, axis=axis, keepdims=True)


def scratch_rows(shape):
    return pltpu.VMEM((shape[1] // LANES, shape[0], LANES), WIDE)


def load_rows(ref, array):
    for tile in range(ref.shape[0]):
        ref[tile] = array[:, tile * LANES : (tile + 1) * LANES].astype(WIDE)


def packed(ref):
    return jnp.concatenate([ref[tile] for tile in range(ref.shape[0])], axis=1).astype(LOW)


def take(ref, start, count, stride, first=0, tiles=None):
    tiles = ref.shape[0] if tiles is None else tiles
    picked = [ref[first + tile, pl.ds(start, count, stride=stride), :] for tile in range(tiles)]
    return jnp.concatenate(picked, axis=1)


def put(ref, start, count, stride, array):
    for tile in range(ref.shape[0]):
        ref[tile, pl.ds(start, count, stride=stride), :] = array[
            :, tile * LANES : (tile + 1) * LANES
        ]


def start_copy(source, target, sem):
    copy = pltpu.make_async_copy(source, target, sem)
    copy.start()
    return copy


def start_halves(source, target, sems):
    images = source.shape[0]
    parts = []
    for index, (first, last) in enumerate(((0, images // 2), (images // 2, images))):
        part = pl.ds(first, last - first)
        copy = start_copy(source.at[part], target.at[part], sems.at[index])
        parts.append((copy, range(first, last)))
    return parts


def gather_kernel(
    tokens, params, grads, w_in, w_out, sent, dispatch, combine, first_in, first_out,
    tokens_v, grads_v, rows, sems,
):
    images = tokens.shape[0]
    slots = params.shape[0]
    stride = KINDS * images
    halves = start_halves(tokens, tokens_v, sems)
    grads_copy = start_copy(grads, grads_v, sems.at[2])
    units = slice(0, first_out.shape[0])
    weight_copies = (
        start_copy(w_in.at[:, units], first_in, sems.at[3]),
        start_copy(w_out.at[units, :], first_out, sems.at[4]),
    )
    logits = []
    for copy, half in halves:
        copy.wait()
        logits += [dot(params[...], tokens_v[image], 1, 1) for image in half]
    over_slots = []
    for image in range(images):
        over_tokens = softmax(logits[image], 1)
        dispatch[image] = over_tokens
        put(
            rows, KINDS * image, slots, stride, dot(over_tokens.astype(LOW), tokens_v[image], 1, 0)
        )
        over_slots.append(softmax(logits[image], 0))
        combine[image] = over_slots[image]
    grads_copy.wait()
    for image in range(images):
        value = dot(over_slots[image].astype(LOW), grads_v[image], 1, 0)
        put(rows, KINDS * image + 1, slots, stride, value)
    sent[...] = packed(rows)
    for copy in weight_copies:
        copy.wait()


def gather(tokens, params, grads, w_in, w_out, first):
    images, length, width = tokens.shape
    slots = params.shape[0]
    weights = shaped((images, slots, length), WIDE)
    rows = (slots * images * KINDS, width)
    return call(
        gather_kernel,
        "gather_slots",
        ROOMY,
        6 * images * slots * length * width,
        4 * images * length * width,
        2 * images * slots * length,
        out_shape=(
            shaped(rows, LOW),
            weights,
            weights,
            shaped((width, first), LOW),
            shaped((first, width), LOW),
        ),
        in_specs=[PLACE, WHOLE, PLACE, PLACE, PLACE],
        out_specs=(WHOLE,) * 5,
        scratch_shapes=[
            pltpu.VMEM(tokens.shape, LOW),
            pltpu.VMEM(grads.shape, LOW),
            scratch_rows(rows),
            pltpu.SemaphoreType.DMA((5,)),
        ],
    )(tokens, params, grads, w_in, w_out)


def chunks_of(first, hidden, tile):
    edges = [*range(first, hidden, tile), hidden]
    return [slice(low, high) for low, high in zip(edges, edges[1:])]


def start_weights(w_in, w_out, w_in_v, w_out_v, sems, chunks):
    copies = []
    for chunk, units in enumerate(chunks):
        copies.append(
            (
                start_copy(w_in.at[:, units], w_in_v.at[:, units], sems.at[0, chunk]),
                start_copy(w_out.at[units, :], w_out_v.at[units, :], sems.at[1, chunk]),
            )
        )
    return copies


def weight_scratch(width, hidden, chunks):
    return [
        pltpu.VMEM((width, hidden), LOW),
        pltpu.VMEM((hidden, width), LOW),
        pltpu.SemaphoreType.DMA((2, len(chunks))),
    ]


def expert_kernel(
    chunks, rows, first_in, first_out, w_in, w_out, back, acts, hidden, mark,
    w_in_v, w_out_v, sems, wide,
):
    del mark
    copies = start_weights(w_in, w_out, w_in_v, w_out_v, sems, chunks)
    count = rows.shape[0] // KINDS
    load_rows(wide, rows[...])
    rows_in = take(wide, 0, count, KINDS).astype(LOW)
    rows_grad = take(wide, 1, count, KINDS).astype(LOW)

    def first_products(weight_in, weight_out):
        return dot(rows_in, weight_in, 1, 0), dot(rows_grad, weight_out, 1, 1)

    def second_products(held, weight_in, weight_out):
        return dot(held[0], weight_out, 1, 0), dot(held[1], weight_in, 1, 1)

    def hold(preact, d_acts, units):
        values, slope = gelu_parts(preact)
        held = (values.astype(LOW), (d_acts * slope).astype(LOW))
        acts[:, units], hidden[:, units] = held
        return held

    held = hold(
        *first_products(first_in[...], first_out[...]), slice(0, first_out.shape[0])
    )
    out, d_in = second_products(held, first_in[...], first_out[...])
    before = None
    for pair, units in zip([*copies, None], [*chunks, None]):
        if pair is not None:
            for copy in pair:
                copy.wait()
            products = first_products(w_in_v[:, units], w_out_v[units, :])
        if before is not None:
            parts = second_products(held, w_in_v[:, before], w_out_v[before, :])
            out, d_in = out + parts[0], d_in + parts[1]
        if pair is not None:
            held = hold(*products, units)
        before = units
    put(wide, 0, count, KINDS, out)
    put(wide, 1, count, KINDS, d_in)
    back[...] = packed(wide)


def expert(rows, first_in, first_out, w_in, w_out, tile):
    total, width = rows.shape
    hidden = w_in.shape[1]
    count = total // KINDS
    kept = shaped((count, hidden), LOW)
    chunks = chunks_of(first_out.shape[0], hidden, tile)
    return call(
        functools.partial(expert_kernel, chunks),
        "expert_rows",
        ROOMY,
        8 * count * hidden * width,
        4 * hidden * width,
        count * hidden,
        out_shape=(shaped(rows.shape, LOW), kept, kept, MARK),
        in_specs=[WHOLE, WHOLE, WHOLE, PLACE, PLACE],
        out_specs=(WHOLE, WHOLE, WHOLE, PLACE),
        scratch_shapes=[*weight_scratch(width, hidden, chunks), scratch_rows(rows.shape)],
    )(rows, first_in, first_out, w_in, w_out)


def replica_kernel(
    chunks, mine, after, rows, other_rows, acts, hidden, w_in, w_out, grad_in, grad_out, mark,
    w_in_v, w_out_v, grad_in_v, grad_out_v, wide, grads, turned, sems, in_sems, out_sems,
):
    del after, mark
    count = rows.shape[0] // KINDS
    size = w_in.shape[1]
    half = grad_out.shape[0]
    spans, copies = [], []
    for chunk, units in enumerate(chunks):
        start = pl.multiple_of(lax.rem(mine[0] * half + units.start, size), LANES)
        span = pl.ds(start, units.stop - units.start)
        spans.append(span)
        copies.append(
            (
                start_copy(w_in.at[:, span], w_in_v.at[:, units], sems.at[0, chunk]),
                start_copy(w_out.at[span, :], w_out_v.at[units, :], sems.at[1, chunk]),
            )
        )
    left, right = [], []
    tiles = turned.shape[0] // LANES
    for source in (rows, other_rows):
        load_rows(wide, source[...])
        left.append(take(wide, 0, count, KINDS, mine[0] * tiles, tiles))
        right.append(take(wide, 1, count, KINDS))
    turned[...] = jnp.concatenate(left, axis=0).T.astype(LOW)
    grads[...] = jnp.concatenate(right, axis=0).astype(LOW)
    rows_in = take(wide, 0, count, KINDS).astype(LOW)
    rows_grad = right[1].astype(LOW)
    results = []
    before = None
    for chunk in range(len(chunks) + 1):
        if chunk < len(chunks):
            units = chunks[chunk]
            for copy in copies[chunk]:
                copy.wait()
            preact = dot(rows_in, w_in_v[:, units], 1, 0)
            d_acts = dot(rows_grad, w_out_v[units, :], 1, 1)
        if before is not None:
            past, span, all_acts, all_hidden = before
            grad_in_v[:, past] = dot(turned[...], all_hidden, 1, 0).astype(LOW)
            results.append(
                start_copy(grad_in_v.at[:, past], grad_in.at[:, span], in_sems.at[chunk - 1])
            )
            if past.stop <= half:
                grad_out_v[past, :] = dot(all_acts, grads[...], 0, 0).astype(LOW)
                results.append(
                    start_copy(
                        grad_out_v.at[past, :], grad_out.at[past, :], out_sems.at[chunk - 1]
                    )
                )
        if chunk < len(chunks):
            span = spans[chunk]
            values, slope = gelu_parts(preact)
            all_acts = jnp.concatenate([acts[:, span], values.astype(LOW)], axis=0)
            all_hidden = jnp.concatenate(
                [hidden[:, span], (d_acts * slope).astype(LOW)], axis=0
            )
            before = (units, span, all_acts, all_hidden)
    for copy in results:
        copy.wait()


def replica_grads(mine, after, rows, other_rows, acts, hidden, w_in, w_out, replicas, tile):
    total, width = rows.shape
    size = w_in.shape[1]
    half = size // replicas
    count = total // KINDS
    chunks = [
        slice(part * half + units.start, part * half + units.stop)
        for part in range(replicas)
        for units in chunks_of(0, half, tile)
    ]
    return call(
        functools.partial(replica_kernel, chunks),
        "replica_grads",
        SHARED,
        64 * count * size * width,
        32 * size * width,
        count * size,
        out_shape=(
            shaped((width // replicas, size), LOW),
            shaped((half, width), LOW),
            MARK,
        ),
        in_specs=[pl.BlockSpec(memory_space=pltpu.SMEM), PLACE]
        + [WHOLE] * 4
        + [PLACE] * 2,
        out_specs=(PLACE,) * 3,
        scratch_shapes=[
            *weight_scratch(width, size, chunks)[:2],
            pltpu.VMEM((width // replicas, size), LOW),
            pltpu.VMEM((half, width), LOW),
            scratch_rows((total, width)),
            pltpu.VMEM((2 * count, width), LOW),
            pltpu.VMEM((width // replicas, 2 * count), LOW),
            pltpu.SemaphoreType.DMA((2, len(chunks))),
            pltpu.SemaphoreType.DMA((len(chunks),)),
            pltpu.SemaphoreType.DMA((len(chunks),)),
        ],
    )(mine, after, rows, other_rows, acts, hidden, w_in, w_out)


def logits_kernel(
    after, back, tokens, params, grads, dispatch, combine, left, right, local, mark,
    tokens_v, grads_v, wide, sems,
):
    del after, mark
    images, slots, _ = dispatch.shape
    halves = start_halves(tokens, tokens_v, sems)
    grads_copy = start_copy(grads, grads_v, sems.at[2])
    load_rows(wide, back[...])
    stride = KINDS * images
    d_slot_in = []
    for image in range(images):
        d_slot_in.append(take(wide, KINDS * image + 1, slots, stride).astype(LOW))
        right[image, :slots, :] = d_slot_in[image]
        right[image, slots:, :] = params[...]
        left[image, :slots, :] = dispatch[image].astype(LOW)
    parts = []
    for copy, half in halves:
        copy.wait()
        for image in half:
            weights = dispatch[image]
            d_dispatch = dot(d_slot_in[image], tokens_v[image], 1, 1)
            parts.append(
                weights * (d_dispatch - jnp.sum(weights * d_dispatch, axis=1, keepdims=True))
            )
    grads_copy.wait()
    total = None
    for image in range(images):
        slot_out = take(wide, KINDS * image, slots, stride).astype(LOW)
        weights = combine[image]
        d_combine = dot(slot_out, grads_v[image], 1, 1)
        d_logits = parts[image] + weights * (
            d_combine - jnp.sum(weights * d_combine, axis=0, keepdims=True)
        )
        low = d_logits.astype(LOW)
        left[image, slots:, :] = low
        part = dot(low, tokens_v[image], 1, 0)
        total = part if image == 0 else total + part
    local[...] = total.astype(LOW)


def logits_grads(after, back, tokens, params, grads, dispatch, combine):
    images, length, width = tokens.shape
    slots = params.shape[0]
    return call(
        logits_kernel,
        "logits_grads",
        SHARED,
        6 * images * slots * length * width,
        4 * images * length * width,
        out_shape=(
            shaped((images, 2 * slots, length), LOW),
            shaped((images, 2 * slots, width), LOW),
            shaped(params.shape, LOW),
            MARK,
        ),
        in_specs=[PLACE, WHOLE, PLACE, WHOLE, PLACE, WHOLE, WHOLE],
        out_specs=(WHOLE, WHOLE, WHOLE, PLACE),
        scratch_shapes=[
            pltpu.VMEM(tokens.shape, LOW),
            pltpu.VMEM(grads.shape, LOW),
            scratch_rows(back.shape),
            pltpu.SemaphoreType.DMA((3,)),
        ],
    )(after, back, tokens, params, grads, dispatch, combine)


def tokens_kernel(after, left, right, out, mark):
    del after, mark
    out[0] = dot(left[0], right[0], 0, 0).astype(LOW)


def tokens_grads(after, left, right):
    images, deep, length = left.shape
    width = right.shape[2]
    return call(
        tokens_kernel,
        "tokens_grads",
        SHARED,
        2 * images * deep * length * width,
        2 * images * length * width,
        grid=(images,),
        out_shape=(shaped((images, length, width), LOW), MARK),
        in_specs=[
            PLACE,
            pl.BlockSpec((1, deep, length), lambda i: (i, 0, 0)),
            pl.BlockSpec((1, deep, width), lambda i: (i, 0, 0)),
        ],
        out_specs=(pl.BlockSpec((1, length, width), lambda i: (i, 0, 0)), PLACE),
    )(after, left, right)


def add_kernel(after, *refs):
    del after
    terms = [ref[...].astype(WIDE) for ref in refs[:-2]]
    while len(terms) > 1:
        terms = [left + right for left, right in zip(terms[::2], terms[1::2])]
    refs[-2][...] = terms[0].astype(refs[-2].dtype)


def add(after, terms, dtype):
    return call(
        add_kernel,
        "add_terms",
        SHARED,
        len(terms) * terms[0].size,
        2 * len(terms) * terms[0].size,
        out_shape=(shaped(terms[0].shape, dtype), MARK),
        in_specs=[PLACE] + [WHOLE] * len(terms),
        out_specs=(WHOLE, PLACE),
    )(after, *terms)


def terms_of_group(array, bits):
    axes = ("rep", "exp")
    distances = [0]
    for bit in bits:
        distances += [distance + (1 << bit) for distance in distances]
    count = lax.axis_size(axes)
    return [array] + [
        lax.ppermute(array, axes, [(i, i ^ distance) for i in range(count)])
        for distance in distances[1:]
    ]


def exchange(rows, axes):
    return lax.all_to_all(rows, axes, split_axis=0, concat_axis=0, tiled=True)


def body(tokens, slot_params, expert_in, expert_out, grad_out):
    params = slot_params.T
    weights = (expert_in[0], expert_out[0])
    replicas = lax.axis_size("rep")
    mine = lax.axis_index("rep").astype(jnp.int32).reshape(1)

    sent, dispatch, combine, *first = gather(tokens, params, grad_out, *weights, 256)
    rows = exchange(sent, "exp")
    other_rows = lax.ppermute(rows, "rep", [(i, (i + 1) % replicas) for i in range(replicas)])
    back, acts, hidden, after = expert(rows, *first, *weights, 512)
    back = exchange(back, "exp")
    grad_in, grad_outer, after = replica_grads(
        mine, after, rows, other_rows, acts, hidden, *weights, replicas, 512
    )
    left, right, local, after = logits_grads(
        after, back, tokens, params, grad_out, dispatch, combine
    )
    exp_bits = lax.axis_size("exp").bit_length() - 1
    rep_bits = replicas.bit_length() - 1
    groups = [(0, 1, *range(exp_bits, exp_bits + rep_bits))]
    groups += [range(bit, min(bit + 2, exp_bits)) for bit in range(2, exp_bits, 2)]
    for bits in groups[:-1]:
        local, after = add(after, terms_of_group(local, bits), LOW)
    terms = terms_of_group(local, groups[-1])
    grad_tokens, after = tokens_grads(after, left, right)
    grad_params, _ = add(after, terms, WIDE)
    return (grad_tokens, grad_params.T, grad_in[None], grad_outer[None])


def solution(mesh):
    in_specs = (
        P(("rep", "exp"), None, None),
        P(),
        P("exp", None, None),
        P("exp", None, None),
        P(("rep", "exp"), None, None),
    )
    out_specs = (P(("rep", "exp"), None, None), P(), P("exp", "rep", None), P("exp", "rep", None))
    return jax.shard_map(body, mesh=mesh, in_specs=in_specs, out_specs=out_specs, check_vma=False)
```

```python
import functools
import math

import jax
import jax.numpy as jnp
from jax import lax
from jax.experimental import pallas as pl
from jax.experimental.pallas import tpu as pltpu
from jax.sharding import PartitionSpec as P

GELU_C = math.sqrt(2.0 / math.pi)
CUBIC = 0.044715
LOW = jnp.bfloat16
WIDE = jnp.float32
LANES = 128
KINDS = 2
SHARED = 52 * 1024 * 1024
ROOMY = 50 * 1024 * 1024
WHOLE = pl.BlockSpec(memory_space=pltpu.VMEM)
PLACE = pl.BlockSpec(memory_space=pl.ANY)


def call(kernel, name, grant, flops, nbytes, exps=0, **kwargs):
    return pl.pallas_call(
        kernel,
        name=name,
        compiler_params=pltpu.CompilerParams(vmem_limit_bytes=grant),
        cost_estimate=pl.CostEstimate(
            flops=flops, bytes_accessed=nbytes, transcendentals=exps
        ),
        **kwargs,
    )


def shaped(shape, dtype):
    return jax.ShapeDtypeStruct(shape, dtype)


MARK = shaped((8, LANES), WIDE)


def gelu_parts(values):
    square = values * values
    tangent = jnp.tanh(GELU_C * (values + CUBIC * square * values))
    half = 0.5 * (1.0 + tangent)
    slope = half + 0.5 * values * (1.0 - tangent * tangent) * GELU_C * (1.0 + 3.0 * CUBIC * square)
    return values * half, slope


def dot(left, right, over_left, over_right):
    return lax.dot_general(
        left, right, (((over_left,), (over_right,)), ((), ())), preferred_element_type=WIDE
    )


def softmax(values, axis):
    raised = jnp.exp(values - jnp.max(values, axis=axis, keepdims=True))
    return raised / jnp.sum(raised, axis=axis, keepdims=True)


def scratch_rows(shape):
    return pltpu.VMEM((shape[1] // LANES, shape[0], LANES), WIDE)


def load_rows(ref, array):
    for tile in range(ref.shape[0]):
        ref[tile] = array[:, tile * LANES : (tile + 1) * LANES].astype(WIDE)


def packed(ref):
    return jnp.concatenate([ref[tile] for tile in range(ref.shape[0])], axis=1).astype(LOW)


def take(ref, start, count, stride, first=0, tiles=None):
    tiles = ref.shape[0] if tiles is None else tiles
    picked = [ref[first + tile, pl.ds(start, count, stride=stride), :] for tile in range(tiles)]
    return jnp.concatenate(picked, axis=1)


def put(ref, start, count, stride, array):
    for tile in range(ref.shape[0]):
        ref[tile, pl.ds(start, count, stride=stride), :] = array[
            :, tile * LANES : (tile + 1) * LANES
        ]


def start_copy(source, target, sem, priority=0):
    copy = pltpu.make_async_copy(source, target, sem)
    copy.start(priority=priority)
    return copy


def far(array):
    return pltpu.with_memory_space_constraint(array, pltpu.HBM)


def start_halves(source, target, sems):
    images = source.shape[0]
    parts = []
    for index, (first, last) in enumerate(((0, images // 2), (images // 2, images))):
        part = pl.ds(first, last - first)
        copy = start_copy(source.at[part], target.at[part], sems.at[index])
        parts.append((copy, range(first, last)))
    return parts


def gather_kernel(
    tokens, params_far, grads, w_in, w_out, sent, dispatch, combine, first_in, first_out,
    tokens_v, grads_v, params, rows, sems,
):
    images = tokens.shape[0]
    slots = params.shape[0]
    stride = KINDS * images
    params_copy = start_copy(params_far, params, sems.at[5], priority=1)
    halves = start_halves(tokens, tokens_v, sems)
    grads_copy = start_copy(grads, grads_v, sems.at[2])
    units = slice(0, first_out.shape[0])
    weight_copies = (
        start_copy(w_in.at[:, units], first_in, sems.at[3]),
        start_copy(w_out.at[units, :], first_out, sems.at[4]),
    )
    logits = []
    params_copy.wait()
    for copy, half in halves:
        copy.wait()
        logits += [dot(params[...], tokens_v[image], 1, 1) for image in half]
    over_slots = []
    for image in range(images):
        over_tokens = softmax(logits[image], 1)
        dispatch[image] = over_tokens
        put(
            rows, KINDS * image, slots, stride, dot(over_tokens.astype(LOW), tokens_v[image], 1, 0)
        )
        over_slots.append(softmax(logits[image], 0))
        combine[image] = over_slots[image]
    grads_copy.wait()
    for image in range(images):
        value = dot(over_slots[image].astype(LOW), grads_v[image], 1, 0)
        put(rows, KINDS * image + 1, slots, stride, value)
    sent[...] = packed(rows)
    for copy in weight_copies:
        copy.wait()


def gather(tokens, params, grads, w_in, w_out, first):
    images, length, width = tokens.shape
    slots = params.shape[0]
    weights = shaped((images, slots, length), WIDE)
    rows = (slots * images * KINDS, width)
    return call(
        gather_kernel,
        "gather_slots",
        ROOMY,
        6 * images * slots * length * width,
        4 * images * length * width,
        2 * images * slots * length,
        out_shape=(
            shaped(rows, LOW),
            weights,
            weights,
            shaped((width, first), LOW),
            shaped((first, width), LOW),
        ),
        in_specs=[PLACE] * 5,
        out_specs=(WHOLE,) * 5,
        scratch_shapes=[
            pltpu.VMEM(tokens.shape, LOW),
            pltpu.VMEM(grads.shape, LOW),
            pltpu.VMEM(params.shape, LOW),
            scratch_rows(rows),
            pltpu.SemaphoreType.DMA((6,)),
        ],
    )(tokens, far(params), grads, w_in, w_out)


def chunks_of(first, hidden, tile):
    edges = [*range(first, hidden, tile), hidden]
    return [slice(low, high) for low, high in zip(edges, edges[1:])]


def start_weights(w_in, w_out, w_in_v, w_out_v, sems, chunks):
    copies = []
    for chunk, units in enumerate(chunks):
        copies.append(
            (
                start_copy(w_in.at[:, units], w_in_v.at[:, units], sems.at[0, chunk]),
                start_copy(w_out.at[units, :], w_out_v.at[units, :], sems.at[1, chunk]),
            )
        )
    return copies


def weight_scratch(width, hidden, chunks):
    return [
        pltpu.VMEM((width, hidden), LOW),
        pltpu.VMEM((hidden, width), LOW),
        pltpu.SemaphoreType.DMA((2, len(chunks))),
    ]


def expert_kernel(
    chunks, rows, first_in, first_out, w_in, w_out, back, acts, hidden, mark,
    w_in_v, w_out_v, sems, wide,
):
    del mark
    copies = start_weights(w_in, w_out, w_in_v, w_out_v, sems, chunks)
    count = rows.shape[0] // KINDS
    load_rows(wide, rows[...])
    rows_in = take(wide, 0, count, KINDS).astype(LOW)
    rows_grad = take(wide, 1, count, KINDS).astype(LOW)

    def first_products(weight_in, weight_out):
        return dot(rows_in, weight_in, 1, 0), dot(rows_grad, weight_out, 1, 1)

    def second_products(held, weight_in, weight_out):
        return dot(held[0], weight_out, 1, 0), dot(held[1], weight_in, 1, 1)

    def hold(preact, d_acts, units):
        values, slope = gelu_parts(preact)
        held = (values.astype(LOW), (d_acts * slope).astype(LOW))
        acts[:, units], hidden[:, units] = held
        return held

    held = hold(
        *first_products(first_in[...], first_out[...]), slice(0, first_out.shape[0])
    )
    out, d_in = second_products(held, first_in[...], first_out[...])
    before = None
    for pair, units in zip([*copies, None], [*chunks, None]):
        if pair is not None:
            for copy in pair:
                copy.wait()
            products = first_products(w_in_v[:, units], w_out_v[units, :])
        if before is not None:
            parts = second_products(held, w_in_v[:, before], w_out_v[before, :])
            out, d_in = out + parts[0], d_in + parts[1]
        if pair is not None:
            held = hold(*products, units)
        before = units
    put(wide, 0, count, KINDS, out)
    put(wide, 1, count, KINDS, d_in)
    back[...] = packed(wide)


def expert(rows, first_in, first_out, w_in, w_out, tile):
    total, width = rows.shape
    hidden = w_in.shape[1]
    count = total // KINDS
    kept = shaped((count, hidden), LOW)
    chunks = chunks_of(first_out.shape[0], hidden, tile)
    return call(
        functools.partial(expert_kernel, chunks),
        "expert_rows",
        ROOMY,
        8 * count * hidden * width,
        4 * hidden * width,
        count * hidden,
        out_shape=(shaped(rows.shape, LOW), kept, kept, MARK),
        in_specs=[WHOLE, WHOLE, WHOLE, PLACE, PLACE],
        out_specs=(WHOLE, WHOLE, WHOLE, PLACE),
        scratch_shapes=[*weight_scratch(width, hidden, chunks), scratch_rows(rows.shape)],
    )(rows, first_in, first_out, w_in, w_out)


def replica_kernel(
    chunks, mine, after, rows, other_rows, acts, hidden, w_in, w_out, tokens,
    grad_in, grad_out, tokens_half, mark,
    w_in_v, w_out_v, grad_in_v, grad_out_v, wide, grads, turned, sems, in_sems, out_sems, half_sem,
):
    del after, mark
    count = rows.shape[0] // KINDS
    size = w_in.shape[1]
    half = grad_out.shape[0]
    spans, copies = [], []
    for chunk, units in enumerate(chunks):
        start = pl.multiple_of(lax.rem(mine[0] * half + units.start, size), LANES)
        span = pl.ds(start, units.stop - units.start)
        spans.append(span)
        copies.append(
            (
                start_copy(w_in.at[:, span], w_in_v.at[:, units], sems.at[0, chunk]),
                start_copy(w_out.at[span, :], w_out_v.at[units, :], sems.at[1, chunk]),
            )
        )
    results = [
        start_copy(tokens.at[pl.ds(0, tokens_half.shape[0])], tokens_half, half_sem.at[0])
    ]
    left, right = [], []
    tiles = turned.shape[0] // LANES
    for source in (rows, other_rows):
        load_rows(wide, source[...])
        left.append(take(wide, 0, count, KINDS, mine[0] * tiles, tiles))
        right.append(take(wide, 1, count, KINDS))
    turned[...] = jnp.concatenate(left, axis=0).T.astype(LOW)
    grads[...] = jnp.concatenate(right, axis=0).astype(LOW)
    rows_in = take(wide, 0, count, KINDS).astype(LOW)
    rows_grad = right[1].astype(LOW)
    before = None
    for chunk in range(len(chunks) + 1):
        if chunk < len(chunks):
            units = chunks[chunk]
            for copy in copies[chunk]:
                copy.wait()
            preact = dot(rows_in, w_in_v[:, units], 1, 0)
            d_acts = dot(rows_grad, w_out_v[units, :], 1, 1)
        if before is not None:
            past, span, all_acts, all_hidden = before
            grad_in_v[:, past] = dot(turned[...], all_hidden, 1, 0).astype(LOW)
            results.append(
                start_copy(grad_in_v.at[:, past], grad_in.at[:, span], in_sems.at[chunk - 1])
            )
            if past.stop <= half:
                grad_out_v[past, :] = dot(all_acts, grads[...], 0, 0).astype(LOW)
                results.append(
                    start_copy(
                        grad_out_v.at[past, :], grad_out.at[past, :], out_sems.at[chunk - 1]
                    )
                )
        if chunk < len(chunks):
            span = spans[chunk]
            values, slope = gelu_parts(preact)
            all_acts = jnp.concatenate([acts[:, span], values.astype(LOW)], axis=0)
            all_hidden = jnp.concatenate(
                [hidden[:, span], (d_acts * slope).astype(LOW)], axis=0
            )
            before = (units, span, all_acts, all_hidden)
    for copy in results:
        copy.wait()


def replica_grads(
    mine, after, rows, other_rows, acts, hidden, w_in, w_out, tokens, replicas, tile
):
    total, width = rows.shape
    size = w_in.shape[1]
    half = size // replicas
    count = total // KINDS
    chunks = [
        slice(part * half + units.start, part * half + units.stop)
        for part in range(replicas)
        for units in chunks_of(0, half, tile)
    ]
    return call(
        functools.partial(replica_kernel, chunks),
        "replica_grads",
        ROOMY,
        64 * count * size * width,
        32 * size * width,
        count * size,
        out_shape=(
            shaped((width // replicas, size), LOW),
            shaped((half, width), LOW),
            shaped((tokens.shape[0] // 2, *tokens.shape[1:]), LOW),
            MARK,
        ),
        in_specs=[pl.BlockSpec(memory_space=pltpu.SMEM), PLACE]
        + [WHOLE] * 4
        + [PLACE] * 3,
        out_specs=(PLACE, PLACE, WHOLE, PLACE),
        scratch_shapes=[
            *weight_scratch(width, size, chunks)[:2],
            pltpu.VMEM((width // replicas, size), LOW),
            pltpu.VMEM((half, width), LOW),
            scratch_rows((total, width)),
            pltpu.VMEM((2 * count, width), LOW),
            pltpu.VMEM((width // replicas, 2 * count), LOW),
            pltpu.SemaphoreType.DMA((2, len(chunks))),
            pltpu.SemaphoreType.DMA((len(chunks),)),
            pltpu.SemaphoreType.DMA((len(chunks),)),
            pltpu.SemaphoreType.DMA((1,)),
        ],
    )(mine, after, rows, other_rows, acts, hidden, w_in, w_out, far(tokens))


def logits_kernel(
    after, back, tokens, tokens_half, params, grads, dispatch, combine, left, right, local, mark,
    tokens_v, grads_v, wide, sems,
):
    del after, mark
    images, slots, _ = dispatch.shape
    ready = tokens_half.shape[0]
    tokens_copy = start_copy(tokens.at[pl.ds(ready, images - ready)], tokens_v, sems.at[0])
    grads_copy = start_copy(grads, grads_v, sems.at[1])

    def tokens_of(image):
        return tokens_half[image] if image < ready else tokens_v[image - ready]

    load_rows(wide, back[...])
    stride = KINDS * images
    d_slot_in = []
    for image in range(images):
        d_slot_in.append(take(wide, KINDS * image + 1, slots, stride).astype(LOW))
        right[image, :slots, :] = d_slot_in[image]
        right[image, slots:, :] = params[...]
        left[image, :slots, :] = dispatch[image].astype(LOW)
    parts = []
    for image in range(images):
        if image == ready:
            tokens_copy.wait()
        weights = dispatch[image]
        d_dispatch = dot(d_slot_in[image], tokens_of(image), 1, 1)
        parts.append(
            weights * (d_dispatch - jnp.sum(weights * d_dispatch, axis=1, keepdims=True))
        )
    grads_copy.wait()
    total = None
    for image in range(images):
        slot_out = take(wide, KINDS * image, slots, stride).astype(LOW)
        weights = combine[image]
        d_combine = dot(slot_out, grads_v[image], 1, 1)
        d_logits = parts[image] + weights * (
            d_combine - jnp.sum(weights * d_combine, axis=0, keepdims=True)
        )
        low = d_logits.astype(LOW)
        left[image, slots:, :] = low
        part = dot(low, tokens_of(image), 1, 0)
        total = part if image == 0 else total + part
    local[...] = total.astype(LOW)


def logits_grads(after, back, tokens, tokens_half, params, grads, dispatch, combine):
    images, length, width = tokens.shape
    slots = params.shape[0]
    return call(
        logits_kernel,
        "logits_grads",
        ROOMY,
        6 * images * slots * length * width,
        4 * images * length * width,
        out_shape=(
            shaped((images, 2 * slots, length), LOW),
            shaped((images, 2 * slots, width), LOW),
            shaped(params.shape, LOW),
            MARK,
        ),
        in_specs=[PLACE, WHOLE, PLACE, WHOLE, WHOLE, PLACE, WHOLE, WHOLE],
        out_specs=(WHOLE, WHOLE, WHOLE, PLACE),
        scratch_shapes=[
            pltpu.VMEM((images - tokens_half.shape[0], length, width), LOW),
            pltpu.VMEM(grads.shape, LOW),
            scratch_rows(back.shape),
            pltpu.SemaphoreType.DMA((2,)),
        ],
    )(after, back, far(tokens), tokens_half, params, far(grads), dispatch, combine)


def tokens_kernel(after, left, right, out, mark):
    del after, mark
    out[0] = dot(left[0], right[0], 0, 0).astype(LOW)


def tokens_grads(after, left, right):
    images, deep, length = left.shape
    width = right.shape[2]
    return call(
        tokens_kernel,
        "tokens_grads",
        SHARED,
        2 * images * deep * length * width,
        2 * images * length * width,
        grid=(images,),
        out_shape=(shaped((images, length, width), LOW), MARK),
        in_specs=[
            PLACE,
            pl.BlockSpec((1, deep, length), lambda i: (i, 0, 0)),
            pl.BlockSpec((1, deep, width), lambda i: (i, 0, 0)),
        ],
        out_specs=(pl.BlockSpec((1, length, width), lambda i: (i, 0, 0)), PLACE),
    )(after, left, right)


def add_kernel(after, *refs):
    del after
    terms = [ref[...].astype(WIDE) for ref in refs[:-2]]
    while len(terms) > 1:
        terms = [left + right for left, right in zip(terms[::2], terms[1::2])]
    refs[-2][...] = terms[0].astype(refs[-2].dtype)


def add(after, terms, dtype):
    return call(
        add_kernel,
        "add_terms",
        SHARED,
        len(terms) * terms[0].size,
        2 * len(terms) * terms[0].size,
        out_shape=(shaped(terms[0].shape, dtype), MARK),
        in_specs=[PLACE] + [WHOLE] * len(terms),
        out_specs=(WHOLE, PLACE),
    )(after, *terms)


def terms_of_group(array, bits):
    axes = ("rep", "exp")
    distances = [0]
    for bit in bits:
        distances += [distance + (1 << bit) for distance in distances]
    count = lax.axis_size(axes)
    return [array] + [
        lax.ppermute(array, axes, [(i, i ^ distance) for i in range(count)])
        for distance in distances[1:]
    ]


def exchange(rows, axes):
    return lax.all_to_all(rows, axes, split_axis=0, concat_axis=0, tiled=True)


def body(tokens, slot_params, expert_in, expert_out, grad_out):
    params = slot_params.T
    weights = (expert_in[0], expert_out[0])
    replicas = lax.axis_size("rep")
    mine = lax.axis_index("rep").astype(jnp.int32).reshape(1)

    sent, dispatch, combine, *first = gather(tokens, params, grad_out, *weights, 256)
    rows = exchange(sent, "exp")
    other_rows = lax.ppermute(rows, "rep", [(i, (i + 1) % replicas) for i in range(replicas)])
    back, acts, hidden, after = expert(rows, *first, *weights, 512)
    back = exchange(back, "exp")
    grad_in, grad_outer, tokens_half, after = replica_grads(
        mine, after, rows, other_rows, acts, hidden, *weights, tokens, replicas, 512
    )
    left, right, local, after = logits_grads(
        after, back, tokens, tokens_half, params, grad_out, dispatch, combine
    )
    exp_bits = lax.axis_size("exp").bit_length() - 1
    rep_bits = replicas.bit_length() - 1
    groups = [(0, 1, *range(exp_bits, exp_bits + rep_bits))]
    groups += [range(bit, min(bit + 2, exp_bits)) for bit in range(2, exp_bits, 2)]
    for bits in groups[:-1]:
        local, after = add(after, terms_of_group(local, bits), LOW)
    terms = terms_of_group(local, groups[-1])
    grad_tokens, after = tokens_grads(after, left, right)
    grad_params, _ = add(after, terms, WIDE)
    return (grad_tokens, grad_params.T, grad_in[None], grad_outer[None])


def solution(mesh):
    in_specs = (
        P(("rep", "exp"), None, None),
        P(),
        P("exp", None, None),
        P("exp", None, None),
        P(("rep", "exp"), None, None),
    )
    out_specs = (P(("rep", "exp"), None, None), P(), P("exp", "rep", None), P("exp", "rep", None))
    return jax.shard_map(body, mesh=mesh, in_specs=in_specs, out_specs=out_specs, check_vma=False)
```

```python
import functools
import math

import jax
import jax.numpy as jnp
from jax import lax
from jax.experimental import pallas as pl
from jax.experimental.pallas import tpu as pltpu
from jax.sharding import PartitionSpec as P

GELU_C = math.sqrt(2.0 / math.pi)
CUBIC = 0.044715
LOW = jnp.bfloat16
WIDE = jnp.float32
LANES = 128
KINDS = 2
SHARED = 52 * 1024 * 1024
ROOMY = 50 * 1024 * 1024
WHOLE = pl.BlockSpec(memory_space=pltpu.VMEM)
PLACE = pl.BlockSpec(memory_space=pl.ANY)


def call(kernel, name, grant, flops, nbytes, exps=0, **kwargs):
    return pl.pallas_call(
        kernel,
        name=name,
        compiler_params=pltpu.CompilerParams(vmem_limit_bytes=grant),
        cost_estimate=pl.CostEstimate(
            flops=flops, bytes_accessed=nbytes, transcendentals=exps
        ),
        **kwargs,
    )


def shaped(shape, dtype):
    return jax.ShapeDtypeStruct(shape, dtype)


MARK = shaped((8, LANES), WIDE)


def gelu_parts(values):
    square = values * values
    tangent = jnp.tanh(GELU_C * (values + CUBIC * square * values))
    half = 0.5 * (1.0 + tangent)
    slope = half + 0.5 * values * (1.0 - tangent * tangent) * GELU_C * (1.0 + 3.0 * CUBIC * square)
    return values * half, slope


def dot(left, right, over_left, over_right):
    return lax.dot_general(
        left, right, (((over_left,), (over_right,)), ((), ())), preferred_element_type=WIDE
    )


def softmax(values, axis):
    raised = jnp.exp(values - jnp.max(values, axis=axis, keepdims=True))
    return raised / jnp.sum(raised, axis=axis, keepdims=True)


def scratch_rows(shape):
    return pltpu.VMEM((shape[1] // LANES, shape[0], LANES), WIDE)


def load_rows(ref, array):
    for tile in range(ref.shape[0]):
        ref[tile] = array[:, tile * LANES : (tile + 1) * LANES].astype(WIDE)


def packed(ref):
    return jnp.concatenate([ref[tile] for tile in range(ref.shape[0])], axis=1).astype(LOW)


def take(ref, start, count, stride, first=0, tiles=None):
    tiles = ref.shape[0] if tiles is None else tiles
    picked = [ref[first + tile, pl.ds(start, count, stride=stride), :] for tile in range(tiles)]
    return jnp.concatenate(picked, axis=1)


def put(ref, start, count, stride, array):
    for tile in range(ref.shape[0]):
        ref[tile, pl.ds(start, count, stride=stride), :] = array[
            :, tile * LANES : (tile + 1) * LANES
        ]


def start_copy(source, target, sem):
    copy = pltpu.make_async_copy(source, target, sem)
    copy.start()
    return copy


def far(array):
    return pltpu.with_memory_space_constraint(array, pltpu.HBM)


def start_halves(source, target, sems):
    images = source.shape[0]
    parts = []
    for index, (first, last) in enumerate(((0, images // 2), (images // 2, images))):
        part = pl.ds(first, last - first)
        copy = start_copy(source.at[part], target.at[part], sems.at[index])
        parts.append((copy, range(first, last)))
    return parts


def gather_kernel(
    tokens, params, grads, w_in, w_out, sent, dispatch, combine, first_in, first_out,
    tokens_v, grads_v, rows, sems,
):
    images = tokens.shape[0]
    slots = params.shape[0]
    stride = KINDS * images
    halves = start_halves(tokens, tokens_v, sems)
    grads_copy = start_copy(grads, grads_v, sems.at[2])
    units = slice(0, first_out.shape[0])
    weight_copies = (
        start_copy(w_in.at[:, units], first_in, sems.at[3]),
        start_copy(w_out.at[units, :], first_out, sems.at[4]),
    )
    logits = []
    for copy, half in halves:
        copy.wait()
        logits += [dot(params[...], tokens_v[image], 1, 1) for image in half]
    over_slots = []
    for image in range(images):
        over_tokens = softmax(logits[image], 1)
        dispatch[image] = over_tokens
        put(
            rows, KINDS * image, slots, stride, dot(over_tokens.astype(LOW), tokens_v[image], 1, 0)
        )
        over_slots.append(softmax(logits[image], 0))
        combine[image] = over_slots[image]
    grads_copy.wait()
    for image in range(images):
        value = dot(over_slots[image].astype(LOW), grads_v[image], 1, 0)
        put(rows, KINDS * image + 1, slots, stride, value)
    sent[...] = packed(rows)
    for copy in weight_copies:
        copy.wait()


def gather(tokens, params, grads, w_in, w_out, first):
    images, length, width = tokens.shape
    slots = params.shape[0]
    weights = shaped((images, slots, length), WIDE)
    rows = (slots * images * KINDS, width)
    return call(
        gather_kernel,
        "gather_slots",
        ROOMY,
        6 * images * slots * length * width,
        4 * images * length * width,
        2 * images * slots * length,
        out_shape=(
            shaped(rows, LOW),
            weights,
            weights,
            shaped((width, first), LOW),
            shaped((first, width), LOW),
        ),
        in_specs=[PLACE, WHOLE, PLACE, PLACE, PLACE],
        out_specs=(WHOLE,) * 5,
        scratch_shapes=[
            pltpu.VMEM(tokens.shape, LOW),
            pltpu.VMEM(grads.shape, LOW),
            scratch_rows(rows),
            pltpu.SemaphoreType.DMA((5,)),
        ],
    )(tokens, params, grads, w_in, w_out)


def chunks_of(first, hidden, tile):
    edges = [*range(first, hidden, tile), hidden]
    return [slice(low, high) for low, high in zip(edges, edges[1:])]


def start_weights(w_in, w_out, w_in_v, w_out_v, sems, chunks):
    copies = []
    for chunk, units in enumerate(chunks):
        copies.append(
            (
                start_copy(w_in.at[:, units], w_in_v.at[:, units], sems.at[0, chunk]),
                start_copy(w_out.at[units, :], w_out_v.at[units, :], sems.at[1, chunk]),
            )
        )
    return copies


def weight_scratch(width, hidden, chunks):
    return [
        pltpu.VMEM((width, hidden), LOW),
        pltpu.VMEM((hidden, width), LOW),
        pltpu.SemaphoreType.DMA((2, len(chunks))),
    ]


def expert_kernel(
    chunks, rows, first_in, first_out, w_in, w_out, back, acts, hidden, mark,
    w_in_v, w_out_v, sems, wide,
):
    del mark
    copies = start_weights(w_in, w_out, w_in_v, w_out_v, sems, chunks)
    count = rows.shape[0] // KINDS
    load_rows(wide, rows[...])
    rows_in = take(wide, 0, count, KINDS).astype(LOW)
    rows_grad = take(wide, 1, count, KINDS).astype(LOW)

    def first_products(weight_in, weight_out):
        return dot(rows_in, weight_in, 1, 0), dot(rows_grad, weight_out, 1, 1)

    def second_products(held, weight_in, weight_out):
        return dot(held[0], weight_out, 1, 0), dot(held[1], weight_in, 1, 1)

    def hold(preact, d_acts, units):
        values, slope = gelu_parts(preact)
        held = (values.astype(LOW), (d_acts * slope).astype(LOW))
        acts[:, units], hidden[:, units] = held
        return held

    held = hold(
        *first_products(first_in[...], first_out[...]), slice(0, first_out.shape[0])
    )
    out, d_in = second_products(held, first_in[...], first_out[...])
    before = None
    for pair, units in zip([*copies, None], [*chunks, None]):
        if pair is not None:
            for copy in pair:
                copy.wait()
            products = first_products(w_in_v[:, units], w_out_v[units, :])
        if before is not None:
            parts = second_products(held, w_in_v[:, before], w_out_v[before, :])
            out, d_in = out + parts[0], d_in + parts[1]
        if pair is not None:
            held = hold(*products, units)
        before = units
    put(wide, 0, count, KINDS, out)
    put(wide, 1, count, KINDS, d_in)
    back[...] = packed(wide)


def expert(rows, first_in, first_out, w_in, w_out, tile):
    total, width = rows.shape
    hidden = w_in.shape[1]
    count = total // KINDS
    kept = shaped((count, hidden), LOW)
    chunks = chunks_of(first_out.shape[0], hidden, tile)
    return call(
        functools.partial(expert_kernel, chunks),
        "expert_rows",
        ROOMY,
        8 * count * hidden * width,
        4 * hidden * width,
        count * hidden,
        out_shape=(shaped(rows.shape, LOW), kept, kept, MARK),
        in_specs=[WHOLE, WHOLE, WHOLE, PLACE, PLACE],
        out_specs=(WHOLE, WHOLE, WHOLE, PLACE),
        scratch_shapes=[*weight_scratch(width, hidden, chunks), scratch_rows(rows.shape)],
    )(rows, first_in, first_out, w_in, w_out)


def replica_kernel(
    chunks, mine, after, rows, other_rows, acts, hidden, w_in, w_out, tokens,
    grad_in, grad_out, tokens_half, mark,
    w_in_v, w_out_v, grad_in_v, grad_out_v, wide, grads, turned, sems, in_sems, out_sems, half_sem,
):
    del after, mark
    count = rows.shape[0] // KINDS
    size = w_in.shape[1]
    half = grad_out.shape[0]
    spans, copies = [], []
    for chunk, units in enumerate(chunks):
        start = pl.multiple_of(lax.rem(mine[0] * half + units.start, size), LANES)
        span = pl.ds(start, units.stop - units.start)
        spans.append(span)
        copies.append(
            (
                start_copy(w_in.at[:, span], w_in_v.at[:, units], sems.at[0, chunk]),
                start_copy(w_out.at[span, :], w_out_v.at[units, :], sems.at[1, chunk]),
            )
        )
    results = [
        start_copy(tokens.at[pl.ds(0, tokens_half.shape[0])], tokens_half, half_sem.at[0])
    ]
    left, right = [], []
    tiles = turned.shape[0] // LANES
    for source in (rows, other_rows):
        load_rows(wide, source[...])
        left.append(take(wide, 0, count, KINDS, mine[0] * tiles, tiles))
        right.append(take(wide, 1, count, KINDS))
    turned[...] = jnp.concatenate(left, axis=0).T.astype(LOW)
    grads[...] = jnp.concatenate(right, axis=0).astype(LOW)
    rows_in = take(wide, 0, count, KINDS).astype(LOW)
    rows_grad = right[1].astype(LOW)
    before = None
    for chunk in range(len(chunks) + 1):
        if chunk < len(chunks):
            units = chunks[chunk]
            for copy in copies[chunk]:
                copy.wait()
            preact = dot(rows_in, w_in_v[:, units], 1, 0)
            d_acts = dot(rows_grad, w_out_v[units, :], 1, 1)
        if before is not None:
            past, span, all_acts, all_hidden = before
            grad_in_v[:, past] = dot(turned[...], all_hidden, 1, 0).astype(LOW)
            results.append(
                start_copy(grad_in_v.at[:, past], grad_in.at[:, span], in_sems.at[chunk - 1])
            )
            if past.stop <= half:
                grad_out_v[past, :] = dot(all_acts, grads[...], 0, 0).astype(LOW)
                results.append(
                    start_copy(
                        grad_out_v.at[past, :], grad_out.at[past, :], out_sems.at[chunk - 1]
                    )
                )
        if chunk < len(chunks):
            span = spans[chunk]
            values, slope = gelu_parts(preact)
            all_acts = jnp.concatenate([acts[:, span], values.astype(LOW)], axis=0)
            all_hidden = jnp.concatenate(
                [hidden[:, span], (d_acts * slope).astype(LOW)], axis=0
            )
            before = (units, span, all_acts, all_hidden)
    for copy in results:
        copy.wait()


def replica_grads(
    mine, after, rows, other_rows, acts, hidden, w_in, w_out, tokens, replicas, tile
):
    total, width = rows.shape
    size = w_in.shape[1]
    half = size // replicas
    count = total // KINDS
    chunks = [
        slice(part * half + units.start, part * half + units.stop)
        for part in range(replicas)
        for units in chunks_of(0, half, tile)
    ]
    return call(
        functools.partial(replica_kernel, chunks),
        "replica_grads",
        ROOMY,
        64 * count * size * width,
        32 * size * width,
        count * size,
        out_shape=(
            shaped((width // replicas, size), LOW),
            shaped((half, width), LOW),
            shaped((tokens.shape[0] // 2, *tokens.shape[1:]), LOW),
            MARK,
        ),
        in_specs=[pl.BlockSpec(memory_space=pltpu.SMEM), PLACE]
        + [WHOLE] * 4
        + [PLACE] * 3,
        out_specs=(PLACE, PLACE, WHOLE, PLACE),
        scratch_shapes=[
            *weight_scratch(width, size, chunks)[:2],
            pltpu.VMEM((width // replicas, size), LOW),
            pltpu.VMEM((half, width), LOW),
            scratch_rows((total, width)),
            pltpu.VMEM((2 * count, width), LOW),
            pltpu.VMEM((width // replicas, 2 * count), LOW),
            pltpu.SemaphoreType.DMA((2, len(chunks))),
            pltpu.SemaphoreType.DMA((len(chunks),)),
            pltpu.SemaphoreType.DMA((len(chunks),)),
            pltpu.SemaphoreType.DMA((1,)),
        ],
    )(mine, after, rows, other_rows, acts, hidden, w_in, w_out, far(tokens))


def logits_kernel(
    after, back, tokens, tokens_half, params, grads, dispatch, combine, left, right, local, mark,
    tokens_v, grads_v, wide, sems,
):
    del after, mark
    images, slots, _ = dispatch.shape
    ready = tokens_half.shape[0]
    tokens_copy = start_copy(tokens.at[pl.ds(ready, images - ready)], tokens_v, sems.at[0])
    grads_copy = start_copy(grads, grads_v, sems.at[1])

    def tokens_of(image):
        return tokens_half[image] if image < ready else tokens_v[image - ready]

    load_rows(wide, back[...])
    stride = KINDS * images
    d_slot_in = []
    for image in range(images):
        d_slot_in.append(take(wide, KINDS * image + 1, slots, stride).astype(LOW))
        right[image, :slots, :] = d_slot_in[image]
        right[image, slots:, :] = params[...]
        left[image, :slots, :] = dispatch[image].astype(LOW)
    parts = []
    for image in range(images):
        if image == ready:
            tokens_copy.wait()
        weights = dispatch[image]
        d_dispatch = dot(d_slot_in[image], tokens_of(image), 1, 1)
        parts.append(
            weights * (d_dispatch - jnp.sum(weights * d_dispatch, axis=1, keepdims=True))
        )
    grads_copy.wait()
    total = None
    for image in range(images):
        slot_out = take(wide, KINDS * image, slots, stride).astype(LOW)
        weights = combine[image]
        d_combine = dot(slot_out, grads_v[image], 1, 1)
        d_logits = parts[image] + weights * (
            d_combine - jnp.sum(weights * d_combine, axis=0, keepdims=True)
        )
        low = d_logits.astype(LOW)
        left[image, slots:, :] = low
        part = dot(low, tokens_of(image), 1, 0)
        total = part if image == 0 else total + part
    local[...] = total.astype(LOW)


def logits_grads(after, back, tokens, tokens_half, params, grads, dispatch, combine):
    images, length, width = tokens.shape
    slots = params.shape[0]
    return call(
        logits_kernel,
        "logits_grads",
        ROOMY,
        6 * images * slots * length * width,
        4 * images * length * width,
        out_shape=(
            shaped((images, 2 * slots, length), LOW),
            shaped((images, 2 * slots, width), LOW),
            shaped(params.shape, LOW),
            MARK,
        ),
        in_specs=[PLACE, WHOLE, PLACE, WHOLE, WHOLE, PLACE, WHOLE, WHOLE],
        out_specs=(WHOLE, WHOLE, WHOLE, PLACE),
        scratch_shapes=[
            pltpu.VMEM((images - tokens_half.shape[0], length, width), LOW),
            pltpu.VMEM(grads.shape, LOW),
            scratch_rows(back.shape),
            pltpu.SemaphoreType.DMA((2,)),
        ],
    )(after, back, far(tokens), tokens_half, params, far(grads), dispatch, combine)


def tokens_kernel(after, left, right, out, mark):
    del after, mark
    out[0] = dot(left[0], right[0], 0, 0).astype(LOW)


def tokens_grads(after, left, right):
    images, deep, length = left.shape
    width = right.shape[2]
    return call(
        tokens_kernel,
        "tokens_grads",
        SHARED,
        2 * images * deep * length * width,
        2 * images * length * width,
        grid=(images,),
        out_shape=(shaped((images, length, width), LOW), MARK),
        in_specs=[
            PLACE,
            pl.BlockSpec((1, deep, length), lambda i: (i, 0, 0)),
            pl.BlockSpec((1, deep, width), lambda i: (i, 0, 0)),
        ],
        out_specs=(pl.BlockSpec((1, length, width), lambda i: (i, 0, 0)), PLACE),
    )(after, left, right)


def add_kernel(after, *refs):
    del after
    terms = [ref[...].astype(WIDE) for ref in refs[:-2]]
    while len(terms) > 1:
        terms = [left + right for left, right in zip(terms[::2], terms[1::2])]
    refs[-2][...] = terms[0].astype(refs[-2].dtype)


def add(after, terms, dtype):
    return call(
        add_kernel,
        "add_terms",
        SHARED,
        len(terms) * terms[0].size,
        2 * len(terms) * terms[0].size,
        out_shape=(shaped(terms[0].shape, dtype), MARK),
        in_specs=[PLACE] + [WHOLE] * len(terms),
        out_specs=(WHOLE, PLACE),
    )(after, *terms)


def terms_of_group(array, bits):
    axes = ("rep", "exp")
    distances = [0]
    for bit in bits:
        distances += [distance + (1 << bit) for distance in distances]
    count = lax.axis_size(axes)
    return [array] + [
        lax.ppermute(array, axes, [(i, i ^ distance) for i in range(count)])
        for distance in distances[1:]
    ]


def exchange(rows, axes):
    return lax.all_to_all(rows, axes, split_axis=0, concat_axis=0, tiled=True)


def body(tokens, slot_params, expert_in, expert_out, grad_out):
    params = slot_params.T
    weights = (expert_in[0], expert_out[0])
    replicas = lax.axis_size("rep")
    mine = lax.axis_index("rep").astype(jnp.int32).reshape(1)

    sent, dispatch, combine, *first = gather(tokens, params, grad_out, *weights, 256)
    rows = exchange(sent, "exp")
    other_rows = lax.ppermute(rows, "rep", [(i, (i + 1) % replicas) for i in range(replicas)])
    back, acts, hidden, after = expert(rows, *first, *weights, 512)
    back = exchange(back, "exp")
    grad_in, grad_outer, tokens_half, after = replica_grads(
        mine, after, rows, other_rows, acts, hidden, *weights, tokens, replicas, 512
    )
    left, right, local, after = logits_grads(
        after, back, tokens, tokens_half, params, grad_out, dispatch, combine
    )
    exp_bits = lax.axis_size("exp").bit_length() - 1
    rep_bits = replicas.bit_length() - 1
    groups = [(0, 1, *range(exp_bits, exp_bits + rep_bits))]
    groups += [range(bit, min(bit + 2, exp_bits)) for bit in range(2, exp_bits, 2)]
    for bits in groups[:-1]:
        local, after = add(after, terms_of_group(local, bits), LOW)
    terms = terms_of_group(local, groups[-1])
    grad_tokens, after = tokens_grads(after, left, right)
    grad_params, _ = add(after, terms, WIDE)
    return (grad_tokens, grad_params.T, grad_in[None], grad_outer[None])


def solution(mesh):
    in_specs = (
        P(("rep", "exp"), None, None),
        P(),
        P("exp", None, None),
        P("exp", None, None),
        P(("rep", "exp"), None, None),
    )
    out_specs = (P(("rep", "exp"), None, None), P(), P("exp", "rep", None), P("exp", "rep", None))
    return jax.shard_map(body, mesh=mesh, in_specs=in_specs, out_specs=out_specs, check_vma=False)
```

```python
import functools
import math

import jax
import jax.numpy as jnp
from jax import lax
from jax.experimental import pallas as pl
from jax.experimental.pallas import tpu as pltpu
from jax.sharding import PartitionSpec as P

GELU_C = math.sqrt(2.0 / math.pi)
CUBIC = 0.044715
LOW = jnp.bfloat16
WIDE = jnp.float32
LANES = 128
KINDS = 2
SHARED = 52 * 1024 * 1024
ROOMY = 50 * 1024 * 1024
WHOLE = pl.BlockSpec(memory_space=pltpu.VMEM)
PLACE = pl.BlockSpec(memory_space=pl.ANY)


def call(kernel, name, grant, flops, nbytes, exps=0, **kwargs):
    return pl.pallas_call(
        kernel,
        name=name,
        compiler_params=pltpu.CompilerParams(vmem_limit_bytes=grant),
        cost_estimate=pl.CostEstimate(
            flops=flops, bytes_accessed=nbytes, transcendentals=exps
        ),
        **kwargs,
    )


def shaped(shape, dtype):
    return jax.ShapeDtypeStruct(shape, dtype)


MARK = shaped((8, LANES), WIDE)


def gelu_parts(values):
    square = values * values
    tangent = jnp.tanh(GELU_C * (values + CUBIC * square * values))
    half = 0.5 * (1.0 + tangent)
    slope = half + 0.5 * values * (1.0 - tangent * tangent) * GELU_C * (1.0 + 3.0 * CUBIC * square)
    return values * half, slope


def dot(left, right, over_left, over_right):
    return lax.dot_general(
        left, right, (((over_left,), (over_right,)), ((), ())), preferred_element_type=WIDE
    )


def softmax(values, axis):
    raised = jnp.exp(values - jnp.max(values, axis=axis, keepdims=True))
    return raised / jnp.sum(raised, axis=axis, keepdims=True)


def scratch_rows(shape):
    return pltpu.VMEM((shape[1] // LANES, shape[0], LANES), WIDE)


def load_rows(ref, array):
    for tile in range(ref.shape[0]):
        ref[tile] = array[:, tile * LANES : (tile + 1) * LANES].astype(WIDE)


def packed(ref):
    return jnp.concatenate([ref[tile] for tile in range(ref.shape[0])], axis=1).astype(LOW)


def take(ref, start, count, stride, first=0, tiles=None):
    tiles = ref.shape[0] if tiles is None else tiles
    picked = [ref[first + tile, pl.ds(start, count, stride=stride), :] for tile in range(tiles)]
    return jnp.concatenate(picked, axis=1)


def put(ref, start, count, stride, array):
    for tile in range(ref.shape[0]):
        ref[tile, pl.ds(start, count, stride=stride), :] = array[
            :, tile * LANES : (tile + 1) * LANES
        ]


def start_copy(source, target, sem):
    copy = pltpu.make_async_copy(source, target, sem)
    copy.start()
    return copy


def far(array):
    return pltpu.with_memory_space_constraint(array, pltpu.HBM)


def start_halves(source, target, sems):
    images = source.shape[0]
    parts = []
    for index, (first, last) in enumerate(((0, images // 2), (images // 2, images))):
        part = pl.ds(first, last - first)
        copy = start_copy(source.at[part], target.at[part], sems.at[index])
        parts.append((copy, range(first, last)))
    return parts


def gather_kernel(
    tokens, params, grads, w_in, w_out, sent, dispatch, combine, first_in, first_out,
    tokens_v, grads_v, rows, sems,
):
    images = tokens.shape[0]
    slots = params.shape[0]
    stride = KINDS * images
    halves = start_halves(tokens, tokens_v, sems)
    grads_copy = start_copy(grads, grads_v, sems.at[2])
    units = slice(0, first_out.shape[0])
    weight_copies = (
        start_copy(w_in.at[:, units], first_in, sems.at[3]),
        start_copy(w_out.at[units, :], first_out, sems.at[4]),
    )
    logits = []
    for copy, half in halves:
        copy.wait()
        logits += [dot(params[...], tokens_v[image], 1, 1) for image in half]
    over_slots = []
    for image in range(images):
        over_tokens = softmax(logits[image], 1)
        dispatch[image] = over_tokens
        put(
            rows, KINDS * image, slots, stride, dot(over_tokens.astype(LOW), tokens_v[image], 1, 0)
        )
        over_slots.append(softmax(logits[image], 0))
        combine[image] = over_slots[image]
    grads_copy.wait()
    for image in range(images):
        value = dot(over_slots[image].astype(LOW), grads_v[image], 1, 0)
        put(rows, KINDS * image + 1, slots, stride, value)
    sent[...] = packed(rows)
    for copy in weight_copies:
        copy.wait()


def gather(tokens, params, grads, w_in, w_out, first):
    images, length, width = tokens.shape
    slots = params.shape[0]
    weights = shaped((images, slots, length), WIDE)
    rows = (slots * images * KINDS, width)
    return call(
        gather_kernel,
        "gather_slots",
        ROOMY,
        6 * images * slots * length * width,
        4 * images * length * width,
        2 * images * slots * length,
        out_shape=(
            shaped(rows, LOW),
            weights,
            weights,
            shaped((width, first), LOW),
            shaped((first, width), LOW),
        ),
        in_specs=[PLACE, WHOLE, PLACE, PLACE, PLACE],
        out_specs=(WHOLE,) * 5,
        scratch_shapes=[
            pltpu.VMEM(tokens.shape, LOW),
            pltpu.VMEM(grads.shape, LOW),
            scratch_rows(rows),
            pltpu.SemaphoreType.DMA((5,)),
        ],
    )(tokens, params, grads, w_in, w_out)


def chunks_of(first, hidden, tile):
    edges = [*range(first, hidden, tile), hidden]
    return [slice(low, high) for low, high in zip(edges, edges[1:])]


def start_weights(w_in, w_out, w_in_v, w_out_v, sems, chunks):
    copies = []
    for chunk, units in enumerate(chunks):
        copies.append(
            (
                start_copy(w_in.at[:, units], w_in_v.at[:, units], sems.at[0, chunk]),
                start_copy(w_out.at[units, :], w_out_v.at[units, :], sems.at[1, chunk]),
            )
        )
    return copies


def weight_scratch(width, hidden, chunks):
    return [
        pltpu.VMEM((width, hidden), LOW),
        pltpu.VMEM((hidden, width), LOW),
        pltpu.SemaphoreType.DMA((2, len(chunks))),
    ]


def expert_kernel(
    chunks, rows, first_in, first_out, w_in, w_out, back, acts, hidden, mark,
    w_in_v, w_out_v, sems, wide,
):
    del mark
    copies = start_weights(w_in, w_out, w_in_v, w_out_v, sems, chunks)
    count = rows.shape[0] // KINDS
    load_rows(wide, rows[...])
    rows_in = take(wide, 0, count, KINDS).astype(LOW)
    rows_grad = take(wide, 1, count, KINDS).astype(LOW)

    def first_products(weight_in, weight_out):
        return dot(rows_in, weight_in, 1, 0), dot(rows_grad, weight_out, 1, 1)

    def second_products(held, weight_in, weight_out):
        return dot(held[0], weight_out, 1, 0), dot(held[1], weight_in, 1, 1)

    def hold(preact, d_acts, units):
        values, slope = gelu_parts(preact)
        held = (values.astype(LOW), (d_acts * slope).astype(LOW))
        acts[:, units], hidden[:, units] = held
        return held

    held = hold(
        *first_products(first_in[...], first_out[...]), slice(0, first_out.shape[0])
    )
    out, d_in = second_products(held, first_in[...], first_out[...])
    before = None
    for pair, units in zip([*copies, None], [*chunks, None]):
        if pair is not None:
            for copy in pair:
                copy.wait()
            products = first_products(w_in_v[:, units], w_out_v[units, :])
        if before is not None:
            parts = second_products(held, w_in_v[:, before], w_out_v[before, :])
            out, d_in = out + parts[0], d_in + parts[1]
        if pair is not None:
            held = hold(*products, units)
        before = units
    put(wide, 0, count, KINDS, out)
    put(wide, 1, count, KINDS, d_in)
    back[...] = packed(wide)


def expert(rows, first_in, first_out, w_in, w_out, tile):
    total, width = rows.shape
    hidden = w_in.shape[1]
    count = total // KINDS
    kept = shaped((count, hidden), LOW)
    chunks = chunks_of(first_out.shape[0], hidden, tile)
    return call(
        functools.partial(expert_kernel, chunks),
        "expert_rows",
        ROOMY,
        8 * count * hidden * width,
        4 * hidden * width,
        count * hidden,
        out_shape=(shaped(rows.shape, LOW), kept, kept, MARK),
        in_specs=[WHOLE, WHOLE, WHOLE, PLACE, PLACE],
        out_specs=(WHOLE, WHOLE, WHOLE, PLACE),
        scratch_shapes=[*weight_scratch(width, hidden, chunks), scratch_rows(rows.shape)],
    )(rows, first_in, first_out, w_in, w_out)


def replica_kernel(
    chunks, mine, after, rows, other_rows, acts, hidden, w_in, w_out, tokens,
    grad_in, grad_out, tokens_half, mark,
    w_in_v, w_out_v, grad_in_v, grad_out_v, wide, grads, turned, sems, in_sems, out_sems, half_sem,
):
    del after, mark
    count = rows.shape[0] // KINDS
    size = w_in.shape[1]
    half = grad_out.shape[0]
    spans, copies = [], []
    for chunk, units in enumerate(chunks):
        start = pl.multiple_of(lax.rem(mine[0] * half + units.start, size), LANES)
        span = pl.ds(start, units.stop - units.start)
        spans.append(span)
        copies.append(
            (
                start_copy(w_in.at[:, span], w_in_v.at[:, units], sems.at[0, chunk]),
                start_copy(w_out.at[span, :], w_out_v.at[units, :], sems.at[1, chunk]),
            )
        )
    results = [
        start_copy(tokens.at[pl.ds(0, tokens_half.shape[0])], tokens_half, half_sem.at[0])
    ]
    left, right = [], []
    tiles = turned.shape[0] // LANES
    for source in (rows, other_rows):
        load_rows(wide, source[...])
        left.append(take(wide, 0, count, KINDS, mine[0] * tiles, tiles))
        right.append(take(wide, 1, count, KINDS))
    turned[...] = jnp.concatenate(left, axis=0).T.astype(LOW)
    grads[...] = jnp.concatenate(right, axis=0).astype(LOW)
    rows_in = take(wide, 0, count, KINDS).astype(LOW)
    rows_grad = right[1].astype(LOW)
    before = None
    for chunk in range(len(chunks) + 1):
        if chunk < len(chunks):
            units = chunks[chunk]
            for copy in copies[chunk]:
                copy.wait()
            preact = dot(rows_in, w_in_v[:, units], 1, 0)
            d_acts = dot(rows_grad, w_out_v[units, :], 1, 1)
        if before is not None:
            past, span, all_acts, all_hidden = before
            grad_in_v[:, past] = dot(turned[...], all_hidden, 1, 0).astype(LOW)
            results.append(
                start_copy(grad_in_v.at[:, past], grad_in.at[:, span], in_sems.at[chunk - 1])
            )
            if past.stop <= half:
                grad_out_v[past, :] = dot(all_acts, grads[...], 0, 0).astype(LOW)
                results.append(
                    start_copy(
                        grad_out_v.at[past, :], grad_out.at[past, :], out_sems.at[chunk - 1]
                    )
                )
        if chunk < len(chunks):
            span = spans[chunk]
            values, slope = gelu_parts(preact)
            all_acts = jnp.concatenate([acts[:, span], values.astype(LOW)], axis=0)
            all_hidden = jnp.concatenate(
                [hidden[:, span], (d_acts * slope).astype(LOW)], axis=0
            )
            before = (units, span, all_acts, all_hidden)
    for copy in results:
        copy.wait()


def replica_grads(
    mine, after, rows, other_rows, acts, hidden, w_in, w_out, tokens, replicas, tile
):
    total, width = rows.shape
    size = w_in.shape[1]
    half = size // replicas
    count = total // KINDS
    chunks = [
        slice(part * half + units.start, part * half + units.stop)
        for part in range(replicas)
        for units in chunks_of(0, half, tile)
    ]
    return call(
        functools.partial(replica_kernel, chunks),
        "replica_grads",
        ROOMY,
        64 * count * size * width,
        32 * size * width,
        count * size,
        out_shape=(
            shaped((width // replicas, size), LOW),
            shaped((half, width), LOW),
            shaped((tokens.shape[0] // 2, *tokens.shape[1:]), LOW),
            MARK,
        ),
        in_specs=[pl.BlockSpec(memory_space=pltpu.SMEM), PLACE]
        + [WHOLE] * 4
        + [PLACE] * 3,
        out_specs=(PLACE, PLACE, WHOLE, PLACE),
        scratch_shapes=[
            *weight_scratch(width, size, chunks)[:2],
            pltpu.VMEM((width // replicas, size), LOW),
            pltpu.VMEM((half, width), LOW),
            scratch_rows((total, width)),
            pltpu.VMEM((2 * count, width), LOW),
            pltpu.VMEM((width // replicas, 2 * count), LOW),
            pltpu.SemaphoreType.DMA((2, len(chunks))),
            pltpu.SemaphoreType.DMA((len(chunks),)),
            pltpu.SemaphoreType.DMA((len(chunks),)),
            pltpu.SemaphoreType.DMA((1,)),
        ],
    )(mine, after, rows, other_rows, acts, hidden, w_in, w_out, far(tokens))


def logits_kernel(
    after, back, tokens, tokens_half, params, grads, dispatch, combine, left, right, local, mark,
    tokens_v, grads_v, wide, sems,
):
    del after, mark
    images, slots, _ = dispatch.shape
    ready = tokens_half.shape[0]
    early, late = pl.ds(0, ready), pl.ds(ready, images - ready)
    copies = (
        (start_copy(grads.at[early], grads_v.at[early], sems.at[0]),),
        (
            start_copy(tokens.at[late], tokens_v, sems.at[1]),
            start_copy(grads.at[late], grads_v.at[late], sems.at[2]),
        ),
    )

    def tokens_of(image):
        return tokens_half[image] if image < ready else tokens_v[image - ready]

    load_rows(wide, back[...])
    stride = KINDS * images
    slot_out, d_slot_in = [], []
    for image in range(images):
        slot_out.append(take(wide, KINDS * image, slots, stride).astype(LOW))
        d_slot_in.append(take(wide, KINDS * image + 1, slots, stride).astype(LOW))
        right[image, :slots, :] = d_slot_in[image]
        right[image, slots:, :] = params[...]
        left[image, :slots, :] = dispatch[image].astype(LOW)

    def dispatch_part(image):
        weights = dispatch[image]
        d_dispatch = dot(d_slot_in[image], tokens_of(image), 1, 1)
        return weights * (d_dispatch - jnp.sum(weights * d_dispatch, axis=1, keepdims=True))

    def combine_part(image):
        weights = combine[image]
        d_combine = dot(slot_out[image], grads_v[image], 1, 1)
        return weights * (d_combine - jnp.sum(weights * d_combine, axis=0, keepdims=True))

    parts = [dispatch_part(image) for image in range(ready)]
    total = None
    for pair, half in zip(copies, (range(ready), range(ready, images))):
        for copy in pair:
            copy.wait()
        for image in half:
            if image >= ready:
                parts.append(dispatch_part(image))
        lows = [(parts[image] + combine_part(image)).astype(LOW) for image in half]
        for image, low in zip(half, lows):
            left[image, slots:, :] = low
            part = dot(low, tokens_of(image), 1, 0)
            total = part if total is None else total + part
    local[...] = total.astype(LOW)


def logits_grads(after, back, tokens, tokens_half, params, grads, dispatch, combine):
    images, length, width = tokens.shape
    slots = params.shape[0]
    return call(
        logits_kernel,
        "logits_grads",
        ROOMY,
        6 * images * slots * length * width,
        4 * images * length * width,
        out_shape=(
            shaped((images, 2 * slots, length), LOW),
            shaped((images, 2 * slots, width), LOW),
            shaped(params.shape, LOW),
            MARK,
        ),
        in_specs=[PLACE, WHOLE, PLACE, WHOLE, WHOLE, PLACE, WHOLE, WHOLE],
        out_specs=(WHOLE, WHOLE, WHOLE, PLACE),
        scratch_shapes=[
            pltpu.VMEM((images - tokens_half.shape[0], length, width), LOW),
            pltpu.VMEM(grads.shape, LOW),
            scratch_rows(back.shape),
            pltpu.SemaphoreType.DMA((3,)),
        ],
    )(after, back, far(tokens), tokens_half, params, far(grads), dispatch, combine)


def tokens_kernel(after, left, right, out, mark):
    del after, mark
    out[0] = dot(left[0], right[0], 0, 0).astype(LOW)


def tokens_grads(after, left, right):
    images, deep, length = left.shape
    width = right.shape[2]
    return call(
        tokens_kernel,
        "tokens_grads",
        SHARED,
        2 * images * deep * length * width,
        2 * images * length * width,
        grid=(images,),
        out_shape=(shaped((images, length, width), LOW), MARK),
        in_specs=[
            PLACE,
            pl.BlockSpec((1, deep, length), lambda i: (i, 0, 0)),
            pl.BlockSpec((1, deep, width), lambda i: (i, 0, 0)),
        ],
        out_specs=(pl.BlockSpec((1, length, width), lambda i: (i, 0, 0)), PLACE),
    )(after, left, right)


def add_kernel(after, *refs):
    del after
    terms = [ref[...].astype(WIDE) for ref in reversed(refs[:-2])]
    while len(terms) > 1:
        terms = [left + right for left, right in zip(terms[::2], terms[1::2])]
    refs[-2][...] = terms[0].astype(refs[-2].dtype)


def add(after, terms, dtype):
    return call(
        add_kernel,
        "add_terms",
        SHARED,
        len(terms) * terms[0].size,
        2 * len(terms) * terms[0].size,
        out_shape=(shaped(terms[0].shape, dtype), MARK),
        in_specs=[PLACE] + [WHOLE] * len(terms),
        out_specs=(WHOLE, PLACE),
    )(after, *reversed(terms))


def terms_of_group(array, bits):
    axes = ("rep", "exp")
    distances = [0]
    for bit in bits:
        distances += [distance + (1 << bit) for distance in distances]
    count = lax.axis_size(axes)
    terms = [
        lax.ppermute(array, axes, [(i, i ^ distance) for i in range(count)])
        for distance in reversed(distances[1:])
    ]
    return [array, *reversed(terms)]


def exchange(rows, axes):
    return lax.all_to_all(rows, axes, split_axis=0, concat_axis=0, tiled=True)


def body(tokens, slot_params, expert_in, expert_out, grad_out):
    params = slot_params.T
    weights = (expert_in[0], expert_out[0])
    replicas = lax.axis_size("rep")
    mine = lax.axis_index("rep").astype(jnp.int32).reshape(1)

    sent, dispatch, combine, *first = gather(tokens, params, grad_out, *weights, 256)
    rows = exchange(sent, "exp")
    other_rows = lax.ppermute(rows, "rep", [(i, (i + 1) % replicas) for i in range(replicas)])
    back, acts, hidden, after = expert(rows, *first, *weights, 512)
    back = exchange(back, "exp")
    grad_in, grad_outer, tokens_half, after = replica_grads(
        mine, after, rows, other_rows, acts, hidden, *weights, tokens, replicas, 512
    )
    left, right, local, after = logits_grads(
        after, back, tokens, tokens_half, params, grad_out, dispatch, combine
    )
    exp_bits = lax.axis_size("exp").bit_length() - 1
    rep_bits = replicas.bit_length() - 1
    groups = [(0, 1, *range(exp_bits, exp_bits + rep_bits))]
    groups += [range(bit, min(bit + 2, exp_bits)) for bit in range(2, exp_bits, 2)]
    for bits in groups[:-1]:
        local, after = add(after, terms_of_group(local, bits), LOW)
    terms = terms_of_group(local, groups[-1])
    grad_tokens, after = tokens_grads(after, left, right)
    grad_params, _ = add(after, terms, WIDE)
    return (grad_tokens, grad_params.T, grad_in[None], grad_outer[None])


def solution(mesh):
    in_specs = (
        P(("rep", "exp"), None, None),
        P(),
        P("exp", None, None),
        P("exp", None, None),
        P(("rep", "exp"), None, None),
    )
    out_specs = (P(("rep", "exp"), None, None), P(), P("exp", "rep", None), P("exp", "rep", None))
    return jax.shard_map(body, mesh=mesh, in_specs=in_specs, out_specs=out_specs, check_vma=False)
```

```python
import functools
import math

import jax
import jax.numpy as jnp
from jax import lax
from jax.experimental import pallas as pl
from jax.experimental.pallas import tpu as pltpu
from jax.sharding import PartitionSpec as P

GELU_C = math.sqrt(2.0 / math.pi)
CUBIC = 0.044715
LOW = jnp.bfloat16
WIDE = jnp.float32
LANES = 128
KINDS = 2
SHARED = 52 * 1024 * 1024
ROOMY = 50 * 1024 * 1024
WHOLE = pl.BlockSpec(memory_space=pltpu.VMEM)
PLACE = pl.BlockSpec(memory_space=pl.ANY)


def call(kernel, name, grant, flops, nbytes, exps=0, **kwargs):
    return pl.pallas_call(
        kernel,
        name=name,
        compiler_params=pltpu.CompilerParams(vmem_limit_bytes=grant),
        cost_estimate=pl.CostEstimate(
            flops=flops, bytes_accessed=nbytes, transcendentals=exps
        ),
        **kwargs,
    )


def shaped(shape, dtype):
    return jax.ShapeDtypeStruct(shape, dtype)


MARK = shaped((8, LANES), WIDE)


def gelu_parts(values):
    square = values * values
    tangent = jnp.tanh(GELU_C * (values + CUBIC * square * values))
    half = 0.5 * (1.0 + tangent)
    slope = half + 0.5 * values * (1.0 - tangent * tangent) * GELU_C * (1.0 + 3.0 * CUBIC * square)
    return values * half, slope


def dot(left, right, over_left, over_right):
    return lax.dot_general(
        left, right, (((over_left,), (over_right,)), ((), ())), preferred_element_type=WIDE
    )


def softmax(values, axis):
    raised = jnp.exp(values - jnp.max(values, axis=axis, keepdims=True))
    return raised / jnp.sum(raised, axis=axis, keepdims=True)


def scratch_rows(shape):
    return pltpu.VMEM((shape[1] // LANES, shape[0], LANES), WIDE)


def load_rows(ref, array):
    for tile in range(ref.shape[0]):
        ref[tile] = array[:, tile * LANES : (tile + 1) * LANES].astype(WIDE)


def packed(ref):
    return jnp.concatenate([ref[tile] for tile in range(ref.shape[0])], axis=1).astype(LOW)


def take(ref, start, count, stride, first=0, tiles=None):
    tiles = ref.shape[0] if tiles is None else tiles
    picked = [ref[first + tile, pl.ds(start, count, stride=stride), :] for tile in range(tiles)]
    return jnp.concatenate(picked, axis=1)


def put(ref, start, count, stride, array):
    for tile in range(ref.shape[0]):
        ref[tile, pl.ds(start, count, stride=stride), :] = array[
            :, tile * LANES : (tile + 1) * LANES
        ]


def start_copy(source, target, sem):
    copy = pltpu.make_async_copy(source, target, sem)
    copy.start()
    return copy


def far(array):
    return pltpu.with_memory_space_constraint(array, pltpu.HBM)


def start_halves(source, target, sems):
    images = source.shape[0]
    parts = []
    for index, (first, last) in enumerate(((0, images // 2), (images // 2, images))):
        part = pl.ds(first, last - first)
        copy = start_copy(source.at[part], target.at[part], sems.at[index])
        parts.append((copy, range(first, last)))
    return parts


def gather_kernel(
    tokens, params, grads, w_in, w_out, sent, dispatch, combine, first_in, first_out,
    tokens_v, grads_v, rows, sems,
):
    images = tokens.shape[0]
    slots = params.shape[0]
    stride = KINDS * images
    halves = start_halves(tokens, tokens_v, sems)
    grads_copy = start_copy(grads, grads_v, sems.at[2])
    units = slice(0, first_out.shape[0])
    weight_copies = (
        start_copy(w_in.at[:, units], first_in, sems.at[3]),
        start_copy(w_out.at[units, :], first_out, sems.at[4]),
    )
    logits = []
    for copy, half in halves:
        copy.wait()
        logits += [dot(params[...], tokens_v[image], 1, 1) for image in half]
    over_slots = []
    for image in range(images):
        over_tokens = softmax(logits[image], 1)
        dispatch[image] = over_tokens
        put(
            rows, KINDS * image, slots, stride, dot(over_tokens.astype(LOW), tokens_v[image], 1, 0)
        )
        over_slots.append(softmax(logits[image], 0))
        combine[image] = over_slots[image]
    grads_copy.wait()
    for image in range(images):
        value = dot(over_slots[image].astype(LOW), grads_v[image], 1, 0)
        put(rows, KINDS * image + 1, slots, stride, value)
    sent[...] = packed(rows)
    for copy in weight_copies:
        copy.wait()


def gather(tokens, params, grads, w_in, w_out, first):
    images, length, width = tokens.shape
    slots = params.shape[0]
    weights = shaped((images, slots, length), WIDE)
    rows = (slots * images * KINDS, width)
    return call(
        gather_kernel,
        "gather_slots",
        ROOMY,
        6 * images * slots * length * width,
        4 * images * length * width,
        2 * images * slots * length,
        out_shape=(
            shaped(rows, LOW),
            weights,
            weights,
            shaped((width, first), LOW),
            shaped((first, width), LOW),
        ),
        in_specs=[PLACE, WHOLE, PLACE, PLACE, PLACE],
        out_specs=(WHOLE,) * 5,
        scratch_shapes=[
            pltpu.VMEM(tokens.shape, LOW),
            pltpu.VMEM(grads.shape, LOW),
            scratch_rows(rows),
            pltpu.SemaphoreType.DMA((5,)),
        ],
    )(tokens, params, grads, w_in, w_out)


def chunks_of(first, hidden, tile):
    edges = [*range(first, hidden, tile), hidden]
    return [slice(low, high) for low, high in zip(edges, edges[1:])]


def start_weights(w_in, w_out, w_in_v, w_out_v, sems, chunks):
    copies = []
    for chunk, units in enumerate(chunks):
        copies.append(
            (
                start_copy(w_in.at[:, units], w_in_v.at[:, units], sems.at[0, chunk]),
                start_copy(w_out.at[units, :], w_out_v.at[units, :], sems.at[1, chunk]),
            )
        )
    return copies


def weight_scratch(width, hidden, chunks):
    return [
        pltpu.VMEM((width, hidden), LOW),
        pltpu.VMEM((hidden, width), LOW),
        pltpu.SemaphoreType.DMA((2, len(chunks))),
    ]


def expert_kernel(
    chunks, rows, first_in, first_out, w_in, w_out, back, acts, hidden, mark,
    w_in_v, w_out_v, sems, wide,
):
    del mark
    copies = start_weights(w_in, w_out, w_in_v, w_out_v, sems, chunks)
    count = rows.shape[0] // KINDS
    load_rows(wide, rows[...])
    rows_in = take(wide, 0, count, KINDS).astype(LOW)
    rows_grad = take(wide, 1, count, KINDS).astype(LOW)

    def first_products(weight_in, weight_out):
        return dot(rows_in, weight_in, 1, 0), dot(rows_grad, weight_out, 1, 1)

    def second_products(held, weight_in, weight_out):
        return dot(held[0], weight_out, 1, 0), dot(held[1], weight_in, 1, 1)

    def hold(preact, d_acts, units):
        values, slope = gelu_parts(preact)
        held = (values.astype(LOW), (d_acts * slope).astype(LOW))
        acts[:, units], hidden[:, units] = held
        return held

    held = hold(
        *first_products(first_in[...], first_out[...]), slice(0, first_out.shape[0])
    )
    out, d_in = second_products(held, first_in[...], first_out[...])
    before = None
    for pair, units in zip([*copies, None], [*chunks, None]):
        if pair is not None:
            for copy in pair:
                copy.wait()
            products = first_products(w_in_v[:, units], w_out_v[units, :])
        if before is not None:
            parts = second_products(held, w_in_v[:, before], w_out_v[before, :])
            out, d_in = out + parts[0], d_in + parts[1]
        if pair is not None:
            held = hold(*products, units)
        before = units
    put(wide, 0, count, KINDS, out)
    put(wide, 1, count, KINDS, d_in)
    back[...] = packed(wide)


def expert(rows, first_in, first_out, w_in, w_out, tile):
    total, width = rows.shape
    hidden = w_in.shape[1]
    count = total // KINDS
    kept = shaped((count, hidden), LOW)
    start = first_out.shape[0]
    chunks = [
        *chunks_of(start, start + tile // 2, tile),
        *chunks_of(start + tile // 2, hidden - tile // 2, tile),
        *chunks_of(hidden - tile // 2, hidden, tile),
    ]
    return call(
        functools.partial(expert_kernel, chunks),
        "expert_rows",
        ROOMY,
        8 * count * hidden * width,
        4 * hidden * width,
        count * hidden,
        out_shape=(shaped(rows.shape, LOW), kept, kept, MARK),
        in_specs=[WHOLE, WHOLE, WHOLE, PLACE, PLACE],
        out_specs=(WHOLE, WHOLE, WHOLE, PLACE),
        scratch_shapes=[*weight_scratch(width, hidden, chunks), scratch_rows(rows.shape)],
    )(rows, first_in, first_out, w_in, w_out)


def replica_kernel(
    chunks, mine, after, rows, other_rows, acts, hidden, w_in, w_out, tokens,
    grad_in, grad_out, tokens_half, mark,
    w_in_v, w_out_v, grad_in_v, grad_out_v, wide, grads, turned, sems, in_sems, out_sems, half_sem,
):
    del after, mark
    count = rows.shape[0] // KINDS
    size = w_in.shape[1]
    half = grad_out.shape[0]
    spans, copies = [], []
    for chunk, units in enumerate(chunks):
        start = pl.multiple_of(lax.rem(mine[0] * half + units.start, size), LANES)
        span = pl.ds(start, units.stop - units.start)
        spans.append(span)
        copies.append(
            (
                start_copy(w_in.at[:, span], w_in_v.at[:, units], sems.at[0, chunk]),
                start_copy(w_out.at[span, :], w_out_v.at[units, :], sems.at[1, chunk]),
            )
        )
    results = [
        start_copy(tokens.at[pl.ds(0, tokens_half.shape[0])], tokens_half, half_sem.at[0])
    ]
    left, right = [], []
    tiles = turned.shape[0] // LANES
    for source in (rows, other_rows):
        load_rows(wide, source[...])
        left.append(take(wide, 0, count, KINDS, mine[0] * tiles, tiles))
        right.append(take(wide, 1, count, KINDS))
    turned[...] = jnp.concatenate(left, axis=0).T.astype(LOW)
    grads[...] = jnp.concatenate(right, axis=0).astype(LOW)
    rows_in = take(wide, 0, count, KINDS).astype(LOW)
    rows_grad = right[1].astype(LOW)
    before = None
    for chunk in range(len(chunks) + 1):
        if chunk < len(chunks):
            units = chunks[chunk]
            for copy in copies[chunk]:
                copy.wait()
            preact = dot(rows_in, w_in_v[:, units], 1, 0)
            d_acts = dot(rows_grad, w_out_v[units, :], 1, 1)
        if before is not None:
            past, span, all_acts, all_hidden = before
            grad_in_v[:, past] = dot(turned[...], all_hidden, 1, 0).astype(LOW)
            results.append(
                start_copy(grad_in_v.at[:, past], grad_in.at[:, span], in_sems.at[chunk - 1])
            )
            if past.stop <= half:
                grad_out_v[past, :] = dot(all_acts, grads[...], 0, 0).astype(LOW)
                results.append(
                    start_copy(
                        grad_out_v.at[past, :], grad_out.at[past, :], out_sems.at[chunk - 1]
                    )
                )
        if chunk < len(chunks):
            span = spans[chunk]
            values, slope = gelu_parts(preact)
            all_acts = jnp.concatenate([acts[:, span], values.astype(LOW)], axis=0)
            all_hidden = jnp.concatenate(
                [hidden[:, span], (d_acts * slope).astype(LOW)], axis=0
            )
            before = (units, span, all_acts, all_hidden)
    for copy in results:
        copy.wait()


def replica_grads(
    mine, after, rows, other_rows, acts, hidden, w_in, w_out, tokens, replicas, tile
):
    total, width = rows.shape
    size = w_in.shape[1]
    half = size // replicas
    count = total // KINDS
    chunks = [
        slice(part * half + units.start, part * half + units.stop)
        for part in range(replicas)
        for units in chunks_of(0, half, tile)
    ]
    return call(
        functools.partial(replica_kernel, chunks),
        "replica_grads",
        ROOMY,
        64 * count * size * width,
        32 * size * width,
        count * size,
        out_shape=(
            shaped((width // replicas, size), LOW),
            shaped((half, width), LOW),
            shaped((tokens.shape[0] // 2, *tokens.shape[1:]), LOW),
            MARK,
        ),
        in_specs=[pl.BlockSpec(memory_space=pltpu.SMEM), PLACE]
        + [WHOLE] * 4
        + [PLACE] * 3,
        out_specs=(PLACE, PLACE, WHOLE, PLACE),
        scratch_shapes=[
            *weight_scratch(width, size, chunks)[:2],
            pltpu.VMEM((width // replicas, size), LOW),
            pltpu.VMEM((half, width), LOW),
            scratch_rows((total, width)),
            pltpu.VMEM((2 * count, width), LOW),
            pltpu.VMEM((width // replicas, 2 * count), LOW),
            pltpu.SemaphoreType.DMA((2, len(chunks))),
            pltpu.SemaphoreType.DMA((len(chunks),)),
            pltpu.SemaphoreType.DMA((len(chunks),)),
            pltpu.SemaphoreType.DMA((1,)),
        ],
    )(mine, after, rows, other_rows, acts, hidden, w_in, w_out, far(tokens))


def logits_kernel(
    after, back, tokens, tokens_half, params, grads, dispatch, combine, left, right, local, mark,
    tokens_v, grads_v, wide, sems,
):
    del after, mark
    images, slots, _ = dispatch.shape
    ready = tokens_half.shape[0]
    early, late = pl.ds(0, ready), pl.ds(ready, images - ready)
    copies = (
        (start_copy(grads.at[early], grads_v.at[early], sems.at[0]),),
        (
            start_copy(tokens.at[late], tokens_v, sems.at[1]),
            start_copy(grads.at[late], grads_v.at[late], sems.at[2]),
        ),
    )

    def tokens_of(image):
        return tokens_half[image] if image < ready else tokens_v[image - ready]

    load_rows(wide, back[...])
    stride = KINDS * images
    slot_out, d_slot_in = [], []
    for image in range(images):
        slot_out.append(take(wide, KINDS * image, slots, stride).astype(LOW))
        d_slot_in.append(take(wide, KINDS * image + 1, slots, stride).astype(LOW))
        right[image, :slots, :] = d_slot_in[image]
        right[image, slots:, :] = params[...]
        left[image, :slots, :] = dispatch[image].astype(LOW)

    def dispatch_part(image):
        weights = dispatch[image]
        d_dispatch = dot(d_slot_in[image], tokens_of(image), 1, 1)
        return weights * (d_dispatch - jnp.sum(weights * d_dispatch, axis=1, keepdims=True))

    def combine_part(image):
        weights = combine[image]
        d_combine = dot(slot_out[image], grads_v[image], 1, 1)
        return weights * (d_combine - jnp.sum(weights * d_combine, axis=0, keepdims=True))

    parts = [dispatch_part(image) for image in range(ready)]
    total = None
    for pair, half in zip(copies, (range(ready), range(ready, images))):
        for copy in pair:
            copy.wait()
        for image in half:
            if image >= ready:
                parts.append(dispatch_part(image))
        lows = [(parts[image] + combine_part(image)).astype(LOW) for image in half]
        for image, low in zip(half, lows):
            left[image, slots:, :] = low
            part = dot(low, tokens_of(image), 1, 0)
            total = part if total is None else total + part
    local[...] = total.astype(LOW)


def logits_grads(after, back, tokens, tokens_half, params, grads, dispatch, combine):
    images, length, width = tokens.shape
    slots = params.shape[0]
    return call(
        logits_kernel,
        "logits_grads",
        ROOMY,
        6 * images * slots * length * width,
        4 * images * length * width,
        out_shape=(
            shaped((images, 2 * slots, length), LOW),
            shaped((images, 2 * slots, width), LOW),
            shaped(params.shape, LOW),
            MARK,
        ),
        in_specs=[PLACE, WHOLE, PLACE, WHOLE, WHOLE, PLACE, WHOLE, WHOLE],
        out_specs=(WHOLE, WHOLE, WHOLE, PLACE),
        scratch_shapes=[
            pltpu.VMEM((images - tokens_half.shape[0], length, width), LOW),
            pltpu.VMEM(grads.shape, LOW),
            scratch_rows(back.shape),
            pltpu.SemaphoreType.DMA((3,)),
        ],
    )(after, back, far(tokens), tokens_half, params, far(grads), dispatch, combine)


def tokens_kernel(after, left, right, out, mark):
    del after, mark
    out[0] = dot(left[0], right[0], 0, 0).astype(LOW)


def tokens_grads(after, left, right):
    images, deep, length = left.shape
    width = right.shape[2]
    return call(
        tokens_kernel,
        "tokens_grads",
        SHARED,
        2 * images * deep * length * width,
        2 * images * length * width,
        grid=(images,),
        out_shape=(shaped((images, length, width), LOW), MARK),
        in_specs=[
            PLACE,
            pl.BlockSpec((1, deep, length), lambda i: (i, 0, 0)),
            pl.BlockSpec((1, deep, width), lambda i: (i, 0, 0)),
        ],
        out_specs=(pl.BlockSpec((1, length, width), lambda i: (i, 0, 0)), PLACE),
    )(after, left, right)


def add_kernel(after, *refs):
    del after
    terms = [ref[...].astype(WIDE) for ref in refs[:-2]]
    while len(terms) > 1:
        terms = [left + right for left, right in zip(terms[::2], terms[1::2])]
    refs[-2][...] = terms[0].astype(refs[-2].dtype)


def add(after, terms, dtype):
    return call(
        add_kernel,
        "add_terms",
        SHARED,
        len(terms) * terms[0].size,
        2 * len(terms) * terms[0].size,
        out_shape=(shaped(terms[0].shape, dtype), MARK),
        in_specs=[PLACE] + [WHOLE] * len(terms),
        out_specs=(WHOLE, PLACE),
    )(after, *terms)


def terms_of_group(array, bits):
    axes = ("rep", "exp")
    distances = [0]
    for bit in bits:
        distances += [distance + (1 << bit) for distance in distances]
    count = lax.axis_size(axes)
    return [array] + [
        lax.ppermute(array, axes, [(i, i ^ distance) for i in range(count)])
        for distance in distances[1:]
    ]


def exchange(rows, axes):
    return lax.all_to_all(rows, axes, split_axis=0, concat_axis=0, tiled=True)


def body(tokens, slot_params, expert_in, expert_out, grad_out):
    params = slot_params.T
    weights = (expert_in[0], expert_out[0])
    replicas = lax.axis_size("rep")
    mine = lax.axis_index("rep").astype(jnp.int32).reshape(1)

    sent, dispatch, combine, *first = gather(tokens, params, grad_out, *weights, 256)
    rows = exchange(sent, "exp")
    other_rows = lax.ppermute(rows, "rep", [(i, (i + 1) % replicas) for i in range(replicas)])
    back, acts, hidden, after = expert(rows, *first, *weights, 512)
    back = exchange(back, "exp")
    grad_in, grad_outer, tokens_half, after = replica_grads(
        mine, after, rows, other_rows, acts, hidden, *weights, tokens, replicas, 512
    )
    left, right, local, after = logits_grads(
        after, back, tokens, tokens_half, params, grad_out, dispatch, combine
    )
    exp_bits = lax.axis_size("exp").bit_length() - 1
    rep_bits = replicas.bit_length() - 1
    groups = [(0, 1, *range(exp_bits, exp_bits + rep_bits))]
    groups += [range(bit, min(bit + 2, exp_bits)) for bit in range(2, exp_bits, 2)]
    for bits in groups[:-1]:
        local, after = add(after, terms_of_group(local, bits), LOW)
    terms = terms_of_group(local, groups[-1])
    grad_tokens, after = tokens_grads(after, left, right)
    grad_params, _ = add(after, terms, WIDE)
    return (grad_tokens, grad_params.T, grad_in[None], grad_outer[None])


def solution(mesh):
    in_specs = (
        P(("rep", "exp"), None, None),
        P(),
        P("exp", None, None),
        P("exp", None, None),
        P(("rep", "exp"), None, None),
    )
    out_specs = (P(("rep", "exp"), None, None), P(), P("exp", "rep", None), P("exp", "rep", None))
    return jax.shard_map(body, mesh=mesh, in_specs=in_specs, out_specs=out_specs, check_vma=False)
```

```python
import functools
import math

import jax
import jax.numpy as jnp
from jax import lax
from jax.experimental import pallas as pl
from jax.experimental.pallas import tpu as pltpu
from jax.sharding import PartitionSpec as P

GELU_C = math.sqrt(2.0 / math.pi)
CUBIC = 0.044715
LOW = jnp.bfloat16
WIDE = jnp.float32
LANES = 128
KINDS = 2
SHARED = 52 * 1024 * 1024
ROOMY = 50 * 1024 * 1024
WHOLE = pl.BlockSpec(memory_space=pltpu.VMEM)
PLACE = pl.BlockSpec(memory_space=pl.ANY)


def call(kernel, name, grant, flops, nbytes, exps=0, **kwargs):
    return pl.pallas_call(
        kernel,
        name=name,
        compiler_params=pltpu.CompilerParams(vmem_limit_bytes=grant),
        cost_estimate=pl.CostEstimate(
            flops=flops, bytes_accessed=nbytes, transcendentals=exps
        ),
        **kwargs,
    )


def shaped(shape, dtype):
    return jax.ShapeDtypeStruct(shape, dtype)


MARK = shaped((8, LANES), WIDE)


def gelu_parts(values):
    square = values * values
    tangent = jnp.tanh(GELU_C * (values + CUBIC * square * values))
    half = 0.5 * (1.0 + tangent)
    slope = half + 0.5 * values * (1.0 - tangent * tangent) * GELU_C * (1.0 + 3.0 * CUBIC * square)
    return values * half, slope


def dot(left, right, over_left, over_right):
    return lax.dot_general(
        left, right, (((over_left,), (over_right,)), ((), ())), preferred_element_type=WIDE
    )


def softmax(values, axis):
    raised = jnp.exp(values - jnp.max(values, axis=axis, keepdims=True))
    return raised / jnp.sum(raised, axis=axis, keepdims=True)


def scratch_rows(shape):
    return pltpu.VMEM((shape[1] // LANES, shape[0], LANES), WIDE)


def load_rows(ref, array):
    for tile in range(ref.shape[0]):
        ref[tile] = array[:, tile * LANES : (tile + 1) * LANES].astype(WIDE)


def packed(ref):
    return jnp.concatenate([ref[tile] for tile in range(ref.shape[0])], axis=1).astype(LOW)


def take(ref, start, count, stride, first=0, tiles=None):
    tiles = ref.shape[0] if tiles is None else tiles
    picked = [ref[first + tile, pl.ds(start, count, stride=stride), :] for tile in range(tiles)]
    return jnp.concatenate(picked, axis=1)


def put(ref, start, count, stride, array):
    for tile in range(ref.shape[0]):
        ref[tile, pl.ds(start, count, stride=stride), :] = array[
            :, tile * LANES : (tile + 1) * LANES
        ]


def start_copy(source, target, sem):
    copy = pltpu.make_async_copy(source, target, sem)
    copy.start()
    return copy


def far(array):
    return pltpu.with_memory_space_constraint(array, pltpu.HBM)


def start_halves(source, target, sems):
    images = source.shape[0]
    parts = []
    for index, (first, last) in enumerate(((0, images // 2), (images // 2, images))):
        part = pl.ds(first, last - first)
        copy = start_copy(source.at[part], target.at[part], sems.at[index])
        parts.append((copy, range(first, last)))
    return parts


def gather_kernel(
    tokens, params, grads, w_in, w_out, sent, dispatch, combine, first_in, first_out,
    tokens_v, grads_v, rows, sems,
):
    images = tokens.shape[0]
    slots = params.shape[0]
    stride = KINDS * images
    halves = start_halves(tokens, tokens_v, sems)
    grads_copy = start_copy(grads, grads_v, sems.at[2])
    units = slice(0, first_out.shape[0])
    weight_copies = (
        start_copy(w_in.at[:, units], first_in, sems.at[3]),
        start_copy(w_out.at[units, :], first_out, sems.at[4]),
    )
    logits = []
    for copy, half in halves:
        copy.wait()
        logits += [dot(params[...], tokens_v[image], 1, 1) for image in half]
    over_slots = []
    for image in range(images):
        over_tokens = softmax(logits[image], 1)
        dispatch[image] = over_tokens
        put(
            rows, KINDS * image, slots, stride, dot(over_tokens.astype(LOW), tokens_v[image], 1, 0)
        )
        over_slots.append(softmax(logits[image], 0))
        combine[image] = over_slots[image]
    grads_copy.wait()
    for image in range(images):
        value = dot(over_slots[image].astype(LOW), grads_v[image], 1, 0)
        put(rows, KINDS * image + 1, slots, stride, value)
    sent[...] = packed(rows)
    for copy in weight_copies:
        copy.wait()


def gather(tokens, params, grads, w_in, w_out, first):
    images, length, width = tokens.shape
    slots = params.shape[0]
    weights = shaped((images, slots, length), WIDE)
    rows = (slots * images * KINDS, width)
    return call(
        gather_kernel,
        "gather_slots",
        ROOMY,
        6 * images * slots * length * width,
        4 * images * length * width,
        2 * images * slots * length,
        out_shape=(
            shaped(rows, LOW),
            weights,
            weights,
            shaped((width, first), LOW),
            shaped((first, width), LOW),
        ),
        in_specs=[PLACE, WHOLE, PLACE, PLACE, PLACE],
        out_specs=(WHOLE,) * 5,
        scratch_shapes=[
            pltpu.VMEM(tokens.shape, LOW),
            pltpu.VMEM(grads.shape, LOW),
            scratch_rows(rows),
            pltpu.SemaphoreType.DMA((5,)),
        ],
    )(tokens, params, grads, w_in, w_out)


def chunks_of(first, hidden, tile):
    edges = [*range(first, hidden, tile), hidden]
    return [slice(low, high) for low, high in zip(edges, edges[1:])]


def start_weights(w_in, w_out, w_in_v, w_out_v, sems, chunks):
    copies = []
    for chunk, units in enumerate(chunks):
        copies.append(
            (
                start_copy(w_in.at[:, units], w_in_v.at[:, units], sems.at[0, chunk]),
                start_copy(w_out.at[units, :], w_out_v.at[units, :], sems.at[1, chunk]),
            )
        )
    return copies


def weight_scratch(width, hidden, chunks):
    return [
        pltpu.VMEM((width, hidden), LOW),
        pltpu.VMEM((hidden, width), LOW),
        pltpu.SemaphoreType.DMA((2, len(chunks))),
    ]


def expert_kernel(
    chunks, rows, first_in, first_out, w_in, w_out, back, acts, hidden, mark,
    w_in_v, w_out_v, sems, wide,
):
    del mark
    copies = start_weights(w_in, w_out, w_in_v, w_out_v, sems, chunks)
    count = rows.shape[0] // KINDS
    load_rows(wide, rows[...])
    rows_in = take(wide, 0, count, KINDS).astype(LOW)
    rows_grad = take(wide, 1, count, KINDS).astype(LOW)

    def first_products(weight_in, weight_out):
        return dot(rows_in, weight_in, 1, 0), dot(rows_grad, weight_out, 1, 1)

    def second_products(held, weight_in, weight_out):
        return dot(held[0], weight_out, 1, 0), dot(held[1], weight_in, 1, 1)

    def hold(preact, d_acts, units):
        values, slope = gelu_parts(preact)
        held = (values.astype(LOW), (d_acts * slope).astype(LOW))
        acts[:, units], hidden[:, units] = held
        return held

    held = hold(
        *first_products(first_in[...], first_out[...]), slice(0, first_out.shape[0])
    )
    out, d_in = second_products(held, first_in[...], first_out[...])
    before = None
    for pair, units in zip([*copies, None], [*chunks, None]):
        if pair is not None:
            for copy in pair:
                copy.wait()
            products = first_products(w_in_v[:, units], w_out_v[units, :])
        if before is not None:
            parts = second_products(held, w_in_v[:, before], w_out_v[before, :])
            out, d_in = out + parts[0], d_in + parts[1]
        if pair is not None:
            held = hold(*products, units)
        before = units
    put(wide, 0, count, KINDS, out)
    put(wide, 1, count, KINDS, d_in)
    back[...] = packed(wide)


def expert(rows, first_in, first_out, w_in, w_out, tile):
    total, width = rows.shape
    hidden = w_in.shape[1]
    count = total // KINDS
    kept = shaped((count, hidden), LOW)
    chunks = chunks_of(first_out.shape[0], hidden, tile)
    return call(
        functools.partial(expert_kernel, chunks),
        "expert_rows",
        ROOMY,
        8 * count * hidden * width,
        4 * hidden * width,
        count * hidden,
        out_shape=(shaped(rows.shape, LOW), kept, kept, MARK),
        in_specs=[WHOLE, WHOLE, WHOLE, PLACE, PLACE],
        out_specs=(WHOLE, WHOLE, WHOLE, PLACE),
        scratch_shapes=[*weight_scratch(width, hidden, chunks), scratch_rows(rows.shape)],
    )(rows, first_in, first_out, w_in, w_out)


def replica_kernel(
    chunks, mine, after, rows, other_rows, acts, hidden, w_in, w_out, tokens,
    grad_in, grad_out, tokens_half, mark,
    w_in_v, w_out_v, grad_in_v, grad_out_v, wide, grads, turned, sems, in_sems, out_sems, half_sem,
):
    del after, mark
    count = rows.shape[0] // KINDS
    size = w_in.shape[1]
    half = grad_out.shape[0]
    spans, copies = [], []
    for chunk, units in enumerate(chunks):
        start = pl.multiple_of(lax.rem(mine[0] * half + units.start, size), LANES)
        span = pl.ds(start, units.stop - units.start)
        spans.append(span)
        copies.append(
            (
                start_copy(w_in.at[:, span], w_in_v.at[:, units], sems.at[0, chunk]),
                start_copy(w_out.at[span, :], w_out_v.at[units, :], sems.at[1, chunk]),
            )
        )
    results = [
        start_copy(tokens.at[pl.ds(0, tokens_half.shape[0])], tokens_half, half_sem.at[0])
    ]
    left, right = [], []
    tiles = turned.shape[0] // LANES
    for source in (rows, other_rows):
        load_rows(wide, source[...])
        left.append(take(wide, 0, count, KINDS, mine[0] * tiles, tiles))
        right.append(take(wide, 1, count, KINDS))
    turned[...] = jnp.concatenate(left, axis=0).T.astype(LOW)
    grads[...] = jnp.concatenate(right, axis=0).astype(LOW)
    rows_in = take(wide, 0, count, KINDS).astype(LOW)
    rows_grad = right[1].astype(LOW)
    before = None
    for chunk in range(len(chunks) + 1):
        if chunk < len(chunks):
            units = chunks[chunk]
            for copy in copies[chunk]:
                copy.wait()
            preact = dot(rows_in, w_in_v[:, units], 1, 0)
            d_acts = dot(rows_grad, w_out_v[units, :], 1, 1)
        if before is not None:
            past, span, all_acts, all_hidden = before
            grad_in_v[:, past] = dot(turned[...], all_hidden, 1, 0).astype(LOW)
            results.append(
                start_copy(grad_in_v.at[:, past], grad_in.at[:, span], in_sems.at[chunk - 1])
            )
            if past.stop <= half:
                grad_out_v[past, :] = dot(all_acts, grads[...], 0, 0).astype(LOW)
                results.append(
                    start_copy(
                        grad_out_v.at[past, :], grad_out.at[past, :], out_sems.at[chunk - 1]
                    )
                )
        if chunk < len(chunks):
            span = spans[chunk]
            values, slope = gelu_parts(preact)
            all_acts = jnp.concatenate([acts[:, span], values.astype(LOW)], axis=0)
            all_hidden = jnp.concatenate(
                [hidden[:, span], (d_acts * slope).astype(LOW)], axis=0
            )
            before = (units, span, all_acts, all_hidden)
    for copy in results:
        copy.wait()


def replica_grads(
    mine, after, rows, other_rows, acts, hidden, w_in, w_out, tokens, replicas, tile
):
    total, width = rows.shape
    size = w_in.shape[1]
    half = size // replicas
    count = total // KINDS
    chunks = [
        slice(part * half + units.start, part * half + units.stop)
        for part in range(replicas)
        for units in chunks_of(0, half, tile)
    ]
    return call(
        functools.partial(replica_kernel, chunks),
        "replica_grads",
        ROOMY,
        64 * count * size * width,
        32 * size * width,
        count * size,
        out_shape=(
            shaped((width // replicas, size), LOW),
            shaped((half, width), LOW),
            shaped((tokens.shape[0] // 2, *tokens.shape[1:]), LOW),
            MARK,
        ),
        in_specs=[pl.BlockSpec(memory_space=pltpu.SMEM), PLACE]
        + [WHOLE] * 4
        + [PLACE] * 3,
        out_specs=(PLACE, PLACE, WHOLE, PLACE),
        scratch_shapes=[
            *weight_scratch(width, size, chunks)[:2],
            pltpu.VMEM((width // replicas, size), LOW),
            pltpu.VMEM((half, width), LOW),
            scratch_rows((total, width)),
            pltpu.VMEM((2 * count, width), LOW),
            pltpu.VMEM((width // replicas, 2 * count), LOW),
            pltpu.SemaphoreType.DMA((2, len(chunks))),
            pltpu.SemaphoreType.DMA((len(chunks),)),
            pltpu.SemaphoreType.DMA((len(chunks),)),
            pltpu.SemaphoreType.DMA((1,)),
        ],
    )(mine, after, rows, other_rows, acts, hidden, w_in, w_out, far(tokens))


def logits_kernel(
    after, back, tokens, tokens_half, params, grads, dispatch, combine, left, right, local, mark,
    tokens_v, grads_v, wide, sems,
):
    del after, mark
    images, slots, _ = dispatch.shape
    ready = tokens_half.shape[0]
    early, late = pl.ds(0, ready), pl.ds(ready, images - ready)
    copies = (
        (start_copy(grads.at[early], grads_v.at[early], sems.at[0]),),
        (
            start_copy(tokens.at[late], tokens_v, sems.at[1]),
            start_copy(grads.at[late], grads_v.at[late], sems.at[2]),
        ),
    )

    def tokens_of(image):
        return tokens_half[image] if image < ready else tokens_v[image - ready]

    load_rows(wide, back[...])
    stride = KINDS * images
    slot_out, d_slot_in = [], []
    for image in range(images):
        slot_out.append(take(wide, KINDS * image, slots, stride).astype(LOW))
        d_slot_in.append(take(wide, KINDS * image + 1, slots, stride).astype(LOW))
        right[image, :slots, :] = d_slot_in[image]
        right[image, slots:, :] = params[...]
        left[image, :slots, :] = dispatch[image].astype(LOW)

    def dispatch_part(image):
        weights = dispatch[image]
        d_dispatch = dot(d_slot_in[image], tokens_of(image), 1, 1)
        return weights * (d_dispatch - jnp.sum(weights * d_dispatch, axis=1, keepdims=True))

    def combine_part(image):
        weights = combine[image]
        d_combine = dot(slot_out[image], grads_v[image], 1, 1)
        return weights * (d_combine - jnp.sum(weights * d_combine, axis=0, keepdims=True))

    parts = [dispatch_part(image) for image in range(ready)]
    total = None
    for pair, half in zip(copies, (range(ready), range(ready, images))):
        for copy in pair:
            copy.wait()
        for image in half:
            if image >= ready:
                parts.append(dispatch_part(image))
        lows = [(parts[image] + combine_part(image)).astype(LOW) for image in half]
        for image, low in zip(half, lows):
            left[image, slots:, :] = low
            part = dot(low, tokens_of(image), 1, 0)
            total = part if total is None else total + part
    local[...] = total.astype(LOW)


def logits_grads(after, back, tokens, tokens_half, params, grads, dispatch, combine):
    images, length, width = tokens.shape
    slots = params.shape[0]
    return call(
        logits_kernel,
        "logits_grads",
        ROOMY,
        6 * images * slots * length * width,
        4 * images * length * width,
        out_shape=(
            shaped((images, 2 * slots, length), LOW),
            shaped((images, 2 * slots, width), LOW),
            shaped(params.shape, LOW),
            MARK,
        ),
        in_specs=[PLACE, WHOLE, PLACE, WHOLE, WHOLE, PLACE, WHOLE, WHOLE],
        out_specs=(WHOLE, WHOLE, WHOLE, PLACE),
        scratch_shapes=[
            pltpu.VMEM((images - tokens_half.shape[0], length, width), LOW),
            pltpu.VMEM(grads.shape, LOW),
            scratch_rows(back.shape),
            pltpu.SemaphoreType.DMA((3,)),
        ],
    )(after, back, far(tokens), tokens_half, params, far(grads), dispatch, combine)


def tokens_kernel(after, left, right, out, mark):
    del after, mark
    out[0] = dot(left[0], right[0], 0, 0).astype(LOW)


def tokens_grads(after, left, right):
    images, deep, length = left.shape
    width = right.shape[2]
    return call(
        tokens_kernel,
        "tokens_grads",
        SHARED,
        2 * images * deep * length * width,
        2 * images * length * width,
        grid=(images,),
        out_shape=(shaped((images, length, width), LOW), MARK),
        in_specs=[
            PLACE,
            pl.BlockSpec((1, deep, length), lambda i: (i, 0, 0)),
            pl.BlockSpec((1, deep, width), lambda i: (i, 0, 0)),
        ],
        out_specs=(pl.BlockSpec((1, length, width), lambda i: (i, 0, 0)), PLACE),
    )(after, left, right)


def add_kernel(after, *refs):
    del after
    terms = [ref[...].astype(WIDE) for ref in refs[:-2]]
    while len(terms) > 1:
        terms = [left + right for left, right in zip(terms[::2], terms[1::2])]
    refs[-2][...] = terms[0].astype(refs[-2].dtype)


def add(after, terms, dtype):
    return call(
        add_kernel,
        "add_terms",
        SHARED,
        len(terms) * terms[0].size,
        2 * len(terms) * terms[0].size,
        out_shape=(shaped(terms[0].shape, dtype), MARK),
        in_specs=[PLACE] + [WHOLE] * len(terms),
        out_specs=(WHOLE, PLACE),
    )(after, *terms)


def terms_of_group(array, bits):
    axes = ("rep", "exp")
    distances = [0]
    for bit in bits:
        distances += [distance + (1 << bit) for distance in distances]
    count = lax.axis_size(axes)
    return [array] + [
        lax.ppermute(array, axes, [(i, i ^ distance) for i in range(count)])
        for distance in distances[1:]
    ]


def exchange(rows, axes):
    return lax.all_to_all(rows, axes, split_axis=0, concat_axis=0, tiled=True)


def body(tokens, slot_params, expert_in, expert_out, grad_out):
    params = slot_params.T
    weights = (expert_in[0], expert_out[0])
    replicas = lax.axis_size("rep")
    mine = lax.axis_index("rep").astype(jnp.int32).reshape(1)

    sent, dispatch, combine, *first = gather(tokens, params, grad_out, *weights, 256)
    rows = exchange(sent, "exp")
    other_rows = lax.ppermute(rows, "rep", [(i, (i + 1) % replicas) for i in range(replicas)])
    back, acts, hidden, after = expert(rows, *first, *weights, 512)
    back = exchange(back, "exp")
    grad_in, grad_outer, tokens_half, after = replica_grads(
        mine, after, rows, other_rows, acts, hidden, *weights, tokens, replicas, 512
    )
    left, right, local, after = logits_grads(
        after, back, tokens, tokens_half, params, grad_out, dispatch, combine
    )
    exp_bits = lax.axis_size("exp").bit_length() - 1
    rep_bits = replicas.bit_length() - 1
    groups = [(0, 1, *range(exp_bits, exp_bits + rep_bits))]
    groups += [range(bit, min(bit + 2, exp_bits)) for bit in range(2, exp_bits, 2)]
    for bits in groups[:-1]:
        local, after = add(after, terms_of_group(local, bits), LOW)
    terms = terms_of_group(local, groups[-1])
    grad_tokens, after = tokens_grads(after, left, right)
    grad_params, _ = add(after, terms, WIDE)
    return (grad_tokens, grad_params.T, grad_in[None], grad_outer[None])


def solution(mesh):
    in_specs = (
        P(("rep", "exp"), None, None),
        P(),
        P("exp", None, None),
        P("exp", None, None),
        P(("rep", "exp"), None, None),
    )
    out_specs = (P(("rep", "exp"), None, None), P(), P("exp", "rep", None), P("exp", "rep", None))
    return jax.shard_map(body, mesh=mesh, in_specs=in_specs, out_specs=out_specs, check_vma=False)
```

```python
import functools
import math

import jax
import jax.numpy as jnp
from jax import lax
from jax.experimental import pallas as pl
from jax.experimental.pallas import tpu as pltpu
from jax.sharding import PartitionSpec as P

GELU_C = math.sqrt(2.0 / math.pi)
CUBIC = 0.044715
LOW = jnp.bfloat16
WIDE = jnp.float32
LANES = 128
KINDS = 2
SHARED = 52 * 1024 * 1024
ROOMY = 50 * 1024 * 1024
WHOLE = pl.BlockSpec(memory_space=pltpu.VMEM)
PLACE = pl.BlockSpec(memory_space=pl.ANY)


def call(kernel, name, grant, flops, nbytes, exps=0, **kwargs):
    return pl.pallas_call(
        kernel,
        name=name,
        compiler_params=pltpu.CompilerParams(vmem_limit_bytes=grant),
        cost_estimate=pl.CostEstimate(
            flops=flops, bytes_accessed=nbytes, transcendentals=exps
        ),
        **kwargs,
    )


def shaped(shape, dtype):
    return jax.ShapeDtypeStruct(shape, dtype)


MARK = shaped((8, LANES), WIDE)


def gelu_parts(values):
    square = values * values
    tangent = jnp.tanh(GELU_C * (values + CUBIC * square * values))
    half = 0.5 * (1.0 + tangent)
    slope = half + 0.5 * values * (1.0 - tangent * tangent) * GELU_C * (1.0 + 3.0 * CUBIC * square)
    return values * half, slope


def dot(left, right, over_left, over_right):
    return lax.dot_general(
        left, right, (((over_left,), (over_right,)), ((), ())), preferred_element_type=WIDE
    )


def softmax(values, axis):
    raised = jnp.exp(values - jnp.max(values, axis=axis, keepdims=True))
    return raised / jnp.sum(raised, axis=axis, keepdims=True)


def scratch_rows(shape):
    return pltpu.VMEM((shape[1] // LANES, shape[0], LANES), WIDE)


def load_rows(ref, array):
    for tile in range(ref.shape[0]):
        ref[tile] = array[:, tile * LANES : (tile + 1) * LANES].astype(WIDE)


def packed(ref):
    return jnp.concatenate([ref[tile] for tile in range(ref.shape[0])], axis=1).astype(LOW)


def take(ref, start, count, stride, first=0, tiles=None):
    tiles = ref.shape[0] if tiles is None else tiles
    picked = [ref[first + tile, pl.ds(start, count, stride=stride), :] for tile in range(tiles)]
    return jnp.concatenate(picked, axis=1)


def put(ref, start, count, stride, array):
    for tile in range(ref.shape[0]):
        ref[tile, pl.ds(start, count, stride=stride), :] = array[
            :, tile * LANES : (tile + 1) * LANES
        ]


def start_copy(source, target, sem):
    copy = pltpu.make_async_copy(source, target, sem)
    copy.start()
    return copy


def far(array):
    return pltpu.with_memory_space_constraint(array, pltpu.HBM)


def start_halves(source, target, sems):
    images = source.shape[0]
    parts = []
    for index, (first, last) in enumerate(((0, images // 2), (images // 2, images))):
        part = pl.ds(first, last - first)
        copy = start_copy(source.at[part], target.at[part], sems.at[index])
        parts.append((copy, range(first, last)))
    return parts


def gather_kernel(
    tokens, params, grads, w_in, w_out, sent, dispatch, combine, first_in, first_out,
    tokens_v, grads_v, rows, sems,
):
    images = tokens.shape[0]
    slots = params.shape[0]
    stride = KINDS * images
    halves = start_halves(tokens, tokens_v, sems)
    grads_copy = start_copy(grads, grads_v, sems.at[2])
    units = slice(0, first_out.shape[0])
    weight_copies = (
        start_copy(w_in.at[:, units], first_in, sems.at[3]),
        start_copy(w_out.at[units, :], first_out, sems.at[4]),
    )
    logits = []
    for copy, half in halves:
        copy.wait()
        logits += [dot(params[...], tokens_v[image], 1, 1) for image in half]
    over_slots = []
    for image in range(images):
        over_tokens = softmax(logits[image], 1)
        dispatch[image] = over_tokens
        put(
            rows, KINDS * image, slots, stride, dot(over_tokens.astype(LOW), tokens_v[image], 1, 0)
        )
        over_slots.append(softmax(logits[image], 0))
        combine[image] = over_slots[image]
    grads_copy.wait()
    for image in range(images):
        value = dot(over_slots[image].astype(LOW), grads_v[image], 1, 0)
        put(rows, KINDS * image + 1, slots, stride, value)
    sent[...] = packed(rows)
    for copy in weight_copies:
        copy.wait()


def gather(tokens, params, grads, w_in, w_out, first):
    images, length, width = tokens.shape
    slots = params.shape[0]
    weights = shaped((images, slots, length), WIDE)
    rows = (slots * images * KINDS, width)
    return call(
        gather_kernel,
        "gather_slots",
        ROOMY,
        6 * images * slots * length * width,
        4 * images * length * width,
        2 * images * slots * length,
        out_shape=(
            shaped(rows, LOW),
            weights,
            weights,
            shaped((width, first), LOW),
            shaped((first, width), LOW),
        ),
        in_specs=[PLACE, WHOLE, PLACE, PLACE, PLACE],
        out_specs=(WHOLE,) * 5,
        scratch_shapes=[
            pltpu.VMEM(tokens.shape, LOW),
            pltpu.VMEM(grads.shape, LOW),
            scratch_rows(rows),
            pltpu.SemaphoreType.DMA((5,)),
        ],
    )(tokens, params, grads, w_in, w_out)


def chunks_of(first, hidden, tile):
    edges = [*range(first, hidden, tile), hidden]
    return [slice(low, high) for low, high in zip(edges, edges[1:])]


def start_weights(w_in, w_out, w_in_v, w_out_v, sems, chunks):
    copies = []
    for chunk, units in enumerate(chunks):
        copies.append(
            (
                start_copy(w_in.at[:, units], w_in_v.at[:, units], sems.at[0, chunk]),
                start_copy(w_out.at[units, :], w_out_v.at[units, :], sems.at[1, chunk]),
            )
        )
    return copies


def weight_scratch(width, hidden, chunks):
    return [
        pltpu.VMEM((width, hidden), LOW),
        pltpu.VMEM((hidden, width), LOW),
        pltpu.SemaphoreType.DMA((2, len(chunks))),
    ]


def expert_kernel(
    chunks, rows, first_in, first_out, w_in, w_out, back, acts, hidden, mark,
    w_in_v, w_out_v, sems, wide,
):
    del mark
    copies = start_weights(w_in, w_out, w_in_v, w_out_v, sems, chunks)
    count = rows.shape[0] // KINDS
    load_rows(wide, rows[...])
    rows_in = take(wide, 0, count, KINDS).astype(LOW)
    rows_grad = take(wide, 1, count, KINDS).astype(LOW)

    def first_products(weight_in, weight_out):
        return dot(rows_in, weight_in, 1, 0), dot(rows_grad, weight_out, 1, 1)

    def second_products(held, weight_in, weight_out):
        return dot(held[0], weight_out, 1, 0), dot(held[1], weight_in, 1, 1)

    def hold(preact, d_acts, units):
        values, slope = gelu_parts(preact)
        held = (values.astype(LOW), (d_acts * slope).astype(LOW))
        acts[:, units], hidden[:, units] = held
        return held

    held = hold(
        *first_products(first_in[...], first_out[...]), slice(0, first_out.shape[0])
    )
    out, d_in = second_products(held, first_in[...], first_out[...])
    before = None
    for pair, units in zip([*copies, None], [*chunks, None]):
        if pair is not None:
            for copy in pair:
                copy.wait()
            products = first_products(w_in_v[:, units], w_out_v[units, :])
        if before is not None:
            parts = second_products(held, w_in_v[:, before], w_out_v[before, :])
            out, d_in = out + parts[0], d_in + parts[1]
        if pair is not None:
            held = hold(*products, units)
        before = units
    put(wide, 0, count, KINDS, out)
    put(wide, 1, count, KINDS, d_in)
    back[...] = packed(wide)


def expert(rows, first_in, first_out, w_in, w_out, tile):
    total, width = rows.shape
    hidden = w_in.shape[1]
    count = total // KINDS
    kept = shaped((count, hidden), LOW)
    start = first_out.shape[0]
    chunks = [
        slice(start, start + tile),
        *chunks_of(start + tile, hidden, tile + tile // 2),
    ]
    return call(
        functools.partial(expert_kernel, chunks),
        "expert_rows",
        ROOMY,
        8 * count * hidden * width,
        4 * hidden * width,
        count * hidden,
        out_shape=(shaped(rows.shape, LOW), kept, kept, MARK),
        in_specs=[WHOLE, WHOLE, WHOLE, PLACE, PLACE],
        out_specs=(WHOLE, WHOLE, WHOLE, PLACE),
        scratch_shapes=[*weight_scratch(width, hidden, chunks), scratch_rows(rows.shape)],
    )(rows, first_in, first_out, w_in, w_out)


def replica_kernel(
    chunks, mine, after, rows, other_rows, acts, hidden, w_in, w_out, tokens,
    grad_in, grad_out, tokens_half, mark,
    w_in_v, w_out_v, grad_in_v, grad_out_v, wide, grads, turned, sems, in_sems, out_sems, half_sem,
):
    del after, mark
    count = rows.shape[0] // KINDS
    size = w_in.shape[1]
    half = grad_out.shape[0]
    spans, copies = [], []
    for chunk, units in enumerate(chunks):
        start = pl.multiple_of(lax.rem(mine[0] * half + units.start, size), LANES)
        span = pl.ds(start, units.stop - units.start)
        spans.append(span)
        copies.append(
            (
                start_copy(w_in.at[:, span], w_in_v.at[:, units], sems.at[0, chunk]),
                start_copy(w_out.at[span, :], w_out_v.at[units, :], sems.at[1, chunk]),
            )
        )
    results = [
        start_copy(tokens.at[pl.ds(0, tokens_half.shape[0])], tokens_half, half_sem.at[0])
    ]
    left, right = [], []
    tiles = turned.shape[0] // LANES
    for source in (rows, other_rows):
        load_rows(wide, source[...])
        left.append(take(wide, 0, count, KINDS, mine[0] * tiles, tiles))
        right.append(take(wide, 1, count, KINDS))
    turned[...] = jnp.concatenate(left, axis=0).T.astype(LOW)
    grads[...] = jnp.concatenate(right, axis=0).astype(LOW)
    rows_in = take(wide, 0, count, KINDS).astype(LOW)
    rows_grad = right[1].astype(LOW)
    before = None
    for chunk in range(len(chunks) + 1):
        if chunk < len(chunks):
            units = chunks[chunk]
            for copy in copies[chunk]:
                copy.wait()
            preact = dot(rows_in, w_in_v[:, units], 1, 0)
            d_acts = dot(rows_grad, w_out_v[units, :], 1, 1)
        if before is not None:
            past, span, all_acts, all_hidden = before
            grad_in_v[:, past] = dot(turned[...], all_hidden, 1, 0).astype(LOW)
            results.append(
                start_copy(grad_in_v.at[:, past], grad_in.at[:, span], in_sems.at[chunk - 1])
            )
            if past.stop <= half:
                grad_out_v[past, :] = dot(all_acts, grads[...], 0, 0).astype(LOW)
                results.append(
                    start_copy(
                        grad_out_v.at[past, :], grad_out.at[past, :], out_sems.at[chunk - 1]
                    )
                )
        if chunk < len(chunks):
            span = spans[chunk]
            values, slope = gelu_parts(preact)
            all_acts = jnp.concatenate([acts[:, span], values.astype(LOW)], axis=0)
            all_hidden = jnp.concatenate(
                [hidden[:, span], (d_acts * slope).astype(LOW)], axis=0
            )
            before = (units, span, all_acts, all_hidden)
    for copy in results:
        copy.wait()


def replica_grads(
    mine, after, rows, other_rows, acts, hidden, w_in, w_out, tokens, replicas, tile
):
    total, width = rows.shape
    size = w_in.shape[1]
    half = size // replicas
    count = total // KINDS
    chunks = [
        slice(part * half + units.start, part * half + units.stop)
        for part in range(replicas)
        for units in chunks_of(0, half, tile)
    ]
    return call(
        functools.partial(replica_kernel, chunks),
        "replica_grads",
        ROOMY,
        64 * count * size * width,
        32 * size * width,
        count * size,
        out_shape=(
            shaped((width // replicas, size), LOW),
            shaped((half, width), LOW),
            shaped((tokens.shape[0] // 2, *tokens.shape[1:]), LOW),
            MARK,
        ),
        in_specs=[pl.BlockSpec(memory_space=pltpu.SMEM), PLACE]
        + [WHOLE] * 4
        + [PLACE] * 3,
        out_specs=(PLACE, PLACE, WHOLE, PLACE),
        scratch_shapes=[
            *weight_scratch(width, size, chunks)[:2],
            pltpu.VMEM((width // replicas, size), LOW),
            pltpu.VMEM((half, width), LOW),
            scratch_rows((total, width)),
            pltpu.VMEM((2 * count, width), LOW),
            pltpu.VMEM((width // replicas, 2 * count), LOW),
            pltpu.SemaphoreType.DMA((2, len(chunks))),
            pltpu.SemaphoreType.DMA((len(chunks),)),
            pltpu.SemaphoreType.DMA((len(chunks),)),
            pltpu.SemaphoreType.DMA((1,)),
        ],
    )(mine, after, rows, other_rows, acts, hidden, w_in, w_out, far(tokens))


def logits_kernel(
    after, back, tokens, tokens_half, params, grads, dispatch, combine, left, right, local, mark,
    tokens_v, grads_v, wide, sems,
):
    del after, mark
    images, slots, _ = dispatch.shape
    ready = tokens_half.shape[0]
    early, late = pl.ds(0, ready), pl.ds(ready, images - ready)
    copies = (
        (start_copy(grads.at[early], grads_v.at[early], sems.at[0]),),
        (
            start_copy(tokens.at[late], tokens_v, sems.at[1]),
            start_copy(grads.at[late], grads_v.at[late], sems.at[2]),
        ),
    )

    def tokens_of(image):
        return tokens_half[image] if image < ready else tokens_v[image - ready]

    load_rows(wide, back[...])
    stride = KINDS * images
    slot_out, d_slot_in = [], []
    for image in range(images):
        slot_out.append(take(wide, KINDS * image, slots, stride).astype(LOW))
        d_slot_in.append(take(wide, KINDS * image + 1, slots, stride).astype(LOW))
        right[image, :slots, :] = d_slot_in[image]
        right[image, slots:, :] = params[...]
        left[image, :slots, :] = dispatch[image].astype(LOW)

    def dispatch_part(image):
        weights = dispatch[image]
        d_dispatch = dot(d_slot_in[image], tokens_of(image), 1, 1)
        return weights * (d_dispatch - jnp.sum(weights * d_dispatch, axis=1, keepdims=True))

    def combine_part(image):
        weights = combine[image]
        d_combine = dot(slot_out[image], grads_v[image], 1, 1)
        return weights * (d_combine - jnp.sum(weights * d_combine, axis=0, keepdims=True))

    parts = [dispatch_part(image) for image in range(ready)]
    total = None
    for pair, half in zip(copies, (range(ready), range(ready, images))):
        for copy in pair:
            copy.wait()
        for image in half:
            if image >= ready:
                parts.append(dispatch_part(image))
        lows = [(parts[image] + combine_part(image)).astype(LOW) for image in half]
        for image, low in zip(half, lows):
            left[image, slots:, :] = low
            part = dot(low, tokens_of(image), 1, 0)
            total = part if total is None else total + part
    local[...] = total.astype(LOW)


def logits_grads(after, back, tokens, tokens_half, params, grads, dispatch, combine):
    images, length, width = tokens.shape
    slots = params.shape[0]
    return call(
        logits_kernel,
        "logits_grads",
        ROOMY,
        6 * images * slots * length * width,
        4 * images * length * width,
        out_shape=(
            shaped((images, 2 * slots, length), LOW),
            shaped((images, 2 * slots, width), LOW),
            shaped(params.shape, LOW),
            MARK,
        ),
        in_specs=[PLACE, WHOLE, PLACE, WHOLE, WHOLE, PLACE, WHOLE, WHOLE],
        out_specs=(WHOLE, WHOLE, WHOLE, PLACE),
        scratch_shapes=[
            pltpu.VMEM((images - tokens_half.shape[0], length, width), LOW),
            pltpu.VMEM(grads.shape, LOW),
            scratch_rows(back.shape),
            pltpu.SemaphoreType.DMA((3,)),
        ],
    )(after, back, far(tokens), tokens_half, params, far(grads), dispatch, combine)


def tokens_kernel(after, left, right, out, mark):
    del after, mark
    out[0] = dot(left[0], right[0], 0, 0).astype(LOW)


def tokens_grads(after, left, right):
    images, deep, length = left.shape
    width = right.shape[2]
    return call(
        tokens_kernel,
        "tokens_grads",
        SHARED,
        2 * images * deep * length * width,
        2 * images * length * width,
        grid=(images,),
        out_shape=(shaped((images, length, width), LOW), MARK),
        in_specs=[
            PLACE,
            pl.BlockSpec((1, deep, length), lambda i: (i, 0, 0)),
            pl.BlockSpec((1, deep, width), lambda i: (i, 0, 0)),
        ],
        out_specs=(pl.BlockSpec((1, length, width), lambda i: (i, 0, 0)), PLACE),
    )(after, left, right)


def add_kernel(after, *refs):
    del after
    terms = [ref[...].astype(WIDE) for ref in refs[:-2]]
    while len(terms) > 1:
        terms = [left + right for left, right in zip(terms[::2], terms[1::2])]
    refs[-2][...] = terms[0].astype(refs[-2].dtype)


def add(after, terms, dtype):
    return call(
        add_kernel,
        "add_terms",
        SHARED,
        len(terms) * terms[0].size,
        2 * len(terms) * terms[0].size,
        out_shape=(shaped(terms[0].shape, dtype), MARK),
        in_specs=[PLACE] + [WHOLE] * len(terms),
        out_specs=(WHOLE, PLACE),
    )(after, *terms)


def terms_of_group(array, bits):
    axes = ("rep", "exp")
    distances = [0]
    for bit in bits:
        distances += [distance + (1 << bit) for distance in distances]
    count = lax.axis_size(axes)
    return [array] + [
        lax.ppermute(array, axes, [(i, i ^ distance) for i in range(count)])
        for distance in distances[1:]
    ]


def exchange(rows, axes):
    return lax.all_to_all(rows, axes, split_axis=0, concat_axis=0, tiled=True)


def body(tokens, slot_params, expert_in, expert_out, grad_out):
    params = slot_params.T
    weights = (expert_in[0], expert_out[0])
    replicas = lax.axis_size("rep")
    mine = lax.axis_index("rep").astype(jnp.int32).reshape(1)

    sent, dispatch, combine, *first = gather(tokens, params, grad_out, *weights, 256)
    rows = exchange(sent, "exp")
    other_rows = lax.ppermute(rows, "rep", [(i, (i + 1) % replicas) for i in range(replicas)])
    back, acts, hidden, after = expert(rows, *first, *weights, 512)
    back = exchange(back, "exp")
    grad_in, grad_outer, tokens_half, after = replica_grads(
        mine, after, rows, other_rows, acts, hidden, *weights, tokens, replicas, 512
    )
    left, right, local, after = logits_grads(
        after, back, tokens, tokens_half, params, grad_out, dispatch, combine
    )
    exp_bits = lax.axis_size("exp").bit_length() - 1
    rep_bits = replicas.bit_length() - 1
    groups = [(0, 1, *range(exp_bits, exp_bits + rep_bits))]
    groups += [range(bit, min(bit + 2, exp_bits)) for bit in range(2, exp_bits, 2)]
    for bits in groups[:-1]:
        local, after = add(after, terms_of_group(local, bits), LOW)
    terms = terms_of_group(local, groups[-1])
    grad_tokens, after = tokens_grads(after, left, right)
    grad_params, _ = add(after, terms, WIDE)
    return (grad_tokens, grad_params.T, grad_in[None], grad_outer[None])


def solution(mesh):
    in_specs = (
        P(("rep", "exp"), None, None),
        P(),
        P("exp", None, None),
        P("exp", None, None),
        P(("rep", "exp"), None, None),
    )
    out_specs = (P(("rep", "exp"), None, None), P(), P("exp", "rep", None), P("exp", "rep", None))
    return jax.shard_map(body, mesh=mesh, in_specs=in_specs, out_specs=out_specs, check_vma=False)
```
